32 devices in a mesh: dp: 4 (over y, core), expert: 8 (over z, x).
Axes of the slice: x: 2, y: 2, z: 4, core: 2. Of those that a mesh axis runs over, the one named last changes fastest.
Arguments:
- grad_out: bfloat16 [4096, 2048], P(('dp', 'expert')), may hold values from -6 to 6
- route_ids: int32 [4096, 2], P(('dp', 'expert')), may hold values from 0 to 15, all different within a row; in each aligned block of 128 rows (0 to 127, 128 to 255, ...) at most 32 rows name the same one
- route_probs: float32 [4096, 2], P(('dp', 'expert')), may hold values from 0.01 to 0.3
- hidden: bfloat16 [4, 8, 16, 32, 768], P('dp', None, 'expert'), may hold values from -2 to 2
- w_down: bfloat16 [16, 768, 2048], P('expert'), may hold values from -0.21875 to 0.21875
Outputs:
- hidden_grad: bfloat16 [4, 8, 16, 32, 768], P('dp', None, 'expert')
- prob_grad: float32 [4096, 2], P(('dp', 'expert'))
- weight_grad: float32 [768, 16, 2048], P('dp', 'expert')
The draws below stay inside these ranges and needn't reach their ends.
Inputs may be any that keep to these rules, and one draw needn't show every extreme that they name: `route_ids`: each row names 2 different experts; among the 128 rows of one device no expert is named more than 32 times, a bound that some block reaches.
All inputs are finite; a program needn't handle non-finite values.
Results may differ from the reference program's by a relative error of at most 0.022.
Values may be sent and summed in bfloat16 or wider, within the bound.
No kernel may reach another device: no remote copies, remote signals or barrier semaphores. Data moves between devices by JAX's collectives and lax.ppermute only.
A program may use at most 128 MiB of HBM per device.

```python
import math
import jax
import jax.numpy as jnp
import numpy as np
from jax import lax

D = 2048
H = 768
TOP = 2
TOK_DEV = 128
EXPERTS = 16
CAP = 32
TOKENS = 4096
N_DP = 4
N_EXPERT = 8


def strengthened(drawn, stream_key, source, target, blocks, factor):
    def block_of(dim):
        return (jnp.arange(drawn.shape[dim]) // (drawn.shape[dim] // blocks)).reshape((-1,) + (1,) * (drawn.ndim - 1 - dim))

    near = jax.random.permutation(stream_key, blocks)[block_of(target)]
    far = (block_of(target) + blocks // 2) % blocks
    return jnp.where((block_of(source) == near) | (block_of(source) == far), factor * drawn, drawn)


def steps_of(rng, shape, split, low, high):
    def one(dim, blocks):
        heights = jax.random.uniform(jax.random.fold_in(jax.random.fold_in(rng, 6), dim), (blocks,), jnp.float32, low / len(split), high / len(split))
        return jnp.repeat(jnp.exp(heights), shape[dim] // blocks).reshape((-1,) + (1,) * (len(shape) - dim - 1))

    factor_of = one(*split[0])
    for cut in split[1:]:
        factor_of = factor_of * one(*cut)
    return factor_of


def shared_out(key, own, number, rows, number_of, top, reach, skew):
    ranking = jax.random.permutation(key, number_of)
    packed, common = shares(number_of, rows * top, reach, skew, True), shares(number_of, rows * top, reach, skew, False)
    places = jnp.arange(number_of)

    def named(sizes, turn):
        used = int((sizes > 0).sum())
        fixed = max(1, used // 4)
        shifted = fixed + (places - fixed + turn * (used - fixed)) % max(1, number_of - fixed)
        return jnp.zeros((number_of,), jnp.int32).at[ranking[jnp.where(places < fixed, places, shifted)]].set(jnp.asarray(sizes, jnp.int32))

    sizes = jnp.where(number % 4 == 0, named(packed, number // 4), named(common, number - number // 4 - 1))
    mixed = jax.random.permutation(jax.random.fold_in(own, 3), number_of)
    source_of, sink = mixed[0:number_of // 2 * 2:2], mixed[1:number_of // 2 * 2:2]
    margin = jnp.minimum(sizes[source_of] - 1, reach - sizes[sink]) // 2
    margin = jnp.where((source_of == ranking[0]) | (sink == ranking[0]) | (sizes[sink] == 0), 0, jnp.maximum(margin, 0))
    shifted = jax.random.randint(jax.random.fold_in(own, 4), (number_of // 2,), 0, 1 << 20) % (margin + 1)
    sizes = sizes.at[source_of].add(-shifted).at[sink].add(shifted)
    labels = jnp.searchsorted(jnp.cumsum(sizes), jnp.arange(rows * top), side="right").astype(jnp.int32)
    grid = labels.reshape(top, rows).T
    grid = grid[jax.random.permutation(jax.random.fold_in(own, 1), rows)]
    turn = jax.random.randint(jax.random.fold_in(own, 2), (rows, 1), 0, top)
    return jnp.take_along_axis(grid, (jnp.arange(top)[None, :] + turn) % top, axis=1)


def shares(number_of, total, limit, skew, full):
    portions = [(1 << 20) // math.isqrt(rank ** skew) + 1 for rank in range(1, number_of + 1)]
    largest = limit if full else min(limit, max(-(-total // number_of), total * portions[0] // sum(portions)))
    least = 1 if total - largest >= number_of - 1 else 0
    given, spare = [largest] + [least] * (number_of - 1), total - largest - least * (number_of - 1)
    while spare > 0:
        candidates = [i for i in range(1, number_of) if given[i] < largest] or [i for i in range(1, number_of) if given[i] < limit]
        mass, budget = sum([portions[i] for i in candidates]), spare
        for i in candidates:
            addition = min(limit - given[i], max(1, budget * portions[i] // mass), spare)
            given[i] = given[i] + addition
            spare = spare - addition
    return np.array(given)


def normal_values(own_key, shape, scale, bound, shards=(), held_as=jnp.bfloat16):
    factor_of = steps_of(own_key, shape, shards, -0.22, 0.18) if shards else 1.0
    array = jax.random.normal(own_key, shape, jnp.float32) * scale * factor_of
    return jnp.minimum(jnp.maximum(array, -bound), bound).astype(held_as)


def noise_with(key, shape, deviation, reach, cuts, heavy, held_as=jnp.bfloat16):
    drawn = deviation * jax.random.normal(key, shape, jnp.float32)
    if cuts:
        drawn = drawn * steps_of(key, shape, cuts, -0.22, 0.18)
    return jnp.clip(strengthened(drawn, jax.random.fold_in(key, 3), *heavy), -reach, reach).astype(held_as)


def setup_inputs(seed: int = 0) -> dict:
    splits = jax.random.split(jax.random.key(seed), 6)
    grad_out = normal_values(splits[0], (TOKENS, D), 1.0, 6.0, ((0, 32),))
    route_ids_keys = jax.random.split(jax.random.fold_in(splits[1], 1), TOKENS // TOK_DEV)
    route_ids_turns = jax.random.permutation(jax.random.fold_in(splits[1], 3), TOKENS // TOK_DEV)
    route_ids = jax.vmap(lambda own, number: shared_out(jax.random.fold_in(splits[1], 2), own, number, TOK_DEV, EXPERTS, TOP, CAP, 2))(route_ids_keys, route_ids_turns).reshape((TOKENS, TOP))
    route_probs = jnp.clip(jnp.exp(math.log(0.3) - 3.4011974 * jax.random.uniform(splits[2], (TOKENS, TOP), jnp.float32) ** steps_of(splits[2], (TOKENS, TOP), ((0, 32),), -0.2, 0.2)), 0.01, 0.3)
    hidden = noise_with(splits[3], (N_DP, N_EXPERT, EXPERTS, CAP, H), 0.3, 2.0, ((0, 4), (2, 8)), (0, 4, 4, 2.0))
    w_down = normal_values(splits[4], (EXPERTS, H, D), H ** -0.5, 0.21875, ((0, 8),))
    return {"grad_out": grad_out, "route_ids": route_ids, "route_probs": route_probs, "hidden": hidden, "w_down": w_down}


def slots_of(route_blocks):
    hits = (route_blocks[..., None] == jnp.arange(EXPERTS, dtype=jnp.int32)).astype(jnp.int32).sum(2)
    before = jnp.cumsum(hits, axis=1) - hits
    return jnp.take_along_axis(before, route_blocks, axis=2)


def reference(grad_out, route_ids, route_probs, hidden, w_down):
    blocks = N_DP * N_EXPERT
    total = jnp.sum(route_probs, axis=1, keepdims=True)
    gates = route_probs / total
    gate_word = lax.optimization_barrier(gates.astype(jnp.bfloat16)).astype(jnp.float32)
    route_blocks = route_ids.reshape(blocks, TOK_DEV, TOP)
    slot = slots_of(route_blocks)
    block_index = jnp.arange(blocks, dtype=jnp.int32)[:, None, None]
    replica = block_index // N_EXPERT
    source = block_index % N_EXPERT
    per_expert = N_DP * N_EXPERT * CAP
    flat = (((route_blocks * N_DP + replica) * N_EXPERT + source) * CAP + slot).reshape(-1).astype(jnp.int32)
    pairs_all = TOKENS * TOP
    inverse = jnp.full((EXPERTS * per_expert,), pairs_all, jnp.int32).at[flat].set(jnp.arange(pairs_all, dtype=jnp.int32))
    gate_flat = gate_word.reshape(-1)

    def expert_step(index):
        picked = lax.dynamic_slice_in_dim(inverse, index * per_expert, per_expert)
        live = picked < pairs_all
        safe = jnp.where(live, picked, 0).astype(jnp.int32)
        rows = jnp.where(live[:, None], grad_out[safe // TOP], jnp.zeros((), jnp.bfloat16))
        factor = jnp.where(live, gate_flat[safe], jnp.zeros((), gate_flat.dtype))
        weight = lax.dynamic_index_in_dim(w_down, index, 0, keepdims=False)
        acts = lax.dynamic_index_in_dim(hidden, index, 2, keepdims=False).reshape(per_expert, H)
        raw = jnp.dot(rows, weight.T, preferred_element_type=jnp.float32)
        grad_hidden = (factor[:, None] * raw).astype(jnp.bfloat16)
        gate_grad = jnp.sum(raw * acts.astype(jnp.float32), axis=1)
        scaled = (factor[:, None] * rows.astype(jnp.float32)).astype(jnp.bfloat16)
        terms = jnp.einsum("prh,prd->phd", acts.reshape(N_DP, -1, H).astype(jnp.float32),
                           scaled.reshape(N_DP, -1, D).astype(jnp.float32))
        rounded = lax.optimization_barrier(terms.astype(jnp.bfloat16)).astype(jnp.float32)
        return grad_hidden, gate_grad, jnp.sum(rounded, axis=0)

    hidden_grads, gate_grads, weight_terms = lax.map(expert_step, jnp.arange(EXPERTS, dtype=jnp.int32))
    hidden_grad = hidden_grads.reshape(EXPERTS, N_DP, N_EXPERT, CAP, H).transpose(1, 2, 0, 3, 4)
    picked_grad = gate_grads.reshape(-1)[flat].reshape(TOKENS, TOP)
    prob_grad = (picked_grad - jnp.sum(gates * picked_grad, axis=1, keepdims=True)) / total
    weight_grad = weight_terms.transpose(1, 0, 2)
    return hidden_grad, prob_grad, weight_grad
```

```python
import jax
import jax.numpy as jnp
from jax import lax
from jax.sharding import PartitionSpec as P


def body(grad_out, route_ids, route_probs, hidden, w_down):
    groups = lax.axis_size("expert")
    dp = lax.axis_size("dp")
    held = w_down.shape[0]
    units = w_down.shape[1]
    experts = groups * held
    capacity = hidden.shape[3]
    chosen = route_ids.shape[1]
    tokens_here = grad_out.shape[0]
    features = grad_out.shape[1]
    slots = experts * capacity
    f32, bf16 = jnp.float32, jnp.bfloat16

    total = jnp.sum(route_probs, axis=1, keepdims=True)
    gates = route_probs / total
    gate_word = gates.astype(bf16)
    named = route_ids[..., None] == jnp.arange(experts, dtype=jnp.int32)
    hits = named.any(1).astype(bf16)
    earlier = jnp.tril(jnp.ones((tokens_here, tokens_here), bf16), -1)
    before = jnp.dot(earlier, hits, preferred_element_type=f32).astype(jnp.int32)
    slot = jnp.sum(jnp.where(named, before[:, None, :], 0), axis=2)
    flat = route_ids * capacity + slot
    fills = flat[None] == jnp.arange(slots, dtype=jnp.int32)[:, None, None]
    place = fills.any(2).astype(bf16)
    send_rows = jnp.dot(place, grad_out, preferred_element_type=f32).astype(bf16)
    send_gates = jnp.sum(
        jnp.where(fills, gate_word.astype(f32)[None], 0.0), axis=(1, 2)
    ).astype(bf16)
    recv_gates = lax.all_to_all(
        send_gates.reshape(groups, held, capacity), "expert", split_axis=0, concat_axis=0, tiled=True
    )
    recv_rows = lax.all_to_all(
        send_rows.reshape(groups, held, capacity, features),
        "expert",
        split_axis=0,
        concat_axis=0,
        tiled=True,
    )
    saved = hidden[0]
    factor = recv_gates.astype(f32)[..., None]
    scaled = (factor * recv_rows.astype(f32)).astype(bf16)

    share = units // dp
    across = dp // 2
    me = lax.axis_index("dp")
    core, row = me % 2, me // 2
    term = jnp.einsum("sech,secd->ehd", saved, scaled, preferred_element_type=f32)
    term = term.astype(bf16).reshape(held, across, 2, share, features)
    keep = lax.dynamic_index_in_dim(term, core, 2, keepdims=False)
    give = lax.dynamic_index_in_dim(term, 1 - core, 2, keepdims=False)
    got = lax.ppermute(give, "dp", [(i, i ^ 1) for i in range(dp)])
    pair = keep.astype(f32) + got.astype(f32)
    sum_here = lax.dynamic_index_in_dim(pair, row, 1, keepdims=False)
    for step in range(1, across):
        there = lax.dynamic_index_in_dim(pair, (row + step) % across, 1, keepdims=False)
        shift = [(2 * r + c, 2 * ((r + step) % across) + c) for r in range(across) for c in range(2)]
        sum_here = sum_here + lax.ppermute(there.astype(bf16), "dp", shift).astype(f32)
    weight_grad = sum_here.transpose(1, 0, 2)

    raw = jnp.einsum("secd,ehd->sech", recv_rows, w_down, preferred_element_type=f32)
    hidden_grad = (factor * raw).astype(bf16)[None]
    gate_grad = jnp.sum(raw * saved.astype(f32), axis=-1)
    returned = lax.all_to_all(gate_grad, "expert", split_axis=0, concat_axis=0, tiled=True)
    picked = jnp.sum(jnp.where(fills, returned.reshape(slots, 1, 1), 0.0), axis=0)
    prob_grad = (picked - jnp.sum(gates * picked, axis=1, keepdims=True)) / total
    return (hidden_grad, prob_grad, weight_grad)


def solution(mesh):
    in_specs = (
        P(("dp", "expert"), None),
        P(("dp", "expert"), None),
        P(("dp", "expert"), None),
        P("dp", None, "expert", None, None),
        P("expert", None, None),
    )
    out_specs = (
        P("dp", None, "expert", None, None),
        P(("dp", "expert"), None),
        P("dp", "expert", None),
    )
    return jax.shard_map(body, mesh=mesh, in_specs=in_specs, out_specs=out_specs, check_vma=False)
```

```python
import functools

import jax
import jax.numpy as jnp
from jax import lax
from jax.experimental import pallas as pl
from jax.experimental.pallas import tpu as pltpu
from jax.sharding import PartitionSpec as P

F32, BF16, I32 = jnp.float32, jnp.bfloat16, jnp.int32
PARAMS = pltpu.CompilerParams(vmem_limit_bytes=24 * 1024 * 1024)


def cost(flops, nbytes):
    return pl.CostEstimate(flops=flops, bytes_accessed=nbytes, transcendentals=0)


def nbytes(shapes):
    return sum(x.size * x.dtype.itemsize for x in jax.tree.leaves(shapes))


def call(kernel, outs, *args, flops=0, **kw):
    return pl.pallas_call(
        kernel,
        out_shape=outs,
        compiler_params=PARAMS,
        cost_estimate=cost(flops, nbytes(args) + nbytes(outs)),
        **kw,
    )(*args)


def gates_of(probs_ref):
    probs = probs_ref[...]
    total = jnp.sum(probs, axis=0, keepdims=True)
    gates = probs / total
    return total, gates, gates.astype(BF16).astype(F32)


def route_kernel(experts, capacity, parts, ids_ref, probs_ref, rows_ref, flat_ref, *out_refs):
    chosen, tokens = ids_ref.shape
    rows = experts * capacity // parts
    _, _, word = gates_of(probs_ref)
    ids = ids_ref[...]
    expert = lax.broadcasted_iota(I32, (experts, tokens), 0)
    named = [ids[k : k + 1] == expert for k in range(chosen)]
    hits = functools.reduce(jnp.add, [n.astype(F32) for n in named]).astype(BF16)
    earlier = lax.broadcasted_iota(I32, (tokens, tokens), 0) < lax.broadcasted_iota(
        I32, (tokens, tokens), 1
    )
    before = jnp.dot(hits, earlier.astype(F32).astype(BF16), preferred_element_type=F32)
    flat = [
        ids[k : k + 1] * capacity
        + jnp.sum(jnp.where(named[k], before, 0.0), axis=0, keepdims=True).astype(I32)
        for k in range(chosen)
    ]
    for k in range(chosen):
        flat_ref[k : k + 1, :] = flat[k]
    me = lax.axis_index("expert") if parts > 1 else 0
    blocks = []
    for part in range(parts):
        slot = lax.broadcasted_iota(I32, (rows, tokens), 0) + (me ^ part) * rows
        blocks.append(
            functools.reduce(
                jnp.add,
                [jnp.where(flat[k] == slot, word[k : k + 1], 0.0) for k in range(chosen)],
            ).astype(BF16)
        )
    place = jnp.concatenate(blocks, axis=0)
    start = 0
    for chunk in range(len(out_refs) // parts):
        outs = out_refs[chunk * parts : (chunk + 1) * parts]
        width = outs[0].shape[1]
        scaled = jnp.dot(
            place, rows_ref[:, start : start + width], preferred_element_type=F32
        ).astype(BF16)
        for part in range(parts):
            outs[part][...] = scaled[part * rows : (part + 1) * rows]
        start += width


def turn_kernel(dp, hidden_ref, out_ref):
    parts, held, _, units = hidden_ref.shape
    share, across = units // dp, dp // 2
    me = lax.axis_index("expert") if parts > 1 else 0
    mine = lax.axis_index("dp")
    core, row = mine % 2, mine // 2
    for e in range(held):
        stacked = jnp.concatenate([hidden_ref[me ^ part, e] for part in range(parts)], axis=0)
        turned = stacked.T
        for piece in range(dp):
            other = (piece % 2) ^ core
            step = (piece // 2 - row + across) % across
            out_ref[e, other, step] = turned[piece * share : (piece + 1) * share]


def stacked_rows(part_refs, held, e):
    own = part_refs[0].shape[0] // held
    return jnp.concatenate([ref[e * own : (e + 1) * own, :] for ref in part_refs], axis=0)


def term_kernel(turned_ref, *refs):
    part_refs, keep_ref, give_ref = refs[:-2], refs[-2], refs[-1]
    held, _, across, share, slots = turned_ref.shape
    for e in range(held):
        scaled = stacked_rows(part_refs, held, e)
        for other, ref in ((1, give_ref), (0, keep_ref)):
            left = turned_ref[e, other].reshape(across * share, slots)
            term = jnp.dot(left, scaled, preferred_element_type=F32).astype(BF16)
            for step in range(across):
                ref[step, e] = term[step * share : (step + 1) * share]


def pair_kernel(keep_ref, got_ref, *out_refs):
    for step, ref in enumerate(out_refs, 1):
        ref[...] = (keep_ref[step].astype(F32) + got_ref[step].astype(F32)).astype(BF16)


def last_kernel(others, keep_ref, got_ref, *refs):
    out_ref = refs[-1]
    for e in range(keep_ref.shape[1]):
        total = keep_ref[0, e].astype(F32) + got_ref[0, e].astype(F32)
        for ref in refs[:others]:
            total = total + ref[e].astype(F32)
        out_ref[:, e, :] = total


def raw_kernel(parts, first, final, weight_ref, *refs):
    part_refs, refs = refs[:parts], refs[parts:]
    if not first:
        acc_ref, refs = refs[0], refs[1:]
    held = weight_ref.shape[0]
    for e in range(held):
        raw = lax.dot_general(
            stacked_rows(part_refs, held, e),
            weight_ref[e],
            (((1,), (1,)), ((), ())),
            preferred_element_type=F32,
        )
        if not first:
            raw = raw + acc_ref[e]
        if not final:
            refs[0][e] = raw
            continue
        hidden_ref, grad_ref, sums_ref = refs
        me = lax.axis_index("expert") if parts > 1 else 0
        own = hidden_ref.shape[2]
        units = raw.shape[1]
        for part in range(parts):
            block = raw[part * own : (part + 1) * own]
            grad_ref[me ^ part, e] = block.astype(BF16)
            product = block * hidden_ref[me ^ part, e].astype(F32)
            folded = functools.reduce(
                jnp.add, [product[:, i : i + 128] for i in range(0, units, 128)]
            )
            sums_ref[me ^ part, e] = jnp.sum(folded, axis=1, keepdims=True)


def prob_kernel(flat_ref, probs_ref, returned_ref, out_ref):
    total, gates, word = gates_of(probs_ref)
    chosen, tokens = flat_ref.shape
    slots = returned_ref.shape[0]
    slot = lax.broadcasted_iota(I32, (slots, tokens), 0)
    returned = returned_ref[...]
    picked = [
        jnp.sum(jnp.where(flat_ref[k : k + 1, :] == slot, returned, 0.0), axis=0, keepdims=True)
        / word[k : k + 1]
        for k in range(chosen)
    ]
    mixed = functools.reduce(jnp.add, [gates[k : k + 1] * picked[k] for k in range(chosen)])
    for k in range(chosen):
        out_ref[k : k + 1, :] = (picked[k] - mixed) / total


def chunks_of(features):
    quarter = features // 4
    return [quarter] * 4


def body(grad_out, route_ids, route_probs, hidden, w_down):
    groups = lax.axis_size("expert")
    dp = lax.axis_size("dp")
    held, units, features = w_down.shape
    capacity = hidden.shape[3]
    experts = groups * held
    slots = experts * capacity
    tokens, chosen = route_ids.shape
    share, across = units // dp, dp // 2
    sds = jax.ShapeDtypeStruct
    direct = groups <= 8
    parts = groups if direct else 1
    rows = slots // parts
    widths = chunks_of(features)
    count = len(widths)

    ids, probs = route_ids.T, route_probs.T
    flat, *sent = call(
        functools.partial(route_kernel, experts, capacity, parts),
        [sds((chosen, tokens), I32)] + [sds((rows, w), BF16) for w in widths for _ in range(parts)],
        ids,
        probs,
        grad_out,
        flops=2 * slots * tokens * features,
    )

    def exchanged(blocks):
        if direct:
            return [blocks[0]] + [
                lax.ppermute(blocks[k], "expert", [(i, i ^ k) for i in range(groups)])
                for k in range(1, parts)
            ]
        width = blocks[0].shape[1]
        got = lax.all_to_all(
            blocks[0].reshape(groups, held, capacity, width),
            "expert",
            split_axis=0,
            concat_axis=0,
            tiled=True,
        )
        return [got.transpose(1, 0, 2, 3).reshape(slots, width)]

    if direct:
        saved = hidden[0]
    else:
        saved = hidden[0].transpose(1, 0, 2, 3).reshape(1, held, groups * capacity, units)
    per_expert = slots // held
    turned = call(
        functools.partial(turn_kernel, dp),
        sds((held, 2, across, share, per_expert), BF16),
        saved,
    )

    arrived = [exchanged(sent[c * parts : (c + 1) * parts]) for c in range(count)]
    flops = [2 * slots * units * w for w in widths]
    weight_grad, raw, start = None, None, 0
    for c, width in enumerate(widths):
        piece = sds((across, held, share, width), BF16)
        keep, give = call(term_kernel, [piece, piece], turned, *arrived[c], flops=flops[c])
        got = lax.ppermute(give, "dp", [(i, i ^ 1) for i in range(dp)])

        final = c == count - 1
        if final:
            outs = [sds(saved.shape, BF16), sds((parts, held, rows // held, 1), F32)]
            extra = [saved]
        else:
            outs, extra = [sds((held, per_expert, units), F32)], []
        extra = extra if c == 0 else [raw] + extra
        whole = pl.BlockSpec(memory_space=pltpu.VMEM)
        made = call(
            functools.partial(raw_kernel, parts, c == 0, final),
            outs,
            w_down,
            *arrived[c],
            *extra,
            flops=flops[c],
            grid=(1,),
            in_specs=[pl.BlockSpec((held, units, width), lambda i, at=start // width: (0, 0, at))]
            + [whole] * (parts + len(extra)),
            out_specs=[whole] * len(outs),
        )
        if final:
            hidden_grad, sums = made
        else:
            raw = made[0]

        piece = sds((held, share, width), BF16)
        pairs = call(pair_kernel, [piece] * (across - 1), keep, got)
        others = []
        for step in range(1, across):
            shift = [(2 * r + i, 2 * ((r + step) % across) + i) for r in range(across) for i in range(2)]
            others.append(lax.ppermute(pairs[step - 1], "dp", shift))
        first = pl.BlockSpec((1, held, share, width), lambda i: (0, 0, 0, 0))
        before = [] if c == 0 else [weight_grad]
        weight_grad = call(
            functools.partial(last_kernel, len(others)),
            sds((share, held, features), F32),
            keep,
            got,
            *others,
            *before,
            grid=(1,),
            in_specs=[first, first]
            + [whole] * len(others)
            + [pl.BlockSpec(memory_space=pl.ANY)] * len(before),
            out_specs=pl.BlockSpec((share, held, width), lambda i, at=start // width: (0, 0, at)),
            input_output_aliases={2 + len(others): 0} if before else {},
        )
        start += width

    if direct:
        sums = sums.reshape(groups, rows)
    else:
        sums = sums.reshape(held, groups, capacity).transpose(1, 0, 2).reshape(groups, -1)
        hidden_grad = hidden_grad.reshape(held, groups, capacity, units).transpose(1, 0, 2, 3)
    returned = lax.all_to_all(sums, "expert", split_axis=0, concat_axis=0, tiled=True)
    prob_grad = call(
        prob_kernel, sds((chosen, tokens), F32), flat, probs, returned.reshape(slots, 1)
    ).T
    return (hidden_grad[None], prob_grad, weight_grad)


def solution(mesh):
    in_specs = (
        P(("dp", "expert"), None),
        P(("dp", "expert"), None),
        P(("dp", "expert"), None),
        P("dp", None, "expert", None, None),
        P("expert", None, None),
    )
    out_specs = (
        P("dp", None, "expert", None, None),
        P(("dp", "expert"), None),
        P("dp", "expert", None),
    )
    return jax.shard_map(body, mesh=mesh, in_specs=in_specs, out_specs=out_specs, check_vma=False)
```

```python
import functools

import jax
import jax.numpy as jnp
from jax import lax
from jax.experimental import pallas as pl
from jax.experimental.pallas import tpu as pltpu
from jax.sharding import PartitionSpec as P

F32, BF16, I32 = jnp.float32, jnp.bfloat16, jnp.int32
PARAMS = pltpu.CompilerParams(vmem_limit_bytes=24 * 1024 * 1024)
VMEM = pl.BlockSpec(memory_space=pltpu.VMEM)
HBM = pl.BlockSpec(memory_space=pltpu.HBM)

LINE, SIDES = 4, 2
FAR, NEAR, PASSED = (3, 2, 1, 0), (1, 0, 3, 2), (2, 0, 3, 1)
FROM = (0, 1, 3, 2)
MASKS = tuple(d * SIDES for d in FROM) + tuple(d * SIDES + 1 for d in FROM)
INFO = 16


def nbytes(shapes):
    return sum(x.size * x.dtype.itemsize for x in jax.tree.leaves(shapes))


def call(kernel, outs, *args, flops=0, **kw):
    return pl.pallas_call(
        kernel,
        out_shape=outs,
        compiler_params=PARAMS,
        cost_estimate=pl.CostEstimate(
            flops=flops, bytes_accessed=nbytes(args) + nbytes(outs), transcendentals=0
        ),
        **kw,
    )(*args)


def gates_of(probs):
    total = jnp.sum(probs, axis=0, keepdims=True)
    gates = probs / total
    return total, gates, gates.astype(BF16).astype(F32)


def slots_of(ids, experts):
    chosen, tokens = ids.shape
    expert = lax.broadcasted_iota(I32, (experts, tokens), 0)
    named = [ids[k : k + 1] == expert for k in range(chosen)]
    hits = functools.reduce(jnp.add, [n.astype(F32) for n in named]).astype(BF16)
    row = lax.broadcasted_iota(I32, (tokens, tokens), 0)
    earlier = (row < lax.broadcasted_iota(I32, (tokens, tokens), 1)).astype(F32).astype(BF16)
    before = jnp.dot(hits, earlier, preferred_element_type=F32)
    return [jnp.sum(jnp.where(n, before, 0.0), axis=0, keepdims=True) for n in named]


def begin_kernel(experts, capacity, ids_ref, probs_ref, rows_ref, flat_ref, out_ref, sem):
    chosen, tokens = ids_ref.shape
    width = out_ref.shape[1]
    copy = pltpu.make_async_copy(rows_ref.at[:, :width], out_ref.at[:tokens], sem)
    copy.start()
    ids = ids_ref[...]
    _, _, word = gates_of(probs_ref[...])
    slots = slots_of(ids, experts)
    for k in range(chosen):
        flat_ref[k : k + 1, :] = ids[k : k + 1] * capacity + slots[k].astype(I32)
    rest = jnp.zeros((INFO - 3 * chosen, tokens), F32)
    info = jnp.concatenate([ids.astype(F32), *slots, word, rest], axis=0).astype(BF16)
    out_ref[tokens:, :tokens] = info
    if width > tokens:
        out_ref[tokens:, tokens:] = jnp.zeros((INFO, width - tokens), BF16)
    copy.wait()


def next_kernel(start, own_ref, far_ref, *refs):
    if start is not None:
        rows_ref, pass_ref, out_ref, sem = refs
        copy = pltpu.make_async_copy(rows_ref.at[:, pl.ds(start, out_ref.shape[1])], out_ref, sem)
        copy.start()
    else:
        (pass_ref,) = refs
    place = lax.axis_index("expert") // SIDES
    inner = jnp.logical_and(place > 0, place < LINE - 1)

    @pl.when(inner)
    def _():
        pass_ref[...] = far_ref[...]

    @pl.when(jnp.logical_not(inner))
    def _():
        pass_ref[...] = own_ref[...]

    if start is not None:
        copy.wait()


def pick_kernel(held, capacity, chosen, first, *refs):
    block_refs, refs = refs[:LINE], refs[LINE:]
    place_ref, own_ref, other_ref = refs
    tokens = place_ref.shape[2]
    if first:
        me = lax.axis_index("expert")
        local = lax.broadcasted_iota(I32, (held * capacity, tokens), 0)
        for j, ref in enumerate(block_refs):
            info = ref[tokens:, :tokens].astype(F32)
            flat = (info[:chosen] * capacity + info[chosen : 2 * chosen]).astype(I32)
            word = info[2 * chosen : 3 * chosen]
            for side in range(SIDES):
                slot = local + (me ^ side) * (held * capacity)
                hits = [
                    jnp.where(flat[k : k + 1] == slot, word[k : k + 1], 0.0) for k in range(chosen)
                ]
                at = pl.ds(side * held * capacity, held * capacity)
                place_ref[j, at, :] = functools.reduce(jnp.add, hits).astype(BF16)
    for j, ref in enumerate(block_refs):
        scaled = jnp.dot(place_ref[j], ref[:tokens, :], preferred_element_type=F32).astype(BF16)
        for side, out_ref in enumerate((own_ref, other_ref)):
            for e in range(held):
                at = (side * held + e) * capacity
                out_ref[e, j * capacity : (j + 1) * capacity, :] = scaled[at : at + capacity]


def turn_kernel(dp, hidden_ref, out_ref):
    parts, held, _, units = hidden_ref.shape
    share, across = units // dp, dp // 2
    me = lax.axis_index("expert") if parts > 1 else 0
    mine = lax.axis_index("dp")
    core, row = mine % 2, mine // 2
    masks = MASKS if parts > 1 else (0,)
    for e in range(held):
        stacked = jnp.concatenate([hidden_ref[me ^ mask, e] for mask in masks], axis=0)
        turned = stacked.T
        for piece in range(dp):
            other = (piece % 2) ^ core
            step = (piece // 2 - row + across) % across
            out_ref[e, other, step] = turned[piece * share : (piece + 1) * share]


def stacked_rows(refs, e):
    return refs[0][e] if len(refs) == 1 else jnp.concatenate([ref[e] for ref in refs], axis=0)


def term_kernel(turned_ref, *refs):
    part_refs, keep_ref, give_ref = refs[:-2], refs[-2], refs[-1]
    held, _, across, share, slots = turned_ref.shape
    for e in range(held):
        scaled = stacked_rows(part_refs, e)
        for other, ref in ((1, give_ref), (0, keep_ref)):
            left = turned_ref[e, other].reshape(across * share, slots)
            term = jnp.dot(left, scaled, preferred_element_type=F32).astype(BF16)
            for step in range(across):
                ref[step, e] = term[step * share : (step + 1) * share]


def pair_kernel(keep_ref, got_ref, *out_refs):
    for step, ref in enumerate(out_refs, 1):
        ref[...] = (keep_ref[step].astype(F32) + got_ref[step].astype(F32)).astype(BF16)


def last_kernel(others, keep_ref, got_ref, *refs):
    out_ref = refs[-1]
    for e in range(keep_ref.shape[1]):
        total = keep_ref[0, e].astype(F32) + got_ref[0, e].astype(F32)
        for ref in refs[:others]:
            total = total + ref[e].astype(F32)
        out_ref[:, e, :] = total


def raw_kernel(parts, first, final, weight_ref, *refs):
    part_refs, refs = refs[:parts], refs[parts:]
    if not first:
        acc_ref, refs = refs[0], refs[1:]
    held = weight_ref.shape[0]
    for e in range(held):
        raw = lax.dot_general(
            stacked_rows(part_refs, e),
            weight_ref[e],
            (((1,), (1,)), ((), ())),
            preferred_element_type=F32,
        )
        if not first:
            raw = raw + acc_ref[e]
        if not final:
            refs[0][e] = raw
            continue
        hidden_ref, grad_ref, sums_ref = refs
        sources, _, own, units = hidden_ref.shape
        me = lax.axis_index("expert") if sources > 1 else 0
        folds = []
        for part, mask in enumerate(MASKS if sources > 1 else (0,)):
            block = raw[part * own : (part + 1) * own]
            grad_ref[me ^ mask, e] = block.astype(BF16)
            product = block * hidden_ref[me ^ mask, e].astype(F32)
            folds.append(
                functools.reduce(jnp.add, [product[:, i : i + 128] for i in range(0, units, 128)])
            )
        folded = jnp.concatenate(folds, axis=0) if len(folds) > 1 else folds[0]
        sums_ref[e : e + 1, :] = jnp.sum(folded.T, axis=0, keepdims=True)


def prob_kernel(direct, capacity, flat_ref, probs_ref, *refs):
    out_ref = refs[-1]
    chosen, tokens = flat_ref.shape
    if direct:
        values = []
        for mask in range(LINE * SIDES):
            at = MASKS.index(mask) * capacity
            ref = refs[mask // SIDES]
            values += [ref[mask % SIDES, e : e + 1, at : at + capacity] for e in range(ref.shape[1])]
        lanes = 128 // capacity
        values = jnp.concatenate(
            [
                jnp.concatenate([v.reshape(1, capacity) for v in values[i : i + lanes]], axis=1)
                for i in range(0, len(values), lanes)
            ],
            axis=0,
        )
        me = lax.axis_index("expert")
    else:
        values = refs[0][...]
        me = 0
    lines = values.shape[0]
    spare = jnp.zeros((-lines % 8, 128), F32)
    columns = jnp.concatenate([values, spare], axis=0).T if spare.size else values.T
    total, gates, word = gates_of(probs_ref[...])
    group = lines * 128 // (LINE * SIDES)
    picked = [jnp.zeros((1, tokens), F32) for _ in range(chosen)]
    for line in range(lines):
        at = lax.broadcasted_iota(I32, (128, tokens), 0) + line * 128
        slot = (at // group ^ me) * group + at % group
        for k in range(chosen):
            hit = jnp.where(flat_ref[k : k + 1, :] == slot, columns[:, line : line + 1], 0.0)
            picked[k] += jnp.sum(hit, axis=0, keepdims=True)
    picked = [picked[k] / word[k : k + 1] for k in range(chosen)]
    mixed = functools.reduce(jnp.add, [gates[k : k + 1] * picked[k] for k in range(chosen)])
    for k in range(chosen):
        out_ref[k : k + 1, :] = (picked[k] - mixed) / total


def chunks_of(features):
    return [features // 4] * 4


sds = jax.ShapeDtypeStruct


def relayed(grad_out, ids, probs, held, capacity, widths):
    tokens, features = grad_out.shape
    chosen = ids.shape[0]
    experts = LINE * SIDES * held

    def along(block, targets):
        pairs = [
            (p * SIDES + s, targets[p] * SIDES + s) for p in range(LINE) for s in range(SIDES)
        ]
        return lax.ppermute(block, "expert", pairs)

    scratch = [pltpu.SemaphoreType.DMA]
    flat, own = call(
        functools.partial(begin_kernel, experts, capacity),
        [sds((chosen, tokens), I32), sds((tokens + INFO, widths[0]), BF16)],
        ids,
        probs,
        grad_out,
        in_specs=[VMEM, VMEM, HBM],
        out_specs=[VMEM, VMEM],
        scratch_shapes=scratch,
    )
    arrived, place, start = [], None, 0
    for c, width in enumerate(widths):
        far = along(own, FAR)
        near = along(own, NEAR)
        start += width
        shape = sds(own.shape, BF16)
        if c + 1 < len(widths):
            hand, following = call(
                functools.partial(next_kernel, start),
                [shape, sds((tokens, widths[c + 1]), BF16)],
                own,
                far,
                grad_out,
                in_specs=[VMEM, VMEM, HBM],
                out_specs=[VMEM, VMEM],
                scratch_shapes=scratch,
            )
        else:
            hand, following = call(functools.partial(next_kernel, None), shape, own, far), None
        passed = along(hand, PASSED)
        blocks = [own, near, far, passed]
        rows = [sds((held, LINE * capacity, width), BF16)] * SIDES
        places = sds((LINE, SIDES * held * capacity, tokens), BF16)
        kernel = functools.partial(pick_kernel, held, capacity, chosen, c == 0)
        flops = 2 * LINE * SIDES * held * capacity * tokens * width
        if c == 0:
            place, mine, other = call(kernel, [places, *rows], *blocks, flops=flops)
        else:
            mine, other = call(kernel, rows, *blocks, place, flops=flops)
        swap = [(i, i ^ 1) for i in range(LINE * SIDES)]
        arrived.append([mine, lax.ppermute(other, "expert", swap)])
        own = following
    return flat, arrived


def exchanged(grad_out, ids, probs, groups, held, capacity, widths):
    tokens = grad_out.shape[0]
    experts = groups * held
    slots = experts * capacity
    _, _, word = gates_of(probs)
    flat = ids * capacity + jnp.concatenate(slots_of(ids, experts), axis=0).astype(I32)
    slot = lax.broadcasted_iota(I32, (slots, tokens), 0)
    place = sum(jnp.where(f == slot, w, 0.0) for f, w in zip(flat, word)).astype(BF16)
    arrived, start = [], 0
    for width in widths:
        rows = grad_out[:, start : start + width]
        sent = jnp.dot(place, rows, preferred_element_type=F32).astype(BF16)
        got = lax.all_to_all(
            sent.reshape(groups, held, capacity, width),
            "expert",
            split_axis=0,
            concat_axis=0,
            tiled=True,
        )
        arrived.append([got.transpose(1, 0, 2, 3).reshape(held, groups * capacity, width)])
        start += width
    return flat, arrived


def body(grad_out, route_ids, route_probs, hidden, w_down):
    groups = lax.axis_size("expert")
    dp = lax.axis_size("dp")
    held, units, features = w_down.shape
    capacity = hidden.shape[3]
    slots = groups * held * capacity
    per_expert = slots // held
    tokens, chosen = route_ids.shape
    share, across = units // dp, dp // 2
    direct = groups == LINE * SIDES
    widths = chunks_of(features)
    count = len(widths)

    ids, probs = route_ids.T, route_probs.T
    if direct:
        flat, arrived = relayed(grad_out, ids, probs, held, capacity, widths)
        saved = hidden[0]
    else:
        flat, arrived = exchanged(grad_out, ids, probs, groups, held, capacity, widths)
        saved = hidden[0].transpose(1, 0, 2, 3).reshape(1, held, per_expert, units)
    parts = len(arrived[0])
    turned = call(
        functools.partial(turn_kernel, dp),
        sds((held, 2, across, share, per_expert), BF16),
        saved,
    )

    flops = [2 * slots * units * w for w in widths]
    weight_grad, raw, start = None, None, 0
    for c, width in enumerate(widths):
        piece = sds((across, held, share, width), BF16)
        keep, give = call(term_kernel, [piece, piece], turned, *arrived[c], flops=flops[c])
        got = lax.ppermute(give, "dp", [(i, i ^ 1) for i in range(dp)])

        final = c == count - 1
        if final:
            outs = [sds(saved.shape, BF16), sds((held, per_expert), F32)]
            extra = [saved]
        else:
            outs, extra = [sds((held, per_expert, units), F32)], []
        extra = extra if c == 0 else [raw] + extra
        made = call(
            functools.partial(raw_kernel, parts, c == 0, final),
            outs,
            w_down,
            *arrived[c],
            *extra,
            flops=flops[c],
            grid=(1,),
            in_specs=[pl.BlockSpec((held, units, width), lambda i, at=start // width: (0, 0, at))]
            + [VMEM] * (parts + len(extra)),
            out_specs=[VMEM] * len(outs),
        )
        if final:
            hidden_grad, sums = made
        else:
            raw = made[0]

        piece = sds((held, share, width), BF16)
        pairs = call(pair_kernel, [piece] * (across - 1), keep, got)
        others = []
        for step in range(1, across):
            shift = [(2 * r + i, 2 * ((r + step) % across) + i) for r in range(across) for i in range(2)]
            others.append(lax.ppermute(pairs[step - 1], "dp", shift))
        first = pl.BlockSpec((1, held, share, width), lambda i: (0, 0, 0, 0))
        before = [] if c == 0 else [weight_grad]
        weight_grad = call(
            functools.partial(last_kernel, len(others)),
            sds((share, held, features), F32),
            keep,
            got,
            *others,
            *before,
            grid=(1,),
            in_specs=[first, first]
            + [VMEM] * len(others)
            + [pl.BlockSpec(memory_space=pl.ANY)] * len(before),
            out_specs=pl.BlockSpec((share, held, width), lambda i, at=start // width: (0, 0, at)),
            input_output_aliases={2 + len(others): 0} if before else {},
        )
        start += width

    if direct:
        swap = [(i, i ^ 1) for i in range(groups)]
        both = jnp.stack([sums, lax.ppermute(sums, "expert", swap)])
        returned = [both] + [
            lax.ppermute(both, "expert", [(i, i ^ (SIDES * d)) for i in range(groups)])
            for d in range(1, LINE)
        ]
    else:
        sums = sums.reshape(held, groups, capacity).transpose(1, 0, 2).reshape(groups, -1)
        hidden_grad = hidden_grad.reshape(held, groups, capacity, units).transpose(1, 0, 2, 3)
        returned = lax.all_to_all(sums, "expert", split_axis=0, concat_axis=0, tiled=True)
        returned = [returned.reshape(-1, 128)]
    prob_grad = call(
        functools.partial(prob_kernel, direct, capacity),
        sds((chosen, tokens), F32),
        flat,
        probs,
        *returned,
    ).T
    return (hidden_grad.reshape(hidden.shape), prob_grad, weight_grad)


def solution(mesh):
    in_specs = (
        P(("dp", "expert"), None),
        P(("dp", "expert"), None),
        P(("dp", "expert"), None),
        P("dp", None, "expert", None, None),
        P("expert", None, None),
    )
    out_specs = (
        P("dp", None, "expert", None, None),
        P(("dp", "expert"), None),
        P("dp", "expert", None),
    )
    return jax.shard_map(body, mesh=mesh, in_specs=in_specs, out_specs=out_specs, check_vma=False)
```

```python
import functools

import jax
import jax.numpy as jnp
from jax import lax
from jax.experimental import pallas as pl
from jax.experimental.pallas import tpu as pltpu
from jax.sharding import PartitionSpec as P

F32, BF16, I32 = jnp.float32, jnp.bfloat16, jnp.int32
PARAMS = pltpu.CompilerParams(vmem_limit_bytes=24 * 1024 * 1024)
VMEM = pl.BlockSpec(memory_space=pltpu.VMEM)
ANY = pl.BlockSpec(memory_space=pl.ANY)
HBM = pl.BlockSpec(memory_space=pltpu.HBM)

LINE, SIDES = 4, 2
INFO = 16


def nbytes(shapes):
    return sum(x.size * x.dtype.itemsize for x in jax.tree.leaves(shapes))


class Chain:
    def __init__(self):
        self.last = None

    def __call__(self, kernel, outs, *args, flops=0, in_specs=None, keep=True, **kw):
        in_specs = list(in_specs or [VMEM] * len(args))
        count = len(args)
        body = kernel
        if self.last is not None:
            args, in_specs = (*args, self.last), in_specs + [ANY]

            def body(*refs):
                kernel(*refs[:count], *refs[count + 1 :])

        made = pl.pallas_call(
            body,
            out_shape=outs,
            in_specs=in_specs,
            compiler_params=PARAMS,
            cost_estimate=pl.CostEstimate(flops=1, bytes_accessed=1, transcendentals=0),
            **kw,
        )(*args)
        if keep:
            self.last = jax.tree.leaves(made)[-1]
        return made


def gates_of(probs):
    total = jnp.sum(probs, axis=0, keepdims=True)
    gates = probs / total
    return total, gates, gates.astype(BF16).astype(F32)


def slots_of(ids, experts):
    chosen, tokens = ids.shape
    expert = lax.broadcasted_iota(I32, (experts, tokens), 0)
    named = [ids[k : k + 1] == expert for k in range(chosen)]
    hits = functools.reduce(jnp.add, [n.astype(F32) for n in named]).astype(BF16)
    row = lax.broadcasted_iota(I32, (tokens, tokens), 0)
    earlier = (row < lax.broadcasted_iota(I32, (tokens, tokens), 1)).astype(F32).astype(BF16)
    before = jnp.dot(hits, earlier, preferred_element_type=F32)
    return [jnp.sum(jnp.where(n, before, 0.0), axis=0, keepdims=True) for n in named]


def begin_kernel(experts, capacity, ids_ref, probs_ref, rows_ref, flat_ref, rest_ref, out_ref, sems):
    chosen, tokens = ids_ref.shape
    width = out_ref.shape[1]
    copies = [
        pltpu.make_async_copy(rows_ref.at[:, :width], out_ref.at[:tokens], sems.at[0]),
        pltpu.make_async_copy(rows_ref.at[:, width:], rest_ref, sems.at[1]),
    ]
    for copy in copies:
        copy.start()
    ids = ids_ref[...]
    _, _, word = gates_of(probs_ref[...])
    slots = slots_of(ids, experts)
    for k in range(chosen):
        flat_ref[k : k + 1, :] = ids[k : k + 1] * capacity + slots[k].astype(I32)
    rest = jnp.zeros((INFO - 3 * chosen, tokens), F32)
    info = jnp.concatenate([ids.astype(F32), *slots, word, rest], axis=0).astype(BF16)
    out_ref[tokens:, :tokens] = info
    if width > tokens:
        out_ref[tokens:, tokens:] = jnp.zeros((INFO, width - tokens), BF16)
    for copy in copies:
        copy.wait()


def pick_kernel(held, capacity, chosen, start, own_ref, other_ref, *refs):
    tokens = own_ref.shape[0] - (INFO if start is None else 0)
    rows = held * capacity
    if start is None:
        place_ref, out_refs = refs[-1], refs[:-1]
        me = lax.axis_index("expert")
        local = lax.broadcasted_iota(I32, (rows, tokens), 0)
        for side, ref in enumerate((own_ref, other_ref)):
            info = ref[tokens:, :tokens].astype(F32)
            flat = (info[:chosen] * capacity + info[chosen : 2 * chosen]).astype(I32)
            word = info[2 * chosen : 3 * chosen]
            for d in range(LINE):
                slot = local + (me ^ (SIDES * d)) * rows
                hits = [
                    jnp.where(flat[k : k + 1] == slot, word[k : k + 1], 0.0) for k in range(chosen)
                ]
                place_ref[side, d * rows : (d + 1) * rows, :] = functools.reduce(
                    jnp.add, hits
                ).astype(BF16)
        blocks = own_ref[:tokens, :], other_ref[:tokens, :]
    else:
        place_ref, out_refs = refs[0], refs[1:]
        width, first = out_refs[0].shape[2], own_ref.shape[1] - other_ref.shape[1]
        blocks = (
            own_ref[:, start : start + width],
            other_ref[:, start - first : start - first + width],
        )
    for side, block in enumerate(blocks):
        scaled = jnp.dot(place_ref[side], block, preferred_element_type=F32).astype(BF16)
        for d, out_ref in enumerate(out_refs):
            for e in range(held):
                at = d * rows + e * capacity
                out_ref[e, side * capacity : (side + 1) * capacity, :] = scaled[at : at + capacity]


def turn_kernel(dp, hidden_ref, out_ref):
    parts, held, _, units = hidden_ref.shape
    share, across = units // dp, dp // 2
    me = lax.axis_index("expert") if parts > 1 else 0
    mine = lax.axis_index("dp")
    core, row = mine % 2, mine // 2
    for e in range(held):
        stacked = jnp.concatenate([hidden_ref[me ^ mask, e] for mask in range(parts)], axis=0)
        turned = stacked.T
        for piece in range(dp):
            other = (piece % 2) ^ core
            step = (piece // 2 - row + across) % across
            out_ref[e, other, step] = turned[piece * share : (piece + 1) * share]


def stacked_rows(refs, e):
    return refs[0][e] if len(refs) == 1 else jnp.concatenate([ref[e] for ref in refs], axis=0)


def term_kernel(turned_ref, *refs):
    part_refs, keep_ref, give_ref = refs[:-2], refs[-2], refs[-1]
    held, _, across, share, slots = turned_ref.shape
    for e in range(held):
        scaled = stacked_rows(part_refs, e)
        for other, ref in ((1, give_ref), (0, keep_ref)):
            left = turned_ref[e, other].reshape(across * share, slots)
            term = jnp.dot(left, scaled, preferred_element_type=F32).astype(BF16)
            for step in range(across):
                ref[step, e] = term[step * share : (step + 1) * share]


def pair_kernel(keep_ref, got_ref, *out_refs):
    for step, ref in enumerate(out_refs, 1):
        ref[...] = (keep_ref[step].astype(F32) + got_ref[step].astype(F32)).astype(BF16)


def last_kernel(others, start, keep_ref, got_ref, *refs):
    out_ref, mark_ref, total_ref, sem = refs[-4:]
    mark_ref[...] = jnp.zeros(mark_ref.shape, F32)
    for e in range(keep_ref.shape[1]):
        total = keep_ref[0, e].astype(F32) + got_ref[0, e].astype(F32)
        for ref in refs[:others]:
            total = total + ref[e].astype(F32)
        total_ref[:, e, :] = total
    copy = pltpu.make_async_copy(
        total_ref, out_ref.at[:, :, start : start + total_ref.shape[2]], sem
    )
    copy.start()
    copy.wait()


def raw_kernel(parts, start, final, weight_ref, *refs):
    part_refs, refs = refs[:parts], refs[parts:]
    if start:
        acc_ref, refs = refs[0], refs[1:]
    width = part_refs[0].shape[2]
    for e in range(weight_ref.shape[0]):
        raw = lax.dot_general(
            stacked_rows(part_refs, e),
            weight_ref[e, :, start : start + width],
            (((1,), (1,)), ((), ())),
            preferred_element_type=F32,
        )
        if start:
            raw = raw + acc_ref[e]
        if not final:
            refs[0][e] = raw
            continue
        hidden_ref, grad_ref, sums_ref = refs
        sources, _, own, units = hidden_ref.shape
        me = lax.axis_index("expert") if sources > 1 else 0
        folds = []
        for mask in range(sources):
            block = raw[mask * own : (mask + 1) * own]
            grad_ref[me ^ mask, e] = block.astype(BF16)
            product = block * hidden_ref[me ^ mask, e].astype(F32)
            folds.append(
                functools.reduce(jnp.add, [product[:, i : i + 128] for i in range(0, units, 128)])
            )
        folded = jnp.concatenate(folds, axis=0) if len(folds) > 1 else folds[0]
        sums_ref[e : e + 1, :] = jnp.sum(folded.T, axis=0, keepdims=True)


def prob_kernel(direct, capacity, flat_ref, probs_ref, *refs):
    out_ref = refs[-1]
    chosen, tokens = flat_ref.shape
    if direct:
        values = []
        for mask in range(LINE * SIDES):
            at = mask * capacity
            ref = refs[mask // SIDES]
            values += [ref[mask % SIDES, e : e + 1, at : at + capacity] for e in range(ref.shape[1])]
        lanes = 128 // capacity
        values = jnp.concatenate(
            [
                jnp.concatenate([v.reshape(1, capacity) for v in values[i : i + lanes]], axis=1)
                for i in range(0, len(values), lanes)
            ],
            axis=0,
        )
        me = lax.axis_index("expert")
    else:
        values = refs[0][...]
        me = 0
    lines = values.shape[0]
    spare = jnp.zeros((-lines % 8, 128), F32)
    columns = jnp.concatenate([values, spare], axis=0).T if spare.size else values.T
    total, gates, word = gates_of(probs_ref[...])
    group = lines * 128 // (LINE * SIDES)
    picked = [jnp.zeros((1, tokens), F32) for _ in range(chosen)]
    for line in range(lines):
        at = lax.broadcasted_iota(I32, (128, tokens), 0) + line * 128
        slot = (at // group ^ me) * group + at % group
        for k in range(chosen):
            hit = jnp.where(flat_ref[k : k + 1, :] == slot, columns[:, line : line + 1], 0.0)
            picked[k] += jnp.sum(hit, axis=0, keepdims=True)
    picked = [picked[k] / word[k : k + 1] for k in range(chosen)]
    mixed = functools.reduce(jnp.add, [gates[k : k + 1] * picked[k] for k in range(chosen)])
    for k in range(chosen):
        out_ref[k : k + 1, :] = (picked[k] - mixed) / total


def chunks_of(features):
    return [features // 4] * 4


sds = jax.ShapeDtypeStruct


class Relay:
    def __init__(self, call, grad_out, ids, probs, held, capacity, widths):
        tokens, features = grad_out.shape
        self.call, self.rows, self.held, self.capacity = call, grad_out, held, capacity
        self.chosen, self.widths, self.place = ids.shape[0], widths, None
        self.flat, rest, self.first = call(
            functools.partial(begin_kernel, LINE * SIDES * held, capacity),
            [
                sds(ids.shape, I32),
                sds((tokens, features - widths[0]), BF16),
                sds((tokens + INFO, widths[0]), BF16),
            ],
            ids,
            probs,
            grad_out,
            in_specs=[VMEM, VMEM, HBM],
            scratch_shapes=[pltpu.SemaphoreType.DMA((2,))],
        )
        self.first_other = self.send(self.first, 1)
        self.rest_other = self.send(rest, 1)

    def send(self, block, mask):
        return lax.ppermute(block, "expert", [(i, i ^ mask) for i in range(LINE * SIDES)])

    def chunk(self, c):
        held, capacity, tokens = self.held, self.capacity, self.rows.shape[0]
        rows = [sds((held, SIDES * capacity, self.widths[c]), BF16)] * LINE
        place = sds((SIDES, LINE * held * capacity, tokens), BF16)
        flops = 2 * SIDES * LINE * held * capacity * tokens * self.widths[c]
        start = sum(self.widths[:c]) if c else None
        kernel = functools.partial(pick_kernel, held, capacity, self.chosen, start)
        if c == 0:
            *sent, self.place = self.call(
                kernel, [*rows, place], self.first, self.first_other, flops=flops
            )
        else:
            sent = self.call(kernel, rows, self.rows, self.rest_other, self.place, flops=flops)
        return [sent[0]] + [self.send(sent[d], SIDES * d) for d in range(1, LINE)]


def exchanged(grad_out, ids, probs, groups, held, capacity, widths):
    tokens = grad_out.shape[0]
    experts = groups * held
    slots = experts * capacity
    _, _, word = gates_of(probs)
    flat = ids * capacity + jnp.concatenate(slots_of(ids, experts), axis=0).astype(I32)
    slot = lax.broadcasted_iota(I32, (slots, tokens), 0)
    place = sum(jnp.where(f == slot, w, 0.0) for f, w in zip(flat, word)).astype(BF16)
    arrived, start = [], 0
    for width in widths:
        rows = grad_out[:, start : start + width]
        sent = jnp.dot(place, rows, preferred_element_type=F32).astype(BF16)
        got = lax.all_to_all(
            sent.reshape(groups, held, capacity, width),
            "expert",
            split_axis=0,
            concat_axis=0,
            tiled=True,
        )
        arrived.append([got.transpose(1, 0, 2, 3).reshape(held, groups * capacity, width)])
        start += width
    return flat, arrived


def body(grad_out, route_ids, route_probs, hidden, w_down):
    groups = lax.axis_size("expert")
    dp = lax.axis_size("dp")
    held, units, features = w_down.shape
    capacity = hidden.shape[3]
    slots = groups * held * capacity
    per_expert = slots // held
    tokens, chosen = route_ids.shape
    share, across = units // dp, dp // 2
    direct = groups == LINE * SIDES
    widths = chunks_of(features)
    count = len(widths)

    ids, probs = route_ids.T, route_probs.T
    call = Chain()
    if direct:
        relay = Relay(call, grad_out, ids, probs, held, capacity, widths)
        flat, saved = relay.flat, hidden[0]
    else:
        flat, arrived = exchanged(grad_out, ids, probs, groups, held, capacity, widths)
        saved = hidden[0].transpose(1, 0, 2, 3).reshape(1, held, per_expert, units)
    turned = call(
        functools.partial(turn_kernel, dp),
        sds((held, 2, across, share, per_expert), BF16),
        saved,
    )
    if direct:
        arrived = [relay.chunk(c) for c in range(min(2, count))]

    starts = [sum(widths[:c]) for c in range(count)]
    flops = [2 * slots * units * w for w in widths]
    state = {"raw": None, "grad": None}
    summed = []

    def reduced(c):
        parts, width = arrived[c], widths[c]
        piece = sds((across, held, share, width), BF16)
        keep, give = call(term_kernel, [piece, piece], turned, *parts, flops=flops[c])
        got = lax.ppermute(give, "dp", [(i, i ^ 1) for i in range(dp)])
        final = c == count - 1
        if final:
            outs = [sds(saved.shape, BF16), sds((held, per_expert), F32)]
        else:
            outs = [sds((held, per_expert, units), F32)]
        extra = ([state["raw"]] if c else []) + ([saved] if final else [])
        kernel = functools.partial(raw_kernel, len(parts), starts[c], final)
        made = call(kernel, outs, w_down, *parts, *extra, flops=flops[c])
        state["raw"] = made if final else made[0]
        pairs = call(pair_kernel, [sds((held, share, width), BF16)] * (across - 1), keep, got)
        others = []
        for step in range(1, across):
            shift = [(2 * r + i, 2 * ((r + step) % across) + i) for r in range(across) for i in range(2)]
            others.append(lax.ppermute(pairs[step - 1], "dp", shift))
        summed.append((keep, got, others))

    def finished(c):
        keep, got, others = summed[c]
        before = [] if state["grad"] is None else [state["grad"]]
        count = 2 + len(others)
        state["grad"], _ = call(
            functools.partial(last_kernel, len(others), starts[c]),
            [sds((share, held, features), F32), sds((8, 128), F32)],
            keep,
            got,
            *others,
            *before,
            in_specs=[VMEM] * count + [ANY] * len(before),
            out_specs=[ANY, VMEM],
            input_output_aliases={count: 0} if before else {},
            scratch_shapes=[
                pltpu.VMEM((share, held, widths[c]), F32),
                pltpu.SemaphoreType.DMA,
            ],
        )

    for c in range(count):
        reduced(c)
        if direct and c + 2 < count:
            arrived.append(relay.chunk(c + 2))
        if c >= 1:
            finished(c - 1)
    hidden_grad, sums = state["raw"]

    if direct:
        swap = [(i, i ^ 1) for i in range(groups)]
        both = jnp.stack([sums, lax.ppermute(sums, "expert", swap)])
        returned = [both] + [
            lax.ppermute(both, "expert", [(i, i ^ (SIDES * d)) for i in range(groups)])
            for d in range(1, LINE)
        ]
    else:
        sums = sums.reshape(held, groups, capacity).transpose(1, 0, 2).reshape(groups, -1)
        hidden_grad = hidden_grad.reshape(held, groups, capacity, units).transpose(1, 0, 2, 3)
        returned = lax.all_to_all(sums, "expert", split_axis=0, concat_axis=0, tiled=True)
        returned = [returned.reshape(-1, 128)]
    prob_grad = call(
        functools.partial(prob_kernel, direct, capacity),
        sds((chosen, tokens), F32),
        flat,
        probs,
        *returned,
        keep=False,
    ).T
    finished(count - 1)
    weight_grad = state["grad"]
    return (hidden_grad.reshape(hidden.shape), prob_grad, weight_grad)


def solution(mesh):
    in_specs = (
        P(("dp", "expert"), None),
        P(("dp", "expert"), None),
        P(("dp", "expert"), None),
        P("dp", None, "expert", None, None),
        P("expert", None, None),
    )
    out_specs = (
        P("dp", None, "expert", None, None),
        P(("dp", "expert"), None),
        P("dp", "expert", None),
    )
    return jax.shard_map(body, mesh=mesh, in_specs=in_specs, out_specs=out_specs, check_vma=False)
```

```python
import functools

import jax
import jax.numpy as jnp
from jax import lax
from jax.experimental import pallas as pl
from jax.experimental.pallas import tpu as pltpu
from jax.sharding import PartitionSpec as P

F32, BF16, I32 = jnp.float32, jnp.bfloat16, jnp.int32
VMEM = pl.BlockSpec(memory_space=pltpu.VMEM)
ANY = pl.BlockSpec(memory_space=pl.ANY)
HBM = pl.BlockSpec(memory_space=pltpu.HBM)

LINE, SIDES = 4, 2
INFO = 16


class Chain:
    def __init__(self):
        self.last = None

    def __call__(self, kernel, outs, *args, in_specs=None, keep=True, after=(), room=24, **kw):
        in_specs = list(in_specs or [VMEM] * len(args))
        count = len(args)
        body = kernel
        unread = [*after] if self.last is None else [self.last, *after]
        if unread:
            args, in_specs = (*args, *unread), in_specs + [ANY] * len(unread)

            def body(*refs):
                kernel(*refs[:count], *refs[count + len(unread) :])

        made = pl.pallas_call(
            body,
            out_shape=outs,
            in_specs=in_specs,
            compiler_params=pltpu.CompilerParams(vmem_limit_bytes=room * 1024 * 1024),
            cost_estimate=pl.CostEstimate(flops=1, bytes_accessed=1, transcendentals=0),
            **kw,
        )(*args)
        if keep:
            self.last = min(jax.tree.leaves(made), key=lambda x: x.size)
        return made


def gates_of(probs):
    total = jnp.sum(probs, axis=0, keepdims=True)
    gates = probs / total
    return total, gates, gates.astype(BF16).astype(F32)


def slots_of(ids, experts):
    chosen, tokens = ids.shape
    expert = lax.broadcasted_iota(I32, (experts, tokens), 0)
    named = [ids[k : k + 1] == expert for k in range(chosen)]
    hits = functools.reduce(jnp.add, [n.astype(F32) for n in named]).astype(BF16)
    row = lax.broadcasted_iota(I32, (tokens, tokens), 0)
    earlier = (row < lax.broadcasted_iota(I32, (tokens, tokens), 1)).astype(F32).astype(BF16)
    before = jnp.dot(hits, earlier, preferred_element_type=F32)
    return [jnp.sum(jnp.where(n, before, 0.0), axis=0, keepdims=True) for n in named]


def begin_kernel(experts, capacity, ids_ref, probs_ref, rows_ref, flat_ref, out_ref, *scratch):
    ids_got, probs_got, sems = scratch
    chosen, tokens = ids_got.shape
    width = out_ref.shape[1]
    copies = [
        pltpu.make_async_copy(ids_ref, ids_got, sems.at[0]),
        pltpu.make_async_copy(probs_ref, probs_got, sems.at[1]),
        pltpu.make_async_copy(rows_ref.at[:, :width], out_ref.at[:tokens], sems.at[2]),
    ]
    for copy in copies:
        copy.start()
    for copy in copies:
        copy.wait()
    ids = ids_got[...]
    _, _, word = gates_of(probs_got[...])
    slots = slots_of(ids, experts)
    for k in range(chosen):
        flat_ref[k : k + 1, :] = ids[k : k + 1] * capacity + slots[k].astype(I32)
    rest = jnp.zeros((INFO - 3 * chosen, tokens), F32)
    info = jnp.concatenate([ids.astype(F32), *slots, word, rest], axis=0).astype(BF16)
    out_ref[tokens:, :tokens] = info
    if width > tokens:
        out_ref[tokens:, tokens:] = jnp.zeros((INFO, width - tokens), BF16)


def pick_kernel(held, capacity, chosen, start, own_ref, other_ref, *refs):
    tokens = own_ref.shape[0] - (INFO if start is None else 0)
    rows = held * capacity
    if start is None:
        rows_ref, *out_refs, place_ref, rest_ref, sem = refs
        copy = pltpu.make_async_copy(rows_ref.at[:, own_ref.shape[1] :], rest_ref, sem)
        copy.start()
        me = lax.axis_index("expert")
        local = lax.broadcasted_iota(I32, (rows, tokens), 0)
        for side, ref in enumerate((own_ref, other_ref)):
            info = ref[tokens:, :tokens].astype(F32)
            flat = (info[:chosen] * capacity + info[chosen : 2 * chosen]).astype(I32)
            word = info[2 * chosen : 3 * chosen]
            for d in range(LINE):
                slot = local + (me ^ (SIDES * d)) * rows
                hits = [
                    jnp.where(flat[k : k + 1] == slot, word[k : k + 1], 0.0) for k in range(chosen)
                ]
                place_ref[side, d * rows : (d + 1) * rows, :] = functools.reduce(
                    jnp.add, hits
                ).astype(BF16)
        blocks = own_ref[:tokens, :], other_ref[:tokens, :]
    else:
        place_ref, out_refs = refs[0], refs[1:]
        width, first = out_refs[0].shape[2], own_ref.shape[1] - other_ref.shape[1]
        blocks = (
            own_ref[:, start : start + width],
            other_ref[:, start - first : start - first + width],
        )
    for side, block in enumerate(blocks):
        scaled = jnp.dot(place_ref[side], block, preferred_element_type=F32).astype(BF16)
        for d, out_ref in enumerate(out_refs):
            for e in range(held):
                at = d * rows + e * capacity
                out_ref[e, side * capacity : (side + 1) * capacity, :] = scaled[at : at + capacity]
    if start is None:
        copy.wait()


def turn_kernel(dp, hidden_ref, *refs):
    out_ref = refs[-1]
    parts, held, _, units = hidden_ref.shape
    share, across = units // dp, dp // 2
    me = lax.axis_index("expert") if parts > 1 else 0
    mine = lax.axis_index("dp")
    core, row = mine % 2, mine // 2
    for e in range(held):
        stacked = jnp.concatenate([hidden_ref[me ^ mask, e] for mask in range(parts)], axis=0)
        turned = stacked.T
        for piece in range(dp):
            other = (piece % 2) ^ core
            step = (piece // 2 - row + across) % across
            out_ref[e, other, step] = turned[piece * share : (piece + 1) * share]


def stacked_rows(refs, e):
    return refs[0][e] if len(refs) == 1 else jnp.concatenate([ref[e] for ref in refs], axis=0)


def term_kernel(turned_ref, *refs):
    part_refs, keep_ref, give_ref = refs[:-2], refs[-2], refs[-1]
    held, _, across, share, slots = turned_ref.shape
    for e in range(held):
        scaled = stacked_rows(part_refs, e)
        for other, ref in ((1, give_ref), (0, keep_ref)):
            left = turned_ref[e, other].reshape(across * share, slots)
            term = jnp.dot(left, scaled, preferred_element_type=F32).astype(BF16)
            for step in range(across):
                ref[step, e] = term[step * share : (step + 1) * share]


def pair_kernel(keep_ref, got_ref, *out_refs):
    for step in range(1, keep_ref.shape[0]):
        start = 0
        for ref in out_refs[2 * step - 2 : 2 * step]:
            at = slice(start, start + ref.shape[1])
            pair = keep_ref[step, :, at].astype(F32) + got_ref[step, :, at].astype(F32)
            ref[...] = pair.astype(BF16)
            start += ref.shape[1]


def last_kernel(others, start, keep_ref, got_ref, *refs):
    out_ref, mark_ref, total_ref, sem = refs[-4:]
    mark_ref[...] = jnp.zeros(mark_ref.shape, F32)
    cut = refs[0].shape[1]
    for e in range(keep_ref.shape[1]):
        for part, at in enumerate((slice(0, cut), slice(cut, keep_ref.shape[2]))):
            total = keep_ref[0, e, at].astype(F32) + got_ref[0, e, at].astype(F32)
            for ref in refs[part:others:2]:
                total = total + ref[e].astype(F32)
            total_ref[at, e, :] = total
    copy = pltpu.make_async_copy(
        total_ref, out_ref.at[:, :, start : start + total_ref.shape[2]], sem
    )
    copy.start()
    copy.wait()


def raw_kernel(parts, start, final, weight_ref, *refs):
    part_refs, refs = refs[:parts], refs[parts:]
    if start:
        acc_ref, refs = refs[0], refs[1:]
    width = part_refs[0].shape[2]
    for e in range(weight_ref.shape[0]):
        raw = lax.dot_general(
            stacked_rows(part_refs, e),
            weight_ref[e, :, start : start + width],
            (((1,), (1,)), ((), ())),
            preferred_element_type=F32,
        )
        if start:
            raw = raw + acc_ref[e]
        if not final:
            refs[0][e] = raw
            continue
        hidden_ref, grad_ref, sums_ref = refs
        sources, _, own, units = hidden_ref.shape
        me = lax.axis_index("expert") if sources > 1 else 0
        folds = []
        for mask in range(sources):
            block = raw[mask * own : (mask + 1) * own]
            grad_ref[me ^ mask, e] = block.astype(BF16)
            product = block * hidden_ref[me ^ mask, e].astype(F32)
            folds.append(
                functools.reduce(jnp.add, [product[:, i : i + 128] for i in range(0, units, 128)])
            )
        folded = jnp.concatenate(folds, axis=0) if len(folds) > 1 else folds[0]
        sums_ref[e : e + 1, :] = jnp.sum(folded.T, axis=0, keepdims=True)


def prob_kernel(direct, capacity, flat_ref, probs_ref, *refs):
    out_ref = refs[-1]
    chosen, tokens = flat_ref.shape
    if direct:
        values = []
        for mask in range(LINE * SIDES):
            at = mask * capacity
            ref = refs[mask // SIDES]
            values += [ref[mask % SIDES, e : e + 1, at : at + capacity] for e in range(ref.shape[1])]
        lanes = 128 // capacity
        values = jnp.concatenate(
            [
                jnp.concatenate([v.reshape(1, capacity) for v in values[i : i + lanes]], axis=1)
                for i in range(0, len(values), lanes)
            ],
            axis=0,
        )
        me = lax.axis_index("expert")
    else:
        values = refs[0][...]
        me = 0
    lines = values.shape[0]
    spare = jnp.zeros((-lines % 8, 128), F32)
    columns = jnp.concatenate([values, spare], axis=0).T if spare.size else values.T
    total, gates, word = gates_of(probs_ref[...])
    group = lines * 128 // (LINE * SIDES)
    picked = [jnp.zeros((1, tokens), F32) for _ in range(chosen)]
    for line in range(lines):
        at = lax.broadcasted_iota(I32, (128, tokens), 0) + line * 128
        slot = (at // group ^ me) * group + at % group
        for k in range(chosen):
            hit = jnp.where(flat_ref[k : k + 1, :] == slot, columns[:, line : line + 1], 0.0)
            picked[k] += jnp.sum(hit, axis=0, keepdims=True)
    picked = [picked[k] / word[k : k + 1] for k in range(chosen)]
    mixed = functools.reduce(jnp.add, [gates[k : k + 1] * picked[k] for k in range(chosen)])
    for k in range(chosen):
        out_ref[k : k + 1, :] = (picked[k] - mixed) / total


def chunks_of(features):
    unit = features // 16
    return [5 * unit, 5 * unit, 4 * unit, 2 * unit]


sds = jax.ShapeDtypeStruct


class Relay:
    def __init__(self, call, grad_out, ids, probs, held, capacity, widths):
        tokens, features = grad_out.shape
        self.call, self.rows, self.held, self.capacity = call, grad_out, held, capacity
        self.chosen, self.widths, self.place = ids.shape[0], widths, None
        self.flat, self.first = call(
            functools.partial(begin_kernel, LINE * SIDES * held, capacity),
            [sds(ids.shape, I32), sds((tokens + INFO, widths[0]), BF16)],
            ids,
            probs,
            grad_out,
            in_specs=[HBM] * 3,
            scratch_shapes=[
                pltpu.VMEM(ids.shape, I32),
                pltpu.VMEM(probs.shape, F32),
                pltpu.SemaphoreType.DMA((3,)),
            ],
            room=60,
        )
        self.first_other = self.send(self.first, 1)

    def send(self, block, mask):
        return lax.ppermute(block, "expert", [(i, i ^ mask) for i in range(LINE * SIDES)])

    def chunk(self, c):
        held, capacity, tokens = self.held, self.capacity, self.rows.shape[0]
        rows = [sds((held, SIDES * capacity, self.widths[c]), BF16)] * LINE
        place = sds((SIDES, LINE * held * capacity, tokens), BF16)
        start = sum(self.widths[:c]) if c else None
        kernel = functools.partial(pick_kernel, held, capacity, self.chosen, start)
        if c == 0:
            rest = sds((tokens, self.rows.shape[1] - self.widths[0]), BF16)
            *sent, self.place, rest = self.call(
                kernel,
                [*rows, place, rest],
                self.first,
                self.first_other,
                self.rows,
                in_specs=[VMEM, VMEM, HBM],
                scratch_shapes=[pltpu.SemaphoreType.DMA],
            )
        else:
            sent = self.call(kernel, rows, self.rows, self.rest_other, self.place)
        got = [sent[0]] + [None] * (LINE - 1)
        for d in range(LINE - 1, 0, -1):
            got[d] = self.send(sent[d], SIDES * d)
        if c == 0:
            self.rest_other = self.send(rest, 1)
        return got


def exchanged(grad_out, ids, probs, groups, held, capacity, widths):
    tokens = grad_out.shape[0]
    experts = groups * held
    slots = experts * capacity
    _, _, word = gates_of(probs)
    flat = ids * capacity + jnp.concatenate(slots_of(ids, experts), axis=0).astype(I32)
    slot = lax.broadcasted_iota(I32, (slots, tokens), 0)
    place = sum(jnp.where(f == slot, w, 0.0) for f, w in zip(flat, word)).astype(BF16)
    arrived, start = [], 0
    for width in widths:
        rows = grad_out[:, start : start + width]
        sent = jnp.dot(place, rows, preferred_element_type=F32).astype(BF16)
        got = lax.all_to_all(
            sent.reshape(groups, held, capacity, width),
            "expert",
            split_axis=0,
            concat_axis=0,
            tiled=True,
        )
        arrived.append([got.transpose(1, 0, 2, 3).reshape(held, groups * capacity, width)])
        start += width
    return flat, arrived


def body(grad_out, route_ids, route_probs, hidden, w_down):
    groups = lax.axis_size("expert")
    dp = lax.axis_size("dp")
    held, units, features = w_down.shape
    capacity = hidden.shape[3]
    slots = groups * held * capacity
    per_expert = slots // held
    tokens, chosen = route_ids.shape
    share, across = units // dp, dp // 2
    direct = groups == LINE * SIDES
    widths = chunks_of(features)
    count = len(widths)

    ids, probs = route_ids.T, route_probs.T
    call = Chain()
    if direct:
        relay = Relay(call, grad_out, ids, probs, held, capacity, widths)
        flat, saved = relay.flat, hidden[0]
    else:
        flat, arrived = exchanged(grad_out, ids, probs, groups, held, capacity, widths)
        saved = hidden[0].transpose(1, 0, 2, 3).reshape(1, held, per_expert, units)
    turned = call(
        functools.partial(turn_kernel, dp),
        sds((held, 2, across, share, per_expert), BF16),
        saved,
        *([grad_out, w_down] if direct else []),
    )
    if direct:
        arrived = [relay.chunk(c) for c in range(min(2, count))]

    starts = [sum(widths[:c]) for c in range(count)]
    state = {"raw": None, "grad": None}
    summed = []

    def reduced(c):
        parts, width = arrived[c], widths[c]
        piece = sds((across, held, share, width), BF16)
        after = summed[-1][2][:1] if c else ()
        keep, give = call(term_kernel, [piece, piece], turned, *parts, after=after)
        got = lax.ppermute(give, "dp", [(i, i ^ 1) for i in range(dp)])
        final = c == count - 1
        if final:
            outs = [sds(saved.shape, BF16), sds((held, per_expert), F32)]
        else:
            outs = [sds((held, per_expert, units), F32)]
        extra = ([state["raw"]] if c else []) + ([saved] if final else [])
        kernel = functools.partial(raw_kernel, len(parts), starts[c], final)
        made = call(
            kernel,
            outs,
            w_down,
            *parts,
            *extra,
        )
        state["raw"] = made if final else made[0]
        cut = 16 * max(1, share // 64)
        pieces = [sds((held, rows, width), BF16) for rows in (cut, share - cut)]
        pairs = call(pair_kernel, pieces * (across - 1), keep, got)
        others = []
        for i, pair in enumerate(pairs):
            step = 1 + i // 2
            shift = [(2 * r + k, 2 * ((r + step) % across) + k) for r in range(across) for k in range(2)]
            others.append(lax.ppermute(pair, "dp", shift))
        summed.append((keep, got, others))

    def finished(c):
        keep, got, others = summed[c]
        before = [] if state["grad"] is None else [state["grad"]]
        count = 2 + len(others)
        state["grad"], _ = call(
            functools.partial(last_kernel, len(others), starts[c]),
            [sds((share, held, features), F32), sds((8, 128), F32)],
            keep,
            got,
            *others,
            *before,
            in_specs=[VMEM] * count + [ANY] * len(before),
            out_specs=[ANY, VMEM],
            input_output_aliases={count: 0} if before else {},
            scratch_shapes=[
                pltpu.VMEM((share, held, widths[c]), F32),
                pltpu.SemaphoreType.DMA,
            ],
        )

    for c in range(count):
        reduced(c)
        if direct and c + 2 < count:
            arrived.append(relay.chunk(c + 2))
        if c >= 1:
            finished(c - 1)
    hidden_grad, sums = state["raw"]

    if direct:
        swap = [(i, i ^ 1) for i in range(groups)]
        both = jnp.stack([sums, lax.ppermute(sums, "expert", swap)])
        returned = [both] + [
            lax.ppermute(both, "expert", [(i, i ^ (SIDES * d)) for i in range(groups)])
            for d in range(1, LINE)
        ]
    else:
        sums = sums.reshape(held, groups, capacity).transpose(1, 0, 2).reshape(groups, -1)
        hidden_grad = hidden_grad.reshape(held, groups, capacity, units).transpose(1, 0, 2, 3)
        returned = lax.all_to_all(sums, "expert", split_axis=0, concat_axis=0, tiled=True)
        returned = [returned.reshape(-1, 128)]
    prob_grad = call(
        functools.partial(prob_kernel, direct, capacity),
        sds((chosen, tokens), F32),
        flat,
        probs,
        *returned,
        keep=False,
    ).T
    finished(count - 1)
    weight_grad = state["grad"]
    return (hidden_grad.reshape(hidden.shape), prob_grad, weight_grad)


def solution(mesh):
    in_specs = (
        P(("dp", "expert"), None),
        P(("dp", "expert"), None),
        P(("dp", "expert"), None),
        P("dp", None, "expert", None, None),
        P("expert", None, None),
    )
    out_specs = (
        P("dp", None, "expert", None, None),
        P(("dp", "expert"), None),
        P("dp", "expert", None),
    )
    return jax.shard_map(body, mesh=mesh, in_specs=in_specs, out_specs=out_specs, check_vma=False)
```

```python
import functools

import jax
import jax.numpy as jnp
from jax import lax
from jax.experimental import pallas as pl
from jax.experimental.pallas import tpu as pltpu
from jax.sharding import PartitionSpec as P

F32, BF16, I32 = jnp.float32, jnp.bfloat16, jnp.int32
VMEM = pl.BlockSpec(memory_space=pltpu.VMEM)
ANY = pl.BlockSpec(memory_space=pl.ANY)
HBM = pl.BlockSpec(memory_space=pltpu.HBM)

LINE, SIDES = 4, 2
FAR, NEAR, PASSED = (3, 2, 1, 0), (1, 0, 3, 2), (2, 0, 3, 1)
FROM = (0, 1, 3, 2)
MASKS = tuple(SIDES * d + s for s in range(SIDES) for d in FROM)
INFO = 16


class Chain:
    def __init__(self):
        self.last = None

    def __call__(self, kernel, outs, *args, in_specs=None, keep=True, after=(), room=24, **kw):
        in_specs = list(in_specs or [VMEM] * len(args))
        count = len(args)
        body = kernel
        unread = [*after] if self.last is None else [self.last, *after]
        if unread:
            args, in_specs = (*args, *unread), in_specs + [ANY] * len(unread)

            def body(*refs):
                kernel(*refs[:count], *refs[count + len(unread) :])

        made = pl.pallas_call(
            body,
            out_shape=outs,
            in_specs=in_specs,
            compiler_params=pltpu.CompilerParams(vmem_limit_bytes=room * 1024 * 1024),
            cost_estimate=pl.CostEstimate(flops=1, bytes_accessed=1, transcendentals=0),
            **kw,
        )(*args)
        if keep:
            self.last = min(jax.tree.leaves(made), key=lambda x: x.size)
        return made


def gates_of(probs):
    total = jnp.sum(probs, axis=0, keepdims=True)
    gates = probs / total
    return total, gates, gates.astype(BF16).astype(F32)


def slots_of(ids, experts):
    chosen, tokens = ids.shape
    expert = lax.broadcasted_iota(I32, (experts, tokens), 0)
    named = [ids[k : k + 1] == expert for k in range(chosen)]
    hits = functools.reduce(jnp.add, [n.astype(F32) for n in named]).astype(BF16)
    row = lax.broadcasted_iota(I32, (tokens, tokens), 0)
    earlier = (row < lax.broadcasted_iota(I32, (tokens, tokens), 1)).astype(F32).astype(BF16)
    before = jnp.dot(hits, earlier, preferred_element_type=F32)
    return [jnp.sum(jnp.where(n, before, 0.0), axis=0, keepdims=True) for n in named]


def begin_kernel(experts, capacity, ids_ref, probs_ref, rows_ref, flat_ref, out_ref, *scratch):
    ids_got, probs_got, sems = scratch
    chosen, tokens = ids_got.shape
    width = out_ref.shape[1]
    copies = [
        pltpu.make_async_copy(ids_ref, ids_got, sems.at[0]),
        pltpu.make_async_copy(probs_ref, probs_got, sems.at[1]),
        pltpu.make_async_copy(rows_ref.at[:, :width], out_ref.at[:tokens], sems.at[2]),
    ]
    for copy in copies:
        copy.start()
    for copy in copies:
        copy.wait()
    ids = ids_got[...]
    _, _, word = gates_of(probs_got[...])
    slots = slots_of(ids, experts)
    for k in range(chosen):
        flat_ref[k : k + 1, :] = ids[k : k + 1] * capacity + slots[k].astype(I32)
    rest = jnp.zeros((INFO - 3 * chosen, tokens), F32)
    info = jnp.concatenate([ids.astype(F32), *slots, word, rest], axis=0).astype(BF16)
    out_ref[tokens:, :tokens] = info
    if width > tokens:
        out_ref[tokens:, tokens:] = jnp.zeros((INFO, width - tokens), BF16)


def places(held, capacity, chosen, ref, place_ref):
    tokens = place_ref.shape[1]
    rows = held * capacity
    me = lax.axis_index("expert")
    local = lax.broadcasted_iota(I32, (rows, tokens), 0)
    info = ref[tokens:, :tokens].astype(F32)
    flat = (info[:chosen] * capacity + info[chosen : 2 * chosen]).astype(I32)
    word = info[2 * chosen : 3 * chosen]
    for side in range(SIDES):
        slot = local + (me ^ side) * rows
        hits = [jnp.where(flat[k : k + 1] == slot, word[k : k + 1], 0.0) for k in range(chosen)]
        place_ref[side * rows : (side + 1) * rows, :] = functools.reduce(jnp.add, hits).astype(BF16)


def pick(held, capacity, block_refs, place_ref, out_refs):
    tokens = place_ref.shape[2]
    for j, ref in enumerate(block_refs):
        scaled = jnp.dot(place_ref[j], ref[:tokens, :], preferred_element_type=F32).astype(BF16)
        for side, out_ref in enumerate(out_refs):
            for e in range(held):
                at = (side * held + e) * capacity
                out_ref[e, j * capacity : (j + 1) * capacity, :] = scaled[at : at + capacity]


def hand_kernel(held, capacity, chosen, first, start, own_ref, near_ref, far_ref, *refs):
    blocks = (own_ref, near_ref, far_ref)
    if start:
        rows_ref, refs = refs[0], refs[1:]
        *refs, sem = refs
        next_ref, refs = refs[-1], refs[:-1]
        copy = pltpu.make_async_copy(
            rows_ref.at[:, start : start + next_ref.shape[1]], next_ref, sem
        )
        copy.start()
    if first:
        mine_ref, other_ref, pass_ref, place_ref = refs
    else:
        place_ref, mine_ref, other_ref, pass_ref = refs
    place = lax.axis_index("expert") // SIDES
    inner = jnp.logical_and(place > 0, place < LINE - 1)

    @pl.when(inner)
    def _():
        pass_ref[...] = far_ref[...]

    @pl.when(jnp.logical_not(inner))
    def _():
        pass_ref[...] = own_ref[...]

    if first:
        for j, ref in enumerate(blocks):
            places(held, capacity, chosen, ref, place_ref.at[j])
    pick(held, capacity, blocks, place_ref, (mine_ref, other_ref))
    if start:
        copy.wait()


def passed_kernel(held, capacity, chosen, first, block_ref, *refs):
    if first:
        mine_ref, other_ref, place_ref = refs
        places(held, capacity, chosen, block_ref, place_ref.at[0])
    else:
        place_ref, mine_ref, other_ref = refs
    pick(held, capacity, (block_ref,), place_ref, (mine_ref, other_ref))


def turn_kernel(dp, hidden_ref, *refs):
    out_ref = refs[-1]
    parts, held, _, units = hidden_ref.shape
    share, across = units // dp, dp // 2
    me = lax.axis_index("expert") if parts > 1 else 0
    masks = MASKS if parts > 1 else (0,)
    mine = lax.axis_index("dp")
    core, row = mine % 2, mine // 2
    for e in range(held):
        stacked = jnp.concatenate([hidden_ref[me ^ mask, e] for mask in masks], axis=0)
        turned = stacked.T
        for piece in range(dp):
            other = (piece % 2) ^ core
            step = (piece // 2 - row + across) % across
            out_ref[e, other, step] = turned[piece * share : (piece + 1) * share]


def stacked_rows(refs, e, at):
    rows = [ref[e, :, at] for ref in refs]
    return rows[0] if len(rows) == 1 else jnp.concatenate(rows, axis=0)


def term_kernel(start, turned_ref, *refs):
    part_refs, keep_ref, give_ref = refs[:-2], refs[-2], refs[-1]
    held, _, across, share, slots = turned_ref.shape
    at = slice(start, start + keep_ref.shape[3])
    for e in range(held):
        scaled = stacked_rows(part_refs, e, at)
        for other, ref in ((1, give_ref), (0, keep_ref)):
            left = turned_ref[e, other].reshape(across * share, slots)
            term = jnp.dot(left, scaled, preferred_element_type=F32).astype(BF16)
            for step in range(across):
                ref[step, e] = term[step * share : (step + 1) * share]


def pair_kernel(keep_ref, got_ref, *out_refs):
    for step, ref in enumerate(out_refs, 1):
        ref[...] = (keep_ref[step].astype(F32) + got_ref[step].astype(F32)).astype(BF16)


def last_kernel(others, start, keep_ref, got_ref, *refs):
    out_ref, mark_ref, total_ref, sem = refs[-4:]
    mark_ref[...] = jnp.zeros(mark_ref.shape, F32)
    for e in range(keep_ref.shape[1]):
        total = keep_ref[0, e].astype(F32) + got_ref[0, e].astype(F32)
        for ref in refs[:others]:
            total = total + ref[e].astype(F32)
        total_ref[:, e, :] = total
    copy = pltpu.make_async_copy(
        total_ref, out_ref.at[:, :, start : start + total_ref.shape[2]], sem
    )
    copy.start()
    copy.wait()


def raw_kernel(parts, start, width, at, final, weight_ref, *refs):
    part_refs, refs = refs[:parts], refs[parts:]
    if start:
        acc_ref, refs = refs[0], refs[1:]
    for e in range(weight_ref.shape[0]):
        raw = lax.dot_general(
            stacked_rows(part_refs, e, slice(at, at + width)),
            weight_ref[e, :, start : start + width],
            (((1,), (1,)), ((), ())),
            preferred_element_type=F32,
        )
        if start:
            raw = raw + acc_ref[e]
        if not final:
            refs[0][e] = raw
            continue
        hidden_ref, grad_ref, sums_ref = refs
        sources, _, own, units = hidden_ref.shape
        me = lax.axis_index("expert") if sources > 1 else 0
        folds = []
        for part, mask in enumerate(MASKS if sources > 1 else (0,)):
            block = raw[part * own : (part + 1) * own]
            grad_ref[me ^ mask, e] = block.astype(BF16)
            product = block * hidden_ref[me ^ mask, e].astype(F32)
            folds.append(
                functools.reduce(jnp.add, [product[:, i : i + 128] for i in range(0, units, 128)])
            )
        folded = jnp.concatenate(folds, axis=0) if len(folds) > 1 else folds[0]
        sums_ref[e : e + 1, :] = jnp.sum(folded.T, axis=0, keepdims=True)


def prob_kernel(direct, capacity, flat_ref, probs_ref, *refs):
    out_ref = refs[-1]
    chosen, tokens = flat_ref.shape
    if direct:
        values = []
        for mask in range(LINE * SIDES):
            at = MASKS.index(mask) * capacity
            ref = refs[mask // SIDES]
            values += [ref[mask % SIDES, e : e + 1, at : at + capacity] for e in range(ref.shape[1])]
        lanes = 128 // capacity
        values = jnp.concatenate(
            [
                jnp.concatenate([v.reshape(1, capacity) for v in values[i : i + lanes]], axis=1)
                for i in range(0, len(values), lanes)
            ],
            axis=0,
        )
        me = lax.axis_index("expert")
    else:
        values = refs[0][...]
        me = 0
    lines = values.shape[0]
    spare = jnp.zeros((-lines % 8, 128), F32)
    columns = jnp.concatenate([values, spare], axis=0).T if spare.size else values.T
    total, gates, word = gates_of(probs_ref[...])
    group = lines * 128 // (LINE * SIDES)
    picked = [jnp.zeros((1, tokens), F32) for _ in range(chosen)]
    for line in range(lines):
        at = lax.broadcasted_iota(I32, (128, tokens), 0) + line * 128
        slot = (at // group ^ me) * group + at % group
        for k in range(chosen):
            hit = jnp.where(flat_ref[k : k + 1, :] == slot, columns[:, line : line + 1], 0.0)
            picked[k] += jnp.sum(hit, axis=0, keepdims=True)
    picked = [picked[k] / word[k : k + 1] for k in range(chosen)]
    mixed = functools.reduce(jnp.add, [gates[k : k + 1] * picked[k] for k in range(chosen)])
    for k in range(chosen):
        out_ref[k : k + 1, :] = (picked[k] - mixed) / total


def chunks_of(features):
    unit = features // 16
    return [[6 * unit], [2 * unit, 4 * unit, 4 * unit]]


sds = jax.ShapeDtypeStruct


class Relay:
    def __init__(self, call, grad_out, ids, probs, held, capacity, widths):
        tokens = grad_out.shape[0]
        self.call, self.rows, self.held, self.capacity = call, grad_out, held, capacity
        self.chosen, self.widths = ids.shape[0], widths
        self.place, self.passed_place, self.blocks = None, None, None
        self.flat, first = call(
            functools.partial(begin_kernel, LINE * SIDES * held, capacity),
            [sds(ids.shape, I32), sds((tokens + INFO, widths[0]), BF16)],
            ids,
            probs,
            grad_out,
            in_specs=[HBM] * 3,
            scratch_shapes=[
                pltpu.VMEM(ids.shape, I32),
                pltpu.VMEM(probs.shape, F32),
                pltpu.SemaphoreType.DMA((3,)),
            ],
            room=60,
            keep=False,
        )
        self.leave(first)

    def leave(self, own):
        self.blocks = [own, self.along(own, NEAR), self.along(own, FAR)]

    def along(self, block, targets):
        pairs = [(p * SIDES + s, targets[p] * SIDES + s) for p in range(LINE) for s in range(SIDES)]
        return lax.ppermute(block, "expert", pairs)

    def swap(self, block):
        return lax.ppermute(block, "expert", [(i, i ^ 1) for i in range(LINE * SIDES)])

    def selected(self, blocks, width):
        return [sds((self.held, blocks * self.capacity, width), BF16)] * SIDES

    def hand(self, c):
        held, capacity, tokens = self.held, self.capacity, self.rows.shape[0]
        start = sum(self.widths[: c + 1]) if c + 1 < len(self.widths) else 0
        kernel = functools.partial(hand_kernel, held, capacity, self.chosen, c == 0, start)
        blocks = self.blocks
        args, outs = list(blocks), self.selected(LINE - 1, self.widths[c])
        outs.append(sds(blocks[0].shape, BF16))
        specs = [VMEM] * 3
        scratch = []
        if start:
            args.append(self.rows)
            specs.append(HBM)
            scratch.append(pltpu.SemaphoreType.DMA)
        if c == 0:
            outs.append(sds((LINE - 1, SIDES * held * capacity, tokens), BF16))
        else:
            args.append(self.place)
            specs.append(VMEM)
        if start:
            outs.append(sds((tokens, self.widths[c + 1]), BF16))
        made = self.call(kernel, outs, *args, in_specs=specs, scratch_shapes=scratch)
        mine, other, handed = made[:3]
        if c == 0:
            self.place = made[3]
        passed = self.along(handed, PASSED)
        if start:
            self.leave(made[-1])
        return passed, [mine, self.swap(other)]

    def arrive(self, c, passed, parts):
        held, capacity, tokens = self.held, self.capacity, self.rows.shape[0]
        kernel = functools.partial(passed_kernel, held, capacity, self.chosen, c == 0)
        rows = self.selected(1, self.widths[c])
        if c == 0:
            place = sds((1, SIDES * held * capacity, tokens), BF16)
            mine, other, self.passed_place = self.call(kernel, [*rows, place], passed)
        else:
            mine, other = self.call(kernel, rows, passed, self.passed_place)
        return [parts[0], mine, parts[1], self.swap(other)]


def exchanged(grad_out, ids, probs, groups, held, capacity, widths):
    tokens = grad_out.shape[0]
    experts = groups * held
    slots = experts * capacity
    _, _, word = gates_of(probs)
    flat = ids * capacity + jnp.concatenate(slots_of(ids, experts), axis=0).astype(I32)
    slot = lax.broadcasted_iota(I32, (slots, tokens), 0)
    place = sum(jnp.where(f == slot, w, 0.0) for f, w in zip(flat, word)).astype(BF16)
    arrived, start = [], 0
    for width in widths:
        rows = grad_out[:, start : start + width]
        sent = jnp.dot(place, rows, preferred_element_type=F32).astype(BF16)
        got = lax.all_to_all(
            sent.reshape(groups, held, capacity, width),
            "expert",
            split_axis=0,
            concat_axis=0,
            tiled=True,
        )
        arrived.append([got.transpose(1, 0, 2, 3).reshape(held, groups * capacity, width)])
        start += width
    return flat, arrived


def body(grad_out, route_ids, route_probs, hidden, w_down):
    groups = lax.axis_size("expert")
    dp = lax.axis_size("dp")
    held, units, features = w_down.shape
    capacity = hidden.shape[3]
    slots = groups * held * capacity
    per_expert = slots // held
    tokens, chosen = route_ids.shape
    share, across = units // dp, dp // 2
    direct = groups == LINE * SIDES
    chunks = chunks_of(features)
    widths = [sum(chunk) for chunk in chunks]

    ids, probs = route_ids.T, route_probs.T
    call = Chain()
    if direct:
        relay = Relay(call, grad_out, ids, probs, held, capacity, widths)
        flat, saved = relay.flat, hidden[0]
    else:
        flat, arrived = exchanged(grad_out, ids, probs, groups, held, capacity, widths)
        saved = hidden[0].transpose(1, 0, 2, 3).reshape(1, held, per_expert, units)
    turned = call(
        functools.partial(turn_kernel, dp),
        sds((held, 2, across, share, per_expert), BF16),
        saved,
        *([grad_out] if direct else []),
    )

    state = {"raw": None, "grad": None, "start": 0}
    summed, starts = [], []

    def reduced(parts, at, width):
        start = state["start"]
        starts.append(start)
        state["start"] = start + width
        piece = sds((across, held, share, width), BF16)
        keep, give = call(functools.partial(term_kernel, at), [piece, piece], turned, *parts)
        got = lax.ppermute(give, "dp", [(i, i ^ 1) for i in range(dp)])
        final = start + width == features
        if final:
            outs = [sds(saved.shape, BF16), sds((held, per_expert), F32)]
        else:
            outs = [sds((held, per_expert, units), F32)]
        extra = ([state["raw"]] if start else []) + ([saved] if final else [])
        kernel = functools.partial(raw_kernel, len(parts), start, width, at, final)
        made = call(kernel, outs, w_down, *parts, *extra)
        state["raw"] = made if final else made[0]
        pairs = call(pair_kernel, [sds((held, share, width), BF16)] * (across - 1), keep, got)
        others = []
        for step, pair in enumerate(pairs, 1):
            shift = [(2 * r + k, 2 * ((r + step) % across) + k) for r in range(across) for k in range(2)]
            others.append(lax.ppermute(pair, "dp", shift))
        summed.append((keep, got, others))

    def finished(j):
        keep, got, others = summed[j]
        before = [] if state["grad"] is None else [state["grad"]]
        count = 2 + len(others)
        state["grad"], _ = call(
            functools.partial(last_kernel, len(others), starts[j]),
            [sds((share, held, features), F32), sds((8, 128), F32)],
            keep,
            got,
            *others,
            *before,
            in_specs=[VMEM] * count + [ANY] * len(before),
            out_specs=[ANY, VMEM],
            input_output_aliases={count: 0} if before else {},
            scratch_shapes=[
                pltpu.VMEM((share, held, keep.shape[3]), F32),
                pltpu.SemaphoreType.DMA,
            ],
        )

    def rest(parts, chunk):
        at = 0
        for width in chunk:
            reduced(parts, at, width)
            at += width
            if 2 <= len(summed) < sum(map(len, chunks)):
                finished(len(summed) - 2)

    if direct:
        passed, parts = relay.hand(0)
        for c, chunk in enumerate(chunks):
            whole = relay.arrive(c, passed, parts)
            if c + 1 < len(chunks):
                passed, parts = relay.hand(c + 1)
            rest(whole, chunk)
    else:
        for c, chunk in enumerate(chunks):
            rest(arrived[c], chunk)
    hidden_grad, sums = state["raw"]
    finished(len(summed) - 2)

    if direct:
        swap = [(i, i ^ 1) for i in range(groups)]
        both = jnp.stack([sums, lax.ppermute(sums, "expert", swap)])
        returned = [both] + [
            lax.ppermute(both, "expert", [(i, i ^ (SIDES * d)) for i in range(groups)])
            for d in range(1, LINE)
        ]
    else:
        sums = sums.reshape(held, groups, capacity).transpose(1, 0, 2).reshape(groups, -1)
        hidden_grad = hidden_grad.reshape(held, groups, capacity, units).transpose(1, 0, 2, 3)
        returned = lax.all_to_all(sums, "expert", split_axis=0, concat_axis=0, tiled=True)
        returned = [returned.reshape(-1, 128)]
    prob_grad = call(
        functools.partial(prob_kernel, direct, capacity),
        sds((chosen, tokens), F32),
        flat,
        probs,
        *returned,
        keep=False,
    ).T
    finished(len(summed) - 1)
    weight_grad = state["grad"]
    return (hidden_grad.reshape(hidden.shape), prob_grad, weight_grad)


def solution(mesh):
    in_specs = (
        P(("dp", "expert"), None),
        P(("dp", "expert"), None),
        P(("dp", "expert"), None),
        P("dp", None, "expert", None, None),
        P("expert", None, None),
    )
    out_specs = (
        P("dp", None, "expert", None, None),
        P(("dp", "expert"), None),
        P("dp", "expert", None),
    )
    return jax.shard_map(body, mesh=mesh, in_specs=in_specs, out_specs=out_specs, check_vma=False)
```

```python
import functools

import jax
import jax.numpy as jnp
from jax import lax
from jax.experimental import pallas as pl
from jax.experimental.pallas import tpu as pltpu
from jax.sharding import PartitionSpec as P

F32, BF16, I32 = jnp.float32, jnp.bfloat16, jnp.int32
VMEM = pl.BlockSpec(memory_space=pltpu.VMEM)
ANY = pl.BlockSpec(memory_space=pl.ANY)
HBM = pl.BlockSpec(memory_space=pltpu.HBM)

GROUPS, INFO = 8, 16


class Chain:
    def __init__(self):
        self.last = None

    def __call__(self, kernel, outs, *args, in_specs=None, keep=True, after=(), room=24, **kw):
        in_specs = list(in_specs or [VMEM] * len(args))
        count = len(args)
        body = kernel
        unread = [*after] if self.last is None else [self.last, *after]
        if unread:
            args, in_specs = (*args, *unread), in_specs + [ANY] * len(unread)

            def body(*refs):
                kernel(*refs[:count], *refs[count + len(unread) :])

        made = pl.pallas_call(
            body,
            out_shape=outs,
            in_specs=in_specs,
            compiler_params=pltpu.CompilerParams(vmem_limit_bytes=room * 1024 * 1024),
            cost_estimate=pl.CostEstimate(flops=1, bytes_accessed=1, transcendentals=0),
            **kw,
        )(*args)
        if keep:
            self.last = min(jax.tree.leaves(made), key=lambda x: x.size)
        return made


def gates_of(probs):
    total = jnp.sum(probs, axis=0, keepdims=True)
    gates = probs / total
    return total, gates, gates.astype(BF16).astype(F32)


def slots_of(ids, experts):
    chosen, tokens = ids.shape
    expert = lax.broadcasted_iota(I32, (experts, tokens), 0)
    named = [ids[k : k + 1] == expert for k in range(chosen)]
    hits = functools.reduce(jnp.add, [n.astype(F32) for n in named]).astype(BF16)
    row = lax.broadcasted_iota(I32, (tokens, tokens), 0)
    earlier = (row < lax.broadcasted_iota(I32, (tokens, tokens), 1)).astype(F32).astype(BF16)
    before = jnp.dot(hits, earlier, preferred_element_type=F32)
    return [jnp.sum(jnp.where(n, before, 0.0), axis=0, keepdims=True) for n in named]


def begin_kernel(experts, capacity, ids_ref, probs_ref, rows_ref, flat_ref, *refs):
    out_refs, (ids_got, probs_got, sems) = refs[:-3], refs[-3:]
    chosen, tokens = ids_got.shape
    copies = [
        pltpu.make_async_copy(ids_ref, ids_got, sems.at[0]),
        pltpu.make_async_copy(probs_ref, probs_got, sems.at[1]),
    ]
    start = 0
    for i, ref in enumerate(out_refs):
        width = ref.shape[1]
        rows = rows_ref.at[:, start : start + width]
        copies.append(pltpu.make_async_copy(rows, ref.at[:tokens], sems.at[2 + i]))
        start += width
    for copy in copies:
        copy.start()
    for copy in copies:
        copy.wait()
    out_ref, width = out_refs[0], out_refs[0].shape[1]
    ids = ids_got[...]
    _, _, word = gates_of(probs_got[...])
    slots = slots_of(ids, experts)
    for k in range(chosen):
        flat_ref[k : k + 1, :] = ids[k : k + 1] * capacity + slots[k].astype(I32)
    rest = jnp.zeros((INFO - 3 * chosen, tokens), F32)
    info = jnp.concatenate([ids.astype(F32), *slots, word, rest], axis=0).astype(BF16)
    out_ref[tokens:, :tokens] = info
    if width > tokens:
        out_ref[tokens:, tokens:] = jnp.zeros((INFO, width - tokens), BF16)


def pick_kernel(held, capacity, chosen, first, blocks_ref, *refs):
    if first:
        out_ref, place_ref = refs
    else:
        place_ref, out_ref = refs
    sources, rows, tokens = place_ref.shape
    me = lax.axis_index("expert")
    for part in range(sources):
        if first:
            info = blocks_ref[me ^ part, tokens:, :tokens].astype(F32)
            flat = (info[:chosen] * capacity + info[chosen : 2 * chosen]).astype(I32)
            word = info[2 * chosen : 3 * chosen]
            slot = lax.broadcasted_iota(I32, (rows, tokens), 0) + me * rows
            hits = [jnp.where(flat[k : k + 1] == slot, word[k : k + 1], 0.0) for k in range(chosen)]
            place_ref[part] = functools.reduce(jnp.add, hits).astype(BF16)
        scaled = jnp.dot(
            place_ref[part], blocks_ref[me ^ part, :tokens], preferred_element_type=F32
        ).astype(BF16)
        for e in range(held):
            at = slice(part * capacity, (part + 1) * capacity)
            out_ref[e, at, :] = scaled[e * capacity : (e + 1) * capacity]


def turn_kernel(dp, hidden_ref, *refs):
    out_ref = refs[-1]
    parts, held, _, units = hidden_ref.shape
    share, across = units // dp, dp // 2
    me = lax.axis_index("expert") if parts > 1 else 0
    masks = range(parts)
    mine = lax.axis_index("dp")
    core, row = mine % 2, mine // 2
    for e in range(held):
        stacked = jnp.concatenate([hidden_ref[me ^ mask, e] for mask in masks], axis=0)
        turned = stacked.T
        for piece in range(dp):
            other = (piece % 2) ^ core
            step = (piece // 2 - row + across) % across
            out_ref[e, other, step] = turned[piece * share : (piece + 1) * share]


def stacked_rows(refs, e, at):
    rows = [ref[e, :, at] for ref in refs]
    return rows[0] if len(rows) == 1 else jnp.concatenate(rows, axis=0)


def term_kernel(start, turned_ref, *refs):
    part_refs, keep_ref, give_ref = refs[:-2], refs[-2], refs[-1]
    held, _, across, share, slots = turned_ref.shape
    at = slice(start, start + keep_ref.shape[3])
    for e in range(held):
        scaled = stacked_rows(part_refs, e, at)
        for other, ref in ((1, give_ref), (0, keep_ref)):
            left = turned_ref[e, other].reshape(across * share, slots)
            term = jnp.dot(left, scaled, preferred_element_type=F32).astype(BF16)
            for step in range(across):
                ref[step, e] = term[step * share : (step + 1) * share]


def pair_kernel(keep_ref, got_ref, *out_refs):
    for step, ref in enumerate(out_refs, 1):
        ref[...] = (keep_ref[step].astype(F32) + got_ref[step].astype(F32)).astype(BF16)


def last_kernel(others, start, keep_ref, got_ref, *refs):
    out_ref, mark_ref, total_ref, sem = refs[-4:]
    mark_ref[...] = jnp.zeros(mark_ref.shape, F32)
    for e in range(keep_ref.shape[1]):
        total = keep_ref[0, e].astype(F32) + got_ref[0, e].astype(F32)
        for ref in refs[:others]:
            total = total + ref[e].astype(F32)
        total_ref[:, e, :] = total
    copy = pltpu.make_async_copy(
        total_ref, out_ref.at[:, :, start : start + total_ref.shape[2]], sem
    )
    copy.start()
    copy.wait()


def raw_kernel(parts, start, width, at, final, weight_ref, *refs):
    part_refs, refs = refs[:parts], refs[parts:]
    if start:
        acc_ref, refs = refs[0], refs[1:]
    for e in range(weight_ref.shape[0]):
        raw = lax.dot_general(
            stacked_rows(part_refs, e, slice(at, at + width)),
            weight_ref[e, :, start : start + width],
            (((1,), (1,)), ((), ())),
            preferred_element_type=F32,
        )
        if start:
            raw = raw + acc_ref[e]
        if not final:
            refs[0][e] = raw
            continue
        hidden_ref, grad_ref, sums_ref = refs
        sources, _, own, units = hidden_ref.shape
        me = lax.axis_index("expert") if sources > 1 else 0
        folds = []
        for part, mask in enumerate(range(sources)):
            block = raw[part * own : (part + 1) * own]
            grad_ref[me ^ mask, e] = block.astype(BF16)
            product = block * hidden_ref[me ^ mask, e].astype(F32)
            folds.append(
                functools.reduce(jnp.add, [product[:, i : i + 128] for i in range(0, units, 128)])
            )
        folded = jnp.concatenate(folds, axis=0) if len(folds) > 1 else folds[0]
        sums_ref[e : e + 1, :] = jnp.sum(folded.T, axis=0, keepdims=True)


def prob_kernel(direct, capacity, flat_ref, probs_ref, *refs):
    out_ref = refs[-1]
    chosen, tokens = flat_ref.shape
    if direct:
        values = []
        for mask in range(GROUPS):
            at = mask * capacity
            ref = refs[mask // 2]
            values += [ref[mask % 2, e : e + 1, at : at + capacity] for e in range(ref.shape[1])]
        lanes = 128 // capacity
        values = jnp.concatenate(
            [
                jnp.concatenate([v.reshape(1, capacity) for v in values[i : i + lanes]], axis=1)
                for i in range(0, len(values), lanes)
            ],
            axis=0,
        )
        me = lax.axis_index("expert")
    else:
        values = refs[0][...]
        me = 0
    lines = values.shape[0]
    spare = jnp.zeros((-lines % 8, 128), F32)
    columns = jnp.concatenate([values, spare], axis=0).T if spare.size else values.T
    total, gates, word = gates_of(probs_ref[...])
    group = lines * 128 // GROUPS
    picked = [jnp.zeros((1, tokens), F32) for _ in range(chosen)]
    for line in range(lines):
        at = lax.broadcasted_iota(I32, (128, tokens), 0) + line * 128
        slot = (at // group ^ me) * group + at % group
        for k in range(chosen):
            hit = jnp.where(flat_ref[k : k + 1, :] == slot, columns[:, line : line + 1], 0.0)
            picked[k] += jnp.sum(hit, axis=0, keepdims=True)
    picked = [picked[k] / word[k : k + 1] for k in range(chosen)]
    mixed = functools.reduce(jnp.add, [gates[k : k + 1] * picked[k] for k in range(chosen)])
    for k in range(chosen):
        out_ref[k : k + 1, :] = (picked[k] - mixed) / total


def chunks_of(features):
    return [features // 4] * 4


sds = jax.ShapeDtypeStruct


def exchanged(grad_out, ids, probs, groups, held, capacity, widths):
    tokens = grad_out.shape[0]
    experts = groups * held
    slots = experts * capacity
    _, _, word = gates_of(probs)
    flat = ids * capacity + jnp.concatenate(slots_of(ids, experts), axis=0).astype(I32)
    slot = lax.broadcasted_iota(I32, (slots, tokens), 0)
    place = sum(jnp.where(f == slot, w, 0.0) for f, w in zip(flat, word)).astype(BF16)
    arrived, start = [], 0
    for width in widths:
        rows = grad_out[:, start : start + width]
        sent = jnp.dot(place, rows, preferred_element_type=F32).astype(BF16)
        got = lax.all_to_all(
            sent.reshape(groups, held, capacity, width),
            "expert",
            split_axis=0,
            concat_axis=0,
            tiled=True,
        )
        arrived.append([got.transpose(1, 0, 2, 3).reshape(held, groups * capacity, width)])
        start += width
    return flat, arrived


def body(grad_out, route_ids, route_probs, hidden, w_down):
    groups = lax.axis_size("expert")
    dp = lax.axis_size("dp")
    held, units, features = w_down.shape
    capacity = hidden.shape[3]
    slots = groups * held * capacity
    per_expert = slots // held
    tokens, chosen = route_ids.shape
    share, across = units // dp, dp // 2
    direct = groups == GROUPS
    widths = chunks_of(features)

    ids, probs = route_ids.T, route_probs.T
    call = Chain()
    if direct:
        flat, *blocks = call(
            functools.partial(begin_kernel, groups * held, capacity),
            [sds(ids.shape, I32)]
            + [sds((tokens + (0 if c else INFO), w), BF16) for c, w in enumerate(widths)],
            ids,
            probs,
            grad_out,
            in_specs=[HBM] * 3,
            scratch_shapes=[
                pltpu.VMEM(ids.shape, I32),
                pltpu.VMEM(probs.shape, F32),
                pltpu.SemaphoreType.DMA((2 + len(widths),)),
            ],
            room=60,
            keep=False,
        )
        gathered = [lax.all_gather(block, "expert") for block in blocks]
        saved = hidden[0]
    else:
        flat, arrived = exchanged(grad_out, ids, probs, groups, held, capacity, widths)
        saved = hidden[0].transpose(1, 0, 2, 3).reshape(1, held, per_expert, units)
    turned = call(
        functools.partial(turn_kernel, dp),
        sds((held, 2, across, share, per_expert), BF16),
        saved,
    )

    state = {"raw": None, "grad": None, "start": 0}
    summed, starts = [], []

    def reduced(parts, at, width):
        start = state["start"]
        starts.append(start)
        state["start"] = start + width
        piece = sds((across, held, share, width), BF16)
        keep, give = call(functools.partial(term_kernel, at), [piece, piece], turned, *parts)
        got = lax.ppermute(give, "dp", [(i, i ^ 1) for i in range(dp)])
        final = start + width == features
        if final:
            outs = [sds(saved.shape, BF16), sds((held, per_expert), F32)]
        else:
            outs = [sds((held, per_expert, units), F32)]
        extra = ([state["raw"]] if start else []) + ([saved] if final else [])
        kernel = functools.partial(raw_kernel, len(parts), start, width, at, final)
        made = call(kernel, outs, w_down, *parts, *extra)
        state["raw"] = made if final else made[0]
        pairs = call(pair_kernel, [sds((held, share, width), BF16)] * (across - 1), keep, got)
        others = []
        for step, pair in enumerate(pairs, 1):
            shift = [(2 * r + k, 2 * ((r + step) % across) + k) for r in range(across) for k in range(2)]
            others.append(lax.ppermute(pair, "dp", shift))
        summed.append((keep, got, others))

    def finished(j):
        keep, got, others = summed[j]
        before = [] if state["grad"] is None else [state["grad"]]
        count = 2 + len(others)
        state["grad"], _ = call(
            functools.partial(last_kernel, len(others), starts[j]),
            [sds((share, held, features), F32), sds((8, 128), F32)],
            keep,
            got,
            *others,
            *before,
            in_specs=[VMEM] * count + [ANY] * len(before),
            out_specs=[ANY, VMEM],
            input_output_aliases={count: 0} if before else {},
            scratch_shapes=[
                pltpu.VMEM((share, held, keep.shape[3]), F32),
                pltpu.SemaphoreType.DMA,
            ],
        )

    place = None
    for c, width in enumerate(widths):
        if direct:
            kernel = functools.partial(pick_kernel, held, capacity, chosen, c == 0)
            rows = sds((held, per_expert, width), BF16)
            if c == 0:
                rows, place = call(
                    kernel, [rows, sds((groups, held * capacity, tokens), BF16)], gathered[c]
                )
            else:
                rows = call(kernel, rows, gathered[c], place)
            reduced([rows], 0, width)
        else:
            reduced(arrived[c], 0, width)
        if c >= 2:
            finished(c - 2)
    hidden_grad, sums = state["raw"]
    finished(len(summed) - 2)

    if direct:
        swap = [(i, i ^ 1) for i in range(groups)]
        both = jnp.stack([sums, lax.ppermute(sums, "expert", swap)])
        returned = [both] + [
            lax.ppermute(both, "expert", [(i, i ^ d) for i in range(groups)])
            for d in range(2, groups, 2)
        ]
    else:
        sums = sums.reshape(held, groups, capacity).transpose(1, 0, 2).reshape(groups, -1)
        hidden_grad = hidden_grad.reshape(held, groups, capacity, units).transpose(1, 0, 2, 3)
        returned = lax.all_to_all(sums, "expert", split_axis=0, concat_axis=0, tiled=True)
        returned = [returned.reshape(-1, 128)]
    prob_grad = call(
        functools.partial(prob_kernel, direct, capacity),
        sds((chosen, tokens), F32),
        flat,
        probs,
        *returned,
        keep=False,
    ).T
    finished(len(summed) - 1)
    weight_grad = state["grad"]
    return (hidden_grad.reshape(hidden.shape), prob_grad, weight_grad)


def solution(mesh):
    in_specs = (
        P(("dp", "expert"), None),
        P(("dp", "expert"), None),
        P(("dp", "expert"), None),
        P("dp", None, "expert", None, None),
        P("expert", None, None),
    )
    out_specs = (
        P("dp", None, "expert", None, None),
        P(("dp", "expert"), None),
        P("dp", "expert", None),
    )
    return jax.shard_map(body, mesh=mesh, in_specs=in_specs, out_specs=out_specs, check_vma=False)
```

```python
import functools

import jax
import jax.numpy as jnp
from jax import lax
from jax.experimental import pallas as pl
from jax.experimental.pallas import tpu as pltpu
from jax.sharding import PartitionSpec as P

F32, BF16, I32 = jnp.float32, jnp.bfloat16, jnp.int32
VMEM = pl.BlockSpec(memory_space=pltpu.VMEM)
ANY = pl.BlockSpec(memory_space=pl.ANY)
HBM = pl.BlockSpec(memory_space=pltpu.HBM)

LINE, SIDES = 4, 2
INFO = 16


class Chain:
    def __init__(self):
        self.last = None

    def __call__(self, kernel, outs, *args, in_specs=None, keep=True, after=(), room=24, **kw):
        in_specs = list(in_specs or [VMEM] * len(args))
        count = len(args)
        body = kernel
        unread = [*after] if self.last is None else [self.last, *after]
        if unread:
            args, in_specs = (*args, *unread), in_specs + [ANY] * len(unread)

            def body(*refs):
                kernel(*refs[:count], *refs[count + len(unread) :])

        made = pl.pallas_call(
            body,
            out_shape=outs,
            in_specs=in_specs,
            compiler_params=pltpu.CompilerParams(vmem_limit_bytes=room * 1024 * 1024),
            cost_estimate=pl.CostEstimate(flops=1, bytes_accessed=1, transcendentals=0),
            **kw,
        )(*args)
        if keep:
            self.last = min(jax.tree.leaves(made), key=lambda x: x.size)
        return made


def gates_of(probs):
    total = jnp.sum(probs, axis=0, keepdims=True)
    gates = probs / total
    return total, gates, gates.astype(BF16).astype(F32)


def slots_of(ids, experts):
    chosen, tokens = ids.shape
    expert = lax.broadcasted_iota(I32, (experts, tokens), 0)
    named = [ids[k : k + 1] == expert for k in range(chosen)]
    hits = functools.reduce(jnp.add, [n.astype(F32) for n in named]).astype(BF16)
    row = lax.broadcasted_iota(I32, (tokens, tokens), 0)
    earlier = (row < lax.broadcasted_iota(I32, (tokens, tokens), 1)).astype(F32).astype(BF16)
    before = jnp.dot(hits, earlier, preferred_element_type=F32)
    return [jnp.sum(jnp.where(n, before, 0.0), axis=0, keepdims=True) for n in named]


def begin_kernel(experts, capacity, ids_ref, probs_ref, rows_ref, flat_ref, out_ref, *scratch):
    ids_got, probs_got, sems = scratch
    chosen, tokens = ids_got.shape
    width = out_ref.shape[1]
    copies = [
        pltpu.make_async_copy(ids_ref, ids_got, sems.at[0]),
        pltpu.make_async_copy(probs_ref, probs_got, sems.at[1]),
        pltpu.make_async_copy(rows_ref.at[:, :width], out_ref.at[:tokens], sems.at[2]),
    ]
    for copy in copies:
        copy.start()
    for copy in copies:
        copy.wait()
    ids = ids_got[...]
    _, _, word = gates_of(probs_got[...])
    slots = slots_of(ids, experts)
    for k in range(chosen):
        flat_ref[k : k + 1, :] = ids[k : k + 1] * capacity + slots[k].astype(I32)
    rest = jnp.zeros((INFO - 3 * chosen, tokens), F32)
    info = jnp.concatenate([ids.astype(F32), *slots, word, rest], axis=0).astype(BF16)
    out_ref[tokens:, :tokens] = info
    if width > tokens:
        out_ref[tokens:, tokens:] = jnp.zeros((INFO, width - tokens), BF16)


def pick_kernel(held, capacity, chosen, start, own_ref, other_ref, *refs):
    tokens = own_ref.shape[0] - (INFO if start is None else 0)
    rows = held * capacity
    if start is None:
        rows_ref, *out_refs, place_ref, rest_ref, sem = refs
        copy = pltpu.make_async_copy(rows_ref.at[:, own_ref.shape[1] :], rest_ref, sem)
        copy.start()
        me = lax.axis_index("expert")
        local = lax.broadcasted_iota(I32, (rows, tokens), 0)
        for side, ref in enumerate((own_ref, other_ref)):
            info = ref[tokens:, :tokens].astype(F32)
            flat = (info[:chosen] * capacity + info[chosen : 2 * chosen]).astype(I32)
            word = info[2 * chosen : 3 * chosen]
            for d in range(LINE):
                slot = local + (me ^ (SIDES * d)) * rows
                hits = [
                    jnp.where(flat[k : k + 1] == slot, word[k : k + 1], 0.0) for k in range(chosen)
                ]
                place_ref[side, d * rows : (d + 1) * rows, :] = functools.reduce(
                    jnp.add, hits
                ).astype(BF16)
        blocks = own_ref[:tokens, :], other_ref[:tokens, :]
    else:
        place_ref, out_refs = refs[0], refs[1:]
        width, first = out_refs[0].shape[2], own_ref.shape[1] - other_ref.shape[1]
        blocks = (
            own_ref[:, start : start + width],
            other_ref[:, start - first : start - first + width],
        )
    for side, block in enumerate(blocks):
        scaled = jnp.dot(place_ref[side], block, preferred_element_type=F32).astype(BF16)
        for d, out_ref in enumerate(out_refs):
            for e in range(held):
                at = d * rows + e * capacity
                out_ref[e, side * capacity : (side + 1) * capacity, :] = scaled[at : at + capacity]
    if start is None:
        copy.wait()


def turn_kernel(dp, hidden_ref, *refs):
    out_ref = refs[-1]
    parts, held, _, units = hidden_ref.shape
    share, across = units // dp, dp // 2
    me = lax.axis_index("expert") if parts > 1 else 0
    mine = lax.axis_index("dp")
    core, row = mine % 2, mine // 2
    for e in range(held):
        stacked = jnp.concatenate([hidden_ref[me ^ mask, e] for mask in range(parts)], axis=0)
        turned = stacked.T
        for piece in range(dp):
            other = (piece % 2) ^ core
            step = (piece // 2 - row + across) % across
            out_ref[e, other, step] = turned[piece * share : (piece + 1) * share]


def stacked_rows(refs, e):
    return refs[0][e] if len(refs) == 1 else jnp.concatenate([ref[e] for ref in refs], axis=0)


def term_kernel(turned_ref, *refs):
    part_refs, keep_ref, give_ref = refs[:-2], refs[-2], refs[-1]
    held, _, across, share, slots = turned_ref.shape
    for e in range(held):
        scaled = stacked_rows(part_refs, e)
        for other, ref in ((1, give_ref), (0, keep_ref)):
            left = turned_ref[e, other].reshape(across * share, slots)
            term = jnp.dot(left, scaled, preferred_element_type=F32).astype(BF16)
            for step in range(across):
                ref[step, e] = term[step * share : (step + 1) * share]


def pair_kernel(cuts, keep_ref, got_ref, *out_refs):
    out_refs = iter(out_refs)
    for step in range(1, keep_ref.shape[0]):
        start = 0
        for rows in cuts:
            at = slice(start, start + rows)
            pair = keep_ref[step, :, at].astype(F32) + got_ref[step, :, at].astype(F32)
            next(out_refs)[...] = pair.astype(BF16)
            start += rows


def last_kernel(cuts, start, keep_ref, got_ref, *refs):
    out_ref, mark_ref, total_ref, sem = refs[-4:]
    mark_ref[...] = jnp.zeros(mark_ref.shape, F32)
    others = len(cuts) * (keep_ref.shape[0] - 1)
    for e in range(keep_ref.shape[1]):
        row = 0
        for part, rows in enumerate(cuts):
            at = slice(row, row + rows)
            total = keep_ref[0, e, at].astype(F32) + got_ref[0, e, at].astype(F32)
            for ref in refs[part : others : len(cuts)]:
                total = total + ref[e].astype(F32)
            total_ref[at, e, :] = total
            row += rows
    copy = pltpu.make_async_copy(
        total_ref, out_ref.at[:, :, start : start + total_ref.shape[2]], sem
    )
    copy.start()
    copy.wait()


def raw_kernel(parts, start, final, weight_ref, *refs):
    part_refs, refs = refs[:parts], refs[parts:]
    if start:
        acc_ref, refs = refs[0], refs[1:]
    width = part_refs[0].shape[2]
    for e in range(weight_ref.shape[0]):
        raw = lax.dot_general(
            stacked_rows(part_refs, e),
            weight_ref[e, :, start : start + width],
            (((1,), (1,)), ((), ())),
            preferred_element_type=F32,
        )
        if start:
            raw = raw + acc_ref[e]
        if not final:
            refs[0][e] = raw
            continue
        hidden_ref, grad_ref, sums_ref = refs
        sources, _, own, units = hidden_ref.shape
        me = lax.axis_index("expert") if sources > 1 else 0
        folds = []
        for mask in range(sources):
            block = raw[mask * own : (mask + 1) * own]
            grad_ref[me ^ mask, e] = block.astype(BF16)
            product = block * hidden_ref[me ^ mask, e].astype(F32)
            folds.append(
                functools.reduce(jnp.add, [product[:, i : i + 128] for i in range(0, units, 128)])
            )
        folded = jnp.concatenate(folds, axis=0) if len(folds) > 1 else folds[0]
        sums_ref[e : e + 1, :] = jnp.sum(folded.T, axis=0, keepdims=True)


def prob_kernel(direct, capacity, flat_ref, probs_ref, *refs):
    out_ref = refs[-1]
    chosen, tokens = flat_ref.shape
    if direct:
        values = []
        for mask in range(LINE * SIDES):
            at = mask * capacity
            ref = refs[mask // SIDES]
            values += [ref[mask % SIDES, e : e + 1, at : at + capacity] for e in range(ref.shape[1])]
        lanes = 128 // capacity
        values = jnp.concatenate(
            [
                jnp.concatenate([v.reshape(1, capacity) for v in values[i : i + lanes]], axis=1)
                for i in range(0, len(values), lanes)
            ],
            axis=0,
        )
        me = lax.axis_index("expert")
    else:
        values = refs[0][...]
        me = 0
    lines = values.shape[0]
    spare = jnp.zeros((-lines % 8, 128), F32)
    columns = jnp.concatenate([values, spare], axis=0).T if spare.size else values.T
    total, gates, word = gates_of(probs_ref[...])
    group = lines * 128 // (LINE * SIDES)
    picked = [jnp.zeros((1, tokens), F32) for _ in range(chosen)]
    for line in range(lines):
        at = lax.broadcasted_iota(I32, (128, tokens), 0) + line * 128
        slot = (at // group ^ me) * group + at % group
        for k in range(chosen):
            hit = jnp.where(flat_ref[k : k + 1, :] == slot, columns[:, line : line + 1], 0.0)
            picked[k] += jnp.sum(hit, axis=0, keepdims=True)
    picked = [picked[k] / word[k : k + 1] for k in range(chosen)]
    mixed = functools.reduce(jnp.add, [gates[k : k + 1] * picked[k] for k in range(chosen)])
    for k in range(chosen):
        out_ref[k : k + 1, :] = (picked[k] - mixed) / total


def chunks_of(features):
    unit = features // 16
    return [6 * unit, 8 * unit, 2 * unit]


def cuts_of(share, c):
    return [share // 3] * 3 if c == 0 else [share]


sds = jax.ShapeDtypeStruct


class Relay:
    def __init__(self, call, grad_out, ids, probs, held, capacity, widths):
        tokens, features = grad_out.shape
        self.call, self.rows, self.held, self.capacity = call, grad_out, held, capacity
        self.chosen, self.widths, self.place = ids.shape[0], widths, None
        self.flat, self.first = call(
            functools.partial(begin_kernel, LINE * SIDES * held, capacity),
            [sds(ids.shape, I32), sds((tokens + INFO, widths[0]), BF16)],
            ids,
            probs,
            grad_out,
            in_specs=[HBM] * 3,
            scratch_shapes=[
                pltpu.VMEM(ids.shape, I32),
                pltpu.VMEM(probs.shape, F32),
                pltpu.SemaphoreType.DMA((3,)),
            ],
            room=60,
            keep=False,
        )
        self.first_other = self.send(self.first, 1)

    def send(self, block, mask):
        return lax.ppermute(block, "expert", [(i, i ^ mask) for i in range(LINE * SIDES)])

    def chunk(self, c):
        held, capacity, tokens = self.held, self.capacity, self.rows.shape[0]
        rows = [sds((held, SIDES * capacity, self.widths[c]), BF16)] * LINE
        place = sds((SIDES, LINE * held * capacity, tokens), BF16)
        start = sum(self.widths[:c]) if c else None
        kernel = functools.partial(pick_kernel, held, capacity, self.chosen, start)
        if c == 0:
            rest = sds((tokens, self.rows.shape[1] - self.widths[0]), BF16)
            *sent, self.place, rest = self.call(
                kernel,
                [*rows, place, rest],
                self.first,
                self.first_other,
                self.rows,
                in_specs=[VMEM, VMEM, HBM],
                scratch_shapes=[pltpu.SemaphoreType.DMA],
            )
        else:
            sent = self.call(kernel, rows, self.rows, self.rest_other, self.place)
        got = [sent[0]] + [None] * (LINE - 1)
        for d in range(LINE - 1, 0, -1):
            got[d] = self.send(sent[d], SIDES * d)
        if c == 0:
            self.rest_other = self.send(rest, 1)
        return got


def exchanged(grad_out, ids, probs, groups, held, capacity, widths):
    tokens = grad_out.shape[0]
    experts = groups * held
    slots = experts * capacity
    _, _, word = gates_of(probs)
    flat = ids * capacity + jnp.concatenate(slots_of(ids, experts), axis=0).astype(I32)
    slot = lax.broadcasted_iota(I32, (slots, tokens), 0)
    place = sum(jnp.where(f == slot, w, 0.0) for f, w in zip(flat, word)).astype(BF16)
    arrived, start = [], 0
    for width in widths:
        rows = grad_out[:, start : start + width]
        sent = jnp.dot(place, rows, preferred_element_type=F32).astype(BF16)
        got = lax.all_to_all(
            sent.reshape(groups, held, capacity, width),
            "expert",
            split_axis=0,
            concat_axis=0,
            tiled=True,
        )
        arrived.append([got.transpose(1, 0, 2, 3).reshape(held, groups * capacity, width)])
        start += width
    return flat, arrived


def body(grad_out, route_ids, route_probs, hidden, w_down):
    groups = lax.axis_size("expert")
    dp = lax.axis_size("dp")
    held, units, features = w_down.shape
    capacity = hidden.shape[3]
    slots = groups * held * capacity
    per_expert = slots // held
    tokens, chosen = route_ids.shape
    share, across = units // dp, dp // 2
    direct = groups == LINE * SIDES
    widths = chunks_of(features)
    count = len(widths)

    ids, probs = route_ids.T, route_probs.T
    call = Chain()
    if direct:
        relay = Relay(call, grad_out, ids, probs, held, capacity, widths)
        flat, saved = relay.flat, hidden[0]
    else:
        flat, arrived = exchanged(grad_out, ids, probs, groups, held, capacity, widths)
        saved = hidden[0].transpose(1, 0, 2, 3).reshape(1, held, per_expert, units)
    turned = call(
        functools.partial(turn_kernel, dp),
        sds((held, 2, across, share, per_expert), BF16),
        saved,
        *([grad_out] if direct else []),
    )
    if direct:
        arrived = [relay.chunk(c) for c in range(min(2, count))]

    starts = [sum(widths[:c]) for c in range(count)]
    state = {"raw": None, "grad": None}
    summed = []

    def reduced(c):
        parts, width = arrived[c], widths[c]
        piece = sds((across, held, share, width), BF16)
        after = summed[0][2][:2] if c == 1 else ()
        keep, give = call(term_kernel, [piece, piece], turned, *parts, after=after)
        got = lax.ppermute(give, "dp", [(i, i ^ 1) for i in range(dp)])
        final = c == count - 1
        if final:
            outs = [sds(saved.shape, BF16), sds((held, per_expert), F32)]
        else:
            outs = [sds((held, per_expert, units), F32)]
        extra = ([state["raw"]] if c else []) + ([saved] if final else [])
        kernel = functools.partial(raw_kernel, len(parts), starts[c], final)
        made = call(
            kernel,
            outs,
            w_down,
            *parts,
            *extra,
        )
        state["raw"] = made if final else made[0]
        cuts = cuts_of(share, c)
        pieces = [sds((held, rows, width), BF16) for rows in cuts]
        pairs = call(functools.partial(pair_kernel, cuts), pieces * (across - 1), keep, got)
        others = []
        for i, pair in enumerate(pairs):
            step = 1 + i // len(cuts)
            shift = [(2 * r + k, 2 * ((r + step) % across) + k) for r in range(across) for k in range(2)]
            others.append(lax.ppermute(pair, "dp", shift))
        summed.append((keep, got, others))

    def finished(c):
        keep, got, others = summed[c]
        before = [] if state["grad"] is None else [state["grad"]]
        count = 2 + len(others)
        state["grad"], _ = call(
            functools.partial(last_kernel, cuts_of(share, c), starts[c]),
            [sds((share, held, features), F32), sds((8, 128), F32)],
            keep,
            got,
            *others,
            *before,
            in_specs=[VMEM] * count + [ANY] * len(before),
            out_specs=[ANY, VMEM],
            input_output_aliases={count: 0} if before else {},
            scratch_shapes=[
                pltpu.VMEM((share, held, widths[c]), F32),
                pltpu.SemaphoreType.DMA,
            ],
        )

    for c in range(count):
        reduced(c)
        if direct and c + 2 < count:
            arrived.append(relay.chunk(c + 2))
        if c >= 1:
            finished(c - 1)
    hidden_grad, sums = state["raw"]

    if direct:
        swap = [(i, i ^ 1) for i in range(groups)]
        both = jnp.stack([sums, lax.ppermute(sums, "expert", swap)])
        returned = [both] + [
            lax.ppermute(both, "expert", [(i, i ^ (SIDES * d)) for i in range(groups)])
            for d in range(1, LINE)
        ]
    else:
        sums = sums.reshape(held, groups, capacity).transpose(1, 0, 2).reshape(groups, -1)
        hidden_grad = hidden_grad.reshape(held, groups, capacity, units).transpose(1, 0, 2, 3)
        returned = lax.all_to_all(sums, "expert", split_axis=0, concat_axis=0, tiled=True)
        returned = [returned.reshape(-1, 128)]
    prob_grad = call(
        functools.partial(prob_kernel, direct, capacity),
        sds((chosen, tokens), F32),
        flat,
        probs,
        *returned,
        keep=False,
    ).T
    finished(count - 1)
    weight_grad = state["grad"]
    return (hidden_grad.reshape(hidden.shape), prob_grad, weight_grad)


def solution(mesh):
    in_specs = (
        P(("dp", "expert"), None),
        P(("dp", "expert"), None),
        P(("dp", "expert"), None),
        P("dp", None, "expert", None, None),
        P("expert", None, None),
    )
    out_specs = (
        P("dp", None, "expert", None, None),
        P(("dp", "expert"), None),
        P("dp", "expert", None),
    )
    return jax.shard_map(body, mesh=mesh, in_specs=in_specs, out_specs=out_specs, check_vma=False)
```

```python
import functools

import jax
import jax.numpy as jnp
from jax import lax
from jax.experimental import pallas as pl
from jax.experimental.pallas import tpu as pltpu
from jax.sharding import PartitionSpec as P

F32, BF16, I32 = jnp.float32, jnp.bfloat16, jnp.int32
VMEM = pl.BlockSpec(memory_space=pltpu.VMEM)
ANY = pl.BlockSpec(memory_space=pl.ANY)
HBM = pl.BlockSpec(memory_space=pltpu.HBM)

LINE, SIDES = 4, 2
INFO = 16


def target_of(me, part):
    return (me // SIDES + part // SIDES) % LINE * SIDES + (me % SIDES ^ part % SIDES)


def source_of(me, part):
    return (me // SIDES + LINE - part // SIDES) % LINE * SIDES + (me % SIDES ^ part % SIDES)


class Chain:
    def __init__(self):
        self.last = None

    def __call__(self, kernel, outs, *args, in_specs=None, keep=True, after=(), room=24, **kw):
        in_specs = list(in_specs or [VMEM] * len(args))
        count = len(args)
        body = kernel
        unread = [*after] if self.last is None else [self.last, *after]
        if unread:
            args, in_specs = (*args, *unread), in_specs + [ANY] * len(unread)

            def body(*refs):
                kernel(*refs[:count], *refs[count + len(unread) :])

        made = pl.pallas_call(
            body,
            out_shape=outs,
            in_specs=in_specs,
            compiler_params=pltpu.CompilerParams(vmem_limit_bytes=room * 1024 * 1024),
            cost_estimate=pl.CostEstimate(flops=1, bytes_accessed=1, transcendentals=0),
            **kw,
        )(*args)
        if keep:
            self.last = min(jax.tree.leaves(made), key=lambda x: x.size)
        return made


def gates_of(probs):
    total = jnp.sum(probs, axis=0, keepdims=True)
    gates = probs / total
    return total, gates, gates.astype(BF16).astype(F32)


def slots_of(ids, experts):
    chosen, tokens = ids.shape
    expert = lax.broadcasted_iota(I32, (experts, tokens), 0)
    named = [ids[k : k + 1] == expert for k in range(chosen)]
    hits = functools.reduce(jnp.add, [n.astype(F32) for n in named]).astype(BF16)
    row = lax.broadcasted_iota(I32, (tokens, tokens), 0)
    earlier = (row < lax.broadcasted_iota(I32, (tokens, tokens), 1)).astype(F32).astype(BF16)
    before = jnp.dot(hits, earlier, preferred_element_type=F32)
    return [jnp.sum(jnp.where(n, before, 0.0), axis=0, keepdims=True) for n in named]


def begin_kernel(experts, capacity, ids_ref, probs_ref, rows_ref, flat_ref, out_ref, *scratch):
    ids_got, probs_got, sems = scratch
    chosen, tokens = ids_got.shape
    width = out_ref.shape[1]
    copies = [
        pltpu.make_async_copy(ids_ref, ids_got, sems.at[0]),
        pltpu.make_async_copy(probs_ref, probs_got, sems.at[1]),
        pltpu.make_async_copy(rows_ref.at[:, :width], out_ref.at[:tokens], sems.at[2]),
    ]
    for copy in copies:
        copy.start()
    for copy in copies:
        copy.wait()
    ids = ids_got[...]
    _, _, word = gates_of(probs_got[...])
    slots = slots_of(ids, experts)
    for k in range(chosen):
        flat_ref[k : k + 1, :] = ids[k : k + 1] * capacity + slots[k].astype(I32)
    rest = jnp.zeros((INFO - 3 * chosen, tokens), F32)
    info = jnp.concatenate([ids.astype(F32), *slots, word, rest], axis=0).astype(BF16)
    out_ref[tokens:, :tokens] = info
    if width > tokens:
        out_ref[tokens:, tokens:] = jnp.zeros((INFO, width - tokens), BF16)


def pick_kernel(held, capacity, chosen, start, own_ref, other_ref, *refs):
    tokens = own_ref.shape[0] - (INFO if start is None else 0)
    rows = held * capacity
    if start is None:
        rows_ref, *out_refs, place_ref, rest_ref, sem = refs
        copy = pltpu.make_async_copy(rows_ref.at[:, own_ref.shape[1] :], rest_ref, sem)
        copy.start()
        me = lax.axis_index("expert")
        local = lax.broadcasted_iota(I32, (rows, tokens), 0)
        for side, ref in enumerate((own_ref, other_ref)):
            info = ref[tokens:, :tokens].astype(F32)
            flat = (info[:chosen] * capacity + info[chosen : 2 * chosen]).astype(I32)
            word = info[2 * chosen : 3 * chosen]
            for d in range(LINE):
                slot = local + target_of(me, SIDES * d) * rows
                hits = [
                    jnp.where(flat[k : k + 1] == slot, word[k : k + 1], 0.0) for k in range(chosen)
                ]
                place_ref[side, d * rows : (d + 1) * rows, :] = functools.reduce(
                    jnp.add, hits
                ).astype(BF16)
        blocks = own_ref[:tokens, :], other_ref[:tokens, :]
    else:
        place_ref, out_refs = refs[0], refs[1:]
        width, first = out_refs[0].shape[2], own_ref.shape[1] - other_ref.shape[1]
        blocks = (
            own_ref[:, start : start + width],
            other_ref[:, start - first : start - first + width],
        )
    for side, block in enumerate(blocks):
        scaled = jnp.dot(place_ref[side], block, preferred_element_type=F32).astype(BF16)
        for d, out_ref in enumerate(out_refs):
            for e in range(held):
                at = d * rows + e * capacity
                out_ref[e, side * capacity : (side + 1) * capacity, :] = scaled[at : at + capacity]
    if start is None:
        copy.wait()


def turn_kernel(dp, hidden_ref, *refs):
    out_ref = refs[-1]
    parts, held, _, units = hidden_ref.shape
    share, across = units // dp, dp // 2
    me = lax.axis_index("expert") if parts > 1 else 0
    mine = lax.axis_index("dp")
    core, row = mine % 2, mine // 2
    for e in range(held):
        sources = [source_of(me, p) if parts > 1 else 0 for p in range(parts)]
        stacked = jnp.concatenate([hidden_ref[source, e] for source in sources], axis=0)
        turned = stacked.T
        for piece in range(dp):
            other = (piece % 2) ^ core
            step = (piece // 2 - row + across) % across
            out_ref[e, other, step] = turned[piece * share : (piece + 1) * share]


def stacked_rows(refs, e):
    return refs[0][e] if len(refs) == 1 else jnp.concatenate([ref[e] for ref in refs], axis=0)


def term_kernel(turned_ref, *refs):
    part_refs, keep_ref, give_ref = refs[:-2], refs[-2], refs[-1]
    held, _, across, share, slots = turned_ref.shape
    for e in range(held):
        scaled = stacked_rows(part_refs, e)
        for other, ref in ((1, give_ref), (0, keep_ref)):
            left = turned_ref[e, other].reshape(across * share, slots)
            term = jnp.dot(left, scaled, preferred_element_type=F32).astype(BF16)
            for step in range(across):
                ref[step, e] = term[step * share : (step + 1) * share]


def pair_kernel(cuts, keep_ref, got_ref, *out_refs):
    out_refs = iter(out_refs)
    for step in range(1, keep_ref.shape[0]):
        start = 0
        for rows in cuts:
            at = slice(start, start + rows)
            pair = keep_ref[step, :, at].astype(F32) + got_ref[step, :, at].astype(F32)
            next(out_refs)[...] = pair.astype(BF16)
            start += rows


def last_kernel(cuts, start, keep_ref, got_ref, *refs):
    out_ref, mark_ref, total_ref, sem = refs[-4:]
    mark_ref[...] = jnp.zeros(mark_ref.shape, F32)
    others = len(cuts) * (keep_ref.shape[0] - 1)
    for e in range(keep_ref.shape[1]):
        row = 0
        for part, rows in enumerate(cuts):
            at = slice(row, row + rows)
            total = keep_ref[0, e, at].astype(F32) + got_ref[0, e, at].astype(F32)
            for ref in refs[part : others : len(cuts)]:
                total = total + ref[e].astype(F32)
            total_ref[at, e, :] = total
            row += rows
    copy = pltpu.make_async_copy(
        total_ref, out_ref.at[:, :, start : start + total_ref.shape[2]], sem
    )
    copy.start()
    copy.wait()


def raw_kernel(parts, start, final, weight_ref, *refs):
    part_refs, refs = refs[:parts], refs[parts:]
    if start:
        acc_ref, refs = refs[0], refs[1:]
    width = part_refs[0].shape[2]
    for e in range(weight_ref.shape[0]):
        raw = lax.dot_general(
            stacked_rows(part_refs, e),
            weight_ref[e, :, start : start + width],
            (((1,), (1,)), ((), ())),
            preferred_element_type=F32,
        )
        if start:
            raw = raw + acc_ref[e]
        if not final:
            refs[0][e] = raw
            continue
        hidden_ref, grad_ref, sums_ref = refs
        sources, _, own, units = hidden_ref.shape
        me = lax.axis_index("expert") if sources > 1 else 0
        folds = []
        for part in range(sources):
            source = source_of(me, part) if sources > 1 else 0
            block = raw[part * own : (part + 1) * own]
            grad_ref[source, e] = block.astype(BF16)
            product = block * hidden_ref[source, e].astype(F32)
            folds.append(
                functools.reduce(jnp.add, [product[:, i : i + 128] for i in range(0, units, 128)])
            )
        folded = jnp.concatenate(folds, axis=0) if len(folds) > 1 else folds[0]
        sums_ref[e : e + 1, :] = jnp.sum(folded.T, axis=0, keepdims=True)


def prob_kernel(direct, capacity, flat_ref, probs_ref, *refs):
    out_ref = refs[-1]
    chosen, tokens = flat_ref.shape
    if direct:
        values = []
        for part in range(LINE * SIDES):
            at = part * capacity
            ref = refs[part // SIDES]
            values += [ref[part % SIDES, e : e + 1, at : at + capacity] for e in range(ref.shape[1])]
        lanes = 128 // capacity
        values = jnp.concatenate(
            [
                jnp.concatenate([v.reshape(1, capacity) for v in values[i : i + lanes]], axis=1)
                for i in range(0, len(values), lanes)
            ],
            axis=0,
        )
        me = lax.axis_index("expert")
    else:
        values = refs[0][...]
        me = 0
    lines = values.shape[0]
    spare = jnp.zeros((-lines % 8, 128), F32)
    columns = jnp.concatenate([values, spare], axis=0).T if spare.size else values.T
    total, gates, word = gates_of(probs_ref[...])
    group = lines * 128 // (LINE * SIDES)
    picked = [jnp.zeros((1, tokens), F32) for _ in range(chosen)]
    for line in range(lines):
        at = lax.broadcasted_iota(I32, (128, tokens), 0) + line * 128
        slot = (target_of(me, at // group) if direct else at // group) * group + at % group
        for k in range(chosen):
            hit = jnp.where(flat_ref[k : k + 1, :] == slot, columns[:, line : line + 1], 0.0)
            picked[k] += jnp.sum(hit, axis=0, keepdims=True)
    picked = [picked[k] / word[k : k + 1] for k in range(chosen)]
    mixed = functools.reduce(jnp.add, [gates[k : k + 1] * picked[k] for k in range(chosen)])
    for k in range(chosen):
        out_ref[k : k + 1, :] = (picked[k] - mixed) / total


def chunks_of(features):
    unit = features // 16
    return [6 * unit, 8 * unit, 2 * unit]


def cuts_of(share, c):
    return [share // 3] * 3 if c == 0 else [share]


sds = jax.ShapeDtypeStruct


class Relay:
    def __init__(self, call, grad_out, ids, probs, held, capacity, widths):
        tokens, features = grad_out.shape
        self.call, self.rows, self.held, self.capacity = call, grad_out, held, capacity
        self.chosen, self.widths, self.place = ids.shape[0], widths, None
        self.flat, self.first = call(
            functools.partial(begin_kernel, LINE * SIDES * held, capacity),
            [sds(ids.shape, I32), sds((tokens + INFO, widths[0]), BF16)],
            ids,
            probs,
            grad_out,
            in_specs=[HBM] * 3,
            scratch_shapes=[
                pltpu.VMEM(ids.shape, I32),
                pltpu.VMEM(probs.shape, F32),
                pltpu.SemaphoreType.DMA((3,)),
            ],
            room=60,
            keep=False,
        )
        self.first_other = self.swap(self.first)

    def swap(self, block):
        return lax.ppermute(block, "expert", [(i, i ^ 1) for i in range(LINE * SIDES)])

    def send(self, block, d):
        pairs = [(i, target_of(i, SIDES * d)) for i in range(LINE * SIDES)]
        return lax.ppermute(block, "expert", pairs)

    def chunk(self, c):
        held, capacity, tokens = self.held, self.capacity, self.rows.shape[0]
        rows = [sds((held, SIDES * capacity, self.widths[c]), BF16)] * LINE
        place = sds((SIDES, LINE * held * capacity, tokens), BF16)
        start = sum(self.widths[:c]) if c else None
        kernel = functools.partial(pick_kernel, held, capacity, self.chosen, start)
        if c == 0:
            rest = sds((tokens, self.rows.shape[1] - self.widths[0]), BF16)
            *sent, self.place, rest = self.call(
                kernel,
                [*rows, place, rest],
                self.first,
                self.first_other,
                self.rows,
                in_specs=[VMEM, VMEM, HBM],
                scratch_shapes=[pltpu.SemaphoreType.DMA],
            )
        else:
            sent = self.call(kernel, rows, self.rows, self.rest_other, self.place)
        got = [sent[0]] + [None] * (LINE - 1)
        for d in range(LINE - 1, 0, -1):
            got[d] = self.send(sent[d], d)
        if c == 0:
            self.rest_other = self.swap(rest)
        return got


def exchanged(grad_out, ids, probs, groups, held, capacity, widths):
    tokens = grad_out.shape[0]
    experts = groups * held
    slots = experts * capacity
    _, _, word = gates_of(probs)
    flat = ids * capacity + jnp.concatenate(slots_of(ids, experts), axis=0).astype(I32)
    slot = lax.broadcasted_iota(I32, (slots, tokens), 0)
    place = sum(jnp.where(f == slot, w, 0.0) for f, w in zip(flat, word)).astype(BF16)
    arrived, start = [], 0
    for width in widths:
        rows = grad_out[:, start : start + width]
        sent = jnp.dot(place, rows, preferred_element_type=F32).astype(BF16)
        got = lax.all_to_all(
            sent.reshape(groups, held, capacity, width),
            "expert",
            split_axis=0,
            concat_axis=0,
            tiled=True,
        )
        arrived.append([got.transpose(1, 0, 2, 3).reshape(held, groups * capacity, width)])
        start += width
    return flat, arrived


def body(grad_out, route_ids, route_probs, hidden, w_down):
    groups = lax.axis_size("expert")
    dp = lax.axis_size("dp")
    held, units, features = w_down.shape
    capacity = hidden.shape[3]
    slots = groups * held * capacity
    per_expert = slots // held
    tokens, chosen = route_ids.shape
    share, across = units // dp, dp // 2
    direct = groups == LINE * SIDES
    widths = chunks_of(features)
    count = len(widths)

    ids, probs = route_ids.T, route_probs.T
    call = Chain()
    if direct:
        relay = Relay(call, grad_out, ids, probs, held, capacity, widths)
        flat, saved = relay.flat, hidden[0]
    else:
        flat, arrived = exchanged(grad_out, ids, probs, groups, held, capacity, widths)
        saved = hidden[0].transpose(1, 0, 2, 3).reshape(1, held, per_expert, units)
    turned = call(
        functools.partial(turn_kernel, dp),
        sds((held, 2, across, share, per_expert), BF16),
        saved,
        *([grad_out] if direct else []),
    )
    if direct:
        arrived = [relay.chunk(c) for c in range(min(2, count))]

    starts = [sum(widths[:c]) for c in range(count)]
    state = {"raw": None, "grad": None}
    summed = []

    def reduced(c):
        parts, width = arrived[c], widths[c]
        piece = sds((across, held, share, width), BF16)
        after = summed[0][2][:2] if c == 1 else ()
        keep, give = call(term_kernel, [piece, piece], turned, *parts, after=after)
        got = lax.ppermute(give, "dp", [(i, i ^ 1) for i in range(dp)])
        final = c == count - 1
        if final:
            outs = [sds(saved.shape, BF16), sds((held, per_expert), F32)]
        else:
            outs = [sds((held, per_expert, units), F32)]
        extra = ([state["raw"]] if c else []) + ([saved] if final else [])
        kernel = functools.partial(raw_kernel, len(parts), starts[c], final)
        made = call(
            kernel,
            outs,
            w_down,
            *parts,
            *extra,
        )
        state["raw"] = made if final else made[0]
        cuts = cuts_of(share, c)
        pieces = [sds((held, rows, width), BF16) for rows in cuts]
        pairs = call(functools.partial(pair_kernel, cuts), pieces * (across - 1), keep, got)
        others = []
        for i, pair in enumerate(pairs):
            step = 1 + i // len(cuts)
            shift = [(2 * r + k, 2 * ((r + step) % across) + k) for r in range(across) for k in range(2)]
            others.append(lax.ppermute(pair, "dp", shift))
        summed.append((keep, got, others))

    def finished(c):
        keep, got, others = summed[c]
        before = [] if state["grad"] is None else [state["grad"]]
        count = 2 + len(others)
        state["grad"], _ = call(
            functools.partial(last_kernel, cuts_of(share, c), starts[c]),
            [sds((share, held, features), F32), sds((8, 128), F32)],
            keep,
            got,
            *others,
            *before,
            in_specs=[VMEM] * count + [ANY] * len(before),
            out_specs=[ANY, VMEM],
            input_output_aliases={count: 0} if before else {},
            scratch_shapes=[
                pltpu.VMEM((share, held, widths[c]), F32),
                pltpu.SemaphoreType.DMA,
            ],
        )

    for c in range(count):
        reduced(c)
        if direct and c + 2 < count:
            arrived.append(relay.chunk(c + 2))
        if c >= 1:
            finished(c - 1)
    hidden_grad, sums = state["raw"]

    if direct:
        swap = [(i, i ^ 1) for i in range(groups)]
        both = jnp.stack([sums, lax.ppermute(sums, "expert", swap)])
        returned = [both] + [
            lax.ppermute(both, "expert", [(target_of(i, SIDES * d), i) for i in range(groups)])
            for d in range(1, LINE)
        ]
    else:
        sums = sums.reshape(held, groups, capacity).transpose(1, 0, 2).reshape(groups, -1)
        hidden_grad = hidden_grad.reshape(held, groups, capacity, units).transpose(1, 0, 2, 3)
        returned = lax.all_to_all(sums, "expert", split_axis=0, concat_axis=0, tiled=True)
        returned = [returned.reshape(-1, 128)]
    prob_grad = call(
        functools.partial(prob_kernel, direct, capacity),
        sds((chosen, tokens), F32),
        flat,
        probs,
        *returned,
        keep=False,
    ).T
    finished(count - 1)
    weight_grad = state["grad"]
    return (hidden_grad.reshape(hidden.shape), prob_grad, weight_grad)


def solution(mesh):
    in_specs = (
        P(("dp", "expert"), None),
        P(("dp", "expert"), None),
        P(("dp", "expert"), None),
        P("dp", None, "expert", None, None),
        P("expert", None, None),
    )
    out_specs = (
        P("dp", None, "expert", None, None),
        P(("dp", "expert"), None),
        P("dp", "expert", None),
    )
    return jax.shard_map(body, mesh=mesh, in_specs=in_specs, out_specs=out_specs, check_vma=False)
```

```python
import functools

import jax
import jax.numpy as jnp
from jax import lax
from jax.experimental import pallas as pl
from jax.experimental.pallas import tpu as pltpu
from jax.sharding import PartitionSpec as P

F32, BF16, I32 = jnp.float32, jnp.bfloat16, jnp.int32
VMEM = pl.BlockSpec(memory_space=pltpu.VMEM)
ANY = pl.BlockSpec(memory_space=pl.ANY)
HBM = pl.BlockSpec(memory_space=pltpu.HBM)

LINE, SIDES = 4, 2
BACK = (0, 1, 3, 2)
INFO = 16


def moved(me, places, side):
    return (me // SIDES + places) % LINE * SIDES + (me % SIDES ^ side)


def source_of(me, part):
    return moved(me, LINE - BACK[part % LINE], part // LINE)


class Chain:
    def __init__(self):
        self.last = None

    def __call__(self, kernel, outs, *args, in_specs=None, keep=True, after=(), room=24, **kw):
        in_specs = list(in_specs or [VMEM] * len(args))
        count = len(args)
        body = kernel
        unread = [*after] if self.last is None else [self.last, *after]
        if unread:
            args, in_specs = (*args, *unread), in_specs + [ANY] * len(unread)

            def body(*refs):
                kernel(*refs[:count], *refs[count + len(unread) :])

        made = pl.pallas_call(
            body,
            out_shape=outs,
            in_specs=in_specs,
            compiler_params=pltpu.CompilerParams(vmem_limit_bytes=room * 1024 * 1024),
            cost_estimate=pl.CostEstimate(flops=1, bytes_accessed=1, transcendentals=0),
            **kw,
        )(*args)
        if keep:
            self.last = min(jax.tree.leaves(made), key=lambda x: x.size)
        return made


def gates_of(probs):
    total = jnp.sum(probs, axis=0, keepdims=True)
    gates = probs / total
    return total, gates, gates.astype(BF16).astype(F32)


def slots_of(ids, experts):
    chosen, tokens = ids.shape
    expert = lax.broadcasted_iota(I32, (experts, tokens), 0)
    named = [ids[k : k + 1] == expert for k in range(chosen)]
    hits = functools.reduce(jnp.add, [n.astype(F32) for n in named]).astype(BF16)
    row = lax.broadcasted_iota(I32, (tokens, tokens), 0)
    earlier = (row < lax.broadcasted_iota(I32, (tokens, tokens), 1)).astype(F32).astype(BF16)
    before = jnp.dot(hits, earlier, preferred_element_type=F32)
    return [jnp.sum(jnp.where(n, before, 0.0), axis=0, keepdims=True) for n in named]


def begin_kernel(experts, capacity, ids_ref, probs_ref, rows_ref, flat_ref, out_ref, *scratch):
    ids_got, probs_got, sems = scratch
    chosen, tokens = ids_got.shape
    width = out_ref.shape[1]
    copies = [
        pltpu.make_async_copy(ids_ref, ids_got, sems.at[0]),
        pltpu.make_async_copy(probs_ref, probs_got, sems.at[1]),
        pltpu.make_async_copy(rows_ref.at[:, :width], out_ref.at[:tokens], sems.at[2]),
    ]
    for copy in copies:
        copy.start()
    for copy in copies:
        copy.wait()
    ids = ids_got[...]
    _, _, word = gates_of(probs_got[...])
    slots = slots_of(ids, experts)
    for k in range(chosen):
        flat_ref[k : k + 1, :] = ids[k : k + 1] * capacity + slots[k].astype(I32)
    rest = jnp.zeros((INFO - 3 * chosen, tokens), F32)
    info = jnp.concatenate([ids.astype(F32), *slots, word, rest], axis=0).astype(BF16)
    out_ref[tokens:, :tokens] = info
    if width > tokens:
        out_ref[tokens:, tokens:] = jnp.zeros((INFO, width - tokens), BF16)


def places(held, capacity, chosen, ref, place_ref):
    tokens = place_ref.shape[1]
    rows = held * capacity
    me = lax.axis_index("expert")
    local = lax.broadcasted_iota(I32, (rows, tokens), 0)
    info = ref[tokens:, :tokens].astype(F32)
    flat = (info[:chosen] * capacity + info[chosen : 2 * chosen]).astype(I32)
    word = info[2 * chosen : 3 * chosen]
    for side in range(SIDES):
        slot = local + (me ^ side) * rows
        hits = [jnp.where(flat[k : k + 1] == slot, word[k : k + 1], 0.0) for k in range(chosen)]
        place_ref[side * rows : (side + 1) * rows, :] = functools.reduce(jnp.add, hits).astype(BF16)


def pick(held, capacity, block_refs, place_ref, out_refs):
    tokens = place_ref.shape[2]
    for j, ref in enumerate(block_refs):
        scaled = jnp.dot(place_ref[j], ref[:tokens, :], preferred_element_type=F32).astype(BF16)
        for side, out_ref in enumerate(out_refs):
            for e in range(held):
                at = (side * held + e) * capacity
                out_ref[e, j * capacity : (j + 1) * capacity, :] = scaled[at : at + capacity]


def pick_kernel(held, capacity, chosen, first, count, *refs):
    block_refs, refs = refs[:count], refs[count:]
    if first:
        mine_ref, other_ref, place_ref = refs
        for j, ref in enumerate(block_refs):
            places(held, capacity, chosen, ref, place_ref.at[j])
    else:
        place_ref, mine_ref, other_ref = refs
    pick(held, capacity, block_refs, place_ref, (mine_ref, other_ref))


def turn_kernel(dp, hidden_ref, *refs):
    out_ref, refs = refs[-1], refs[:-1]
    parts, held, _, units = hidden_ref.shape
    share, across = units // dp, dp // 2
    me = lax.axis_index("expert") if parts > 1 else 0
    mine = lax.axis_index("dp")
    core, row = mine % 2, mine // 2
    for e in range(held):
        sources = [source_of(me, p) if parts > 1 else 0 for p in range(parts)]
        stacked = jnp.concatenate([hidden_ref[source, e] for source in sources], axis=0)
        turned = stacked.T
        for piece in range(dp):
            other = (piece % 2) ^ core
            step = (piece // 2 - row + across) % across
            out_ref[e, other, step] = turned[piece * share : (piece + 1) * share]


def cut_kernel(start, rows_ref, *refs):
    out_refs, sems = refs[:-1], refs[-1]
    copies = []
    for i, ref in enumerate(out_refs):
        at = slice(start, start + ref.shape[1])
        copies.append(pltpu.make_async_copy(rows_ref.at[:, at], ref, sems.at[i]))
        start += ref.shape[1]
    for copy in copies:
        copy.start()
    for copy in copies:
        copy.wait()


def stacked_rows(refs, e):
    return refs[0][e] if len(refs) == 1 else jnp.concatenate([ref[e] for ref in refs], axis=0)


def term_kernel(turned_ref, *refs):
    part_refs, keep_ref, give_ref = refs[:-2], refs[-2], refs[-1]
    held, _, across, share, slots = turned_ref.shape
    for e in range(held):
        scaled = stacked_rows(part_refs, e)
        for other, ref in ((1, give_ref), (0, keep_ref)):
            left = turned_ref[e, other].reshape(across * share, slots)
            term = jnp.dot(left, scaled, preferred_element_type=F32).astype(BF16)
            for step in range(across):
                ref[step, e] = term[step * share : (step + 1) * share]


def pair_kernel(cuts, keep_ref, got_ref, *out_refs):
    out_refs = iter(out_refs)
    for step in range(1, keep_ref.shape[0]):
        start = 0
        for rows in cuts:
            at = slice(start, start + rows)
            pair = keep_ref[step, :, at].astype(F32) + got_ref[step, :, at].astype(F32)
            next(out_refs)[...] = pair.astype(BF16)
            start += rows


def last_kernel(cuts, start, keep_ref, got_ref, *refs):
    out_ref, mark_ref, total_ref, sem = refs[-4:]
    mark_ref[...] = jnp.zeros(mark_ref.shape, F32)
    others = len(cuts) * (keep_ref.shape[0] - 1)
    for e in range(keep_ref.shape[1]):
        row = 0
        for part, rows in enumerate(cuts):
            at = slice(row, row + rows)
            total = keep_ref[0, e, at].astype(F32) + got_ref[0, e, at].astype(F32)
            for ref in refs[part : others : len(cuts)]:
                total = total + ref[e].astype(F32)
            total_ref[at, e, :] = total
            row += rows
    copy = pltpu.make_async_copy(
        total_ref, out_ref.at[:, :, start : start + total_ref.shape[2]], sem
    )
    copy.start()
    copy.wait()


def raw_kernel(parts, start, final, weight_ref, *refs):
    part_refs, refs = refs[:parts], refs[parts:]
    if start:
        acc_ref, refs = refs[0], refs[1:]
    width = part_refs[0].shape[2]
    for e in range(weight_ref.shape[0]):
        raw = lax.dot_general(
            stacked_rows(part_refs, e),
            weight_ref[e, :, start : start + width],
            (((1,), (1,)), ((), ())),
            preferred_element_type=F32,
        )
        if start:
            raw = raw + acc_ref[e]
        if not final:
            refs[0][e] = raw
            continue
        hidden_ref, grad_ref, sums_ref = refs
        sources, _, own, units = hidden_ref.shape
        me = lax.axis_index("expert") if sources > 1 else 0
        folds = []
        for part in range(sources):
            source = source_of(me, part) if sources > 1 else 0
            block = raw[part * own : (part + 1) * own]
            grad_ref[source, e] = block.astype(BF16)
            product = block * hidden_ref[source, e].astype(F32)
            folds.append(
                functools.reduce(jnp.add, [product[:, i : i + 128] for i in range(0, units, 128)])
            )
        folded = jnp.concatenate(folds, axis=0) if len(folds) > 1 else folds[0]
        sums_ref[e : e + 1, :] = jnp.sum(folded.T, axis=0, keepdims=True)


def prob_kernel(direct, capacity, flat_ref, probs_ref, *refs):
    out_ref = refs[-1]
    chosen, tokens = flat_ref.shape
    if direct:
        values = []
        for q in range(LINE * SIDES):
            at = (BACK.index(q // SIDES) + LINE * (q % SIDES)) * capacity
            ref = refs[q // SIDES]
            values += [ref[q % SIDES, e : e + 1, at : at + capacity] for e in range(ref.shape[1])]
        lanes = 128 // capacity
        values = jnp.concatenate(
            [
                jnp.concatenate([v.reshape(1, capacity) for v in values[i : i + lanes]], axis=1)
                for i in range(0, len(values), lanes)
            ],
            axis=0,
        )
        me = lax.axis_index("expert")
    else:
        values = refs[0][...]
        me = 0
    lines = values.shape[0]
    spare = jnp.zeros((-lines % 8, 128), F32)
    columns = jnp.concatenate([values, spare], axis=0).T if spare.size else values.T
    total, gates, word = gates_of(probs_ref[...])
    group = lines * 128 // (LINE * SIDES)
    picked = [jnp.zeros((1, tokens), F32) for _ in range(chosen)]
    for line in range(lines):
        at = lax.broadcasted_iota(I32, (128, tokens), 0) + line * 128
        q = at // group
        slot = (moved(me, q // SIDES, q % SIDES) if direct else q) * group + at % group
        for k in range(chosen):
            hit = jnp.where(flat_ref[k : k + 1, :] == slot, columns[:, line : line + 1], 0.0)
            picked[k] += jnp.sum(hit, axis=0, keepdims=True)
    picked = [picked[k] / word[k : k + 1] for k in range(chosen)]
    mixed = functools.reduce(jnp.add, [gates[k : k + 1] * picked[k] for k in range(chosen)])
    for k in range(chosen):
        out_ref[k : k + 1, :] = (picked[k] - mixed) / total


def chunks_of(features):
    unit = features // 16
    return [4 * unit, 6 * unit, 6 * unit]


def cuts_of(share, c):
    first = 16 * (share // 32)
    return [first, share - first] if c == 1 else [share]


sds = jax.ShapeDtypeStruct


class Relay:
    def __init__(self, call, grad_out, ids, probs, held, capacity, widths):
        tokens, features = grad_out.shape
        self.call, self.held, self.capacity, self.widths = call, held, capacity, widths
        self.tokens, self.chosen, self.place = tokens, ids.shape[0], {}
        self.flat, first = call(
            functools.partial(begin_kernel, LINE * SIDES * held, capacity),
            [sds(ids.shape, I32), sds((tokens + INFO, widths[0]), BF16)],
            ids,
            probs,
            grad_out,
            in_specs=[HBM] * 3,
            scratch_shapes=[
                pltpu.VMEM(ids.shape, I32),
                pltpu.VMEM(probs.shape, F32),
                pltpu.SemaphoreType.DMA((3,)),
            ],
            room=60,
            keep=False,
        )
        rest = call(
            functools.partial(cut_kernel, widths[0]),
            [sds((tokens, w), BF16) for w in widths[1:]],
            grad_out,
            in_specs=[HBM],
            scratch_shapes=[pltpu.SemaphoreType.DMA((len(widths) - 1,))],
            keep=False,
        )
        self.blocks, self.passed = [], []
        for own in [first, *rest]:
            on, back = self.along(own, 1), self.along(own, LINE - 1)
            self.blocks.append([own, on, back])
            self.passed.append(self.along(on, 1))

    def along(self, block, places):
        pairs = [(i, moved(i, places, 0)) for i in range(LINE * SIDES)]
        return lax.ppermute(block, "expert", pairs)

    def pick(self, c, name, blocks):
        held, capacity, count = self.held, self.capacity, len(blocks)
        rows = [sds((held, count * capacity, self.widths[c]), BF16)] * SIDES
        kernel = functools.partial(pick_kernel, held, capacity, self.chosen, c == 0, count)
        if c == 0:
            place = sds((count, SIDES * held * capacity, self.tokens), BF16)
            mine, other, self.place[name] = self.call(kernel, [*rows, place], *blocks)
        else:
            mine, other = self.call(kernel, rows, *blocks, self.place[name])
        return mine, lax.ppermute(other, "expert", [(i, i ^ 1) for i in range(LINE * SIDES)])

    def early(self, c):
        return self.pick(c, "early", self.blocks[c])

    def late(self, c, early):
        late = self.pick(c, "late", [self.passed[c]])
        return [early[0], late[0], early[1], late[1]]


def exchanged(grad_out, ids, probs, groups, held, capacity, widths):
    tokens = grad_out.shape[0]
    experts = groups * held
    slots = experts * capacity
    _, _, word = gates_of(probs)
    flat = ids * capacity + jnp.concatenate(slots_of(ids, experts), axis=0).astype(I32)
    slot = lax.broadcasted_iota(I32, (slots, tokens), 0)
    place = sum(jnp.where(f == slot, w, 0.0) for f, w in zip(flat, word)).astype(BF16)
    arrived, start = [], 0
    for width in widths:
        rows = grad_out[:, start : start + width]
        sent = jnp.dot(place, rows, preferred_element_type=F32).astype(BF16)
        got = lax.all_to_all(
            sent.reshape(groups, held, capacity, width),
            "expert",
            split_axis=0,
            concat_axis=0,
            tiled=True,
        )
        arrived.append([got.transpose(1, 0, 2, 3).reshape(held, groups * capacity, width)])
        start += width
    return flat, arrived


def body(grad_out, route_ids, route_probs, hidden, w_down):
    groups = lax.axis_size("expert")
    dp = lax.axis_size("dp")
    held, units, features = w_down.shape
    capacity = hidden.shape[3]
    slots = groups * held * capacity
    per_expert = slots // held
    tokens, chosen = route_ids.shape
    share, across = units // dp, dp // 2
    direct = groups == LINE * SIDES
    widths = chunks_of(features)
    count = len(widths)

    ids, probs = route_ids.T, route_probs.T
    call = Chain()
    if direct:
        relay = Relay(call, grad_out, ids, probs, held, capacity, widths)
        flat, saved = relay.flat, hidden[0]
    else:
        flat, arrived = exchanged(grad_out, ids, probs, groups, held, capacity, widths)
        saved = hidden[0].transpose(1, 0, 2, 3).reshape(1, held, per_expert, units)
    turned = call(
        functools.partial(turn_kernel, dp),
        sds((held, 2, across, share, per_expert), BF16),
        saved,
    )
    starts = [sum(widths[:c]) for c in range(count)]
    state = {"raw": None, "grad": None}
    summed = []

    def accumulated(c):
        parts, width, final = arrived[c], widths[c], c == count - 1
        if final:
            outs = [sds(saved.shape, BF16), sds((held, per_expert), F32)]
        else:
            outs = [sds((held, per_expert, units), F32)]
        extra = ([state["raw"]] if c else []) + ([saved] if final else [])
        kernel = functools.partial(raw_kernel, len(parts), starts[c], final)
        made = call(
            kernel,
            outs,
            w_down,
            *parts,
            *extra,
        )
        state["raw"] = made if final else made[0]

    def reduced(c):
        parts, width = arrived[c], widths[c]
        piece = sds((across, held, share, width), BF16)
        after = summed[-1][2][:1] if c else ()
        keep, give = call(term_kernel, [piece, piece], turned, *parts, after=after)
        got = lax.ppermute(give, "dp", [(i, i ^ 1) for i in range(dp)])
        if c == count - 1:
            accumulated(c)
        cuts = cuts_of(share, c)
        pieces = [sds((held, rows, width), BF16) for rows in cuts]
        pairs = call(functools.partial(pair_kernel, cuts), pieces * (across - 1), keep, got)
        others = []
        for i, pair in enumerate(pairs):
            step = 1 + i // len(cuts)
            shift = [(2 * r + k, 2 * ((r + step) % across) + k) for r in range(across) for k in range(2)]
            others.append(lax.ppermute(pair, "dp", shift))
        summed.append((keep, got, others))

    def finished(c):
        keep, got, others = summed[c]
        before = [] if state["grad"] is None else [state["grad"]]
        count = 2 + len(others)
        state["grad"], _ = call(
            functools.partial(last_kernel, cuts_of(share, c), starts[c]),
            [sds((share, held, features), F32), sds((8, 128), F32)],
            keep,
            got,
            *others,
            *before,
            in_specs=[VMEM] * count + [ANY] * len(before),
            out_specs=[ANY, VMEM],
            input_output_aliases={count: 0} if before else {},
            scratch_shapes=[
                pltpu.VMEM((share, held, widths[c]), F32),
                pltpu.SemaphoreType.DMA,
            ],
        )

    if direct:
        arrived, early = [], relay.early(0)
    for c in range(count):
        if direct:
            arrived.append(relay.late(c, early))
            if c + 1 < count:
                early = relay.early(c + 1)
        if c >= 1:
            accumulated(c - 1)
        reduced(c)
        if c >= 1:
            finished(c - 1)
    hidden_grad, sums = state["raw"]

    if direct:
        swap = [(i, i ^ 1) for i in range(groups)]
        both = jnp.stack([sums, lax.ppermute(sums, "expert", swap)])
        returned = [both] + [
            lax.ppermute(both, "expert", [(moved(i, d, 0), i) for i in range(groups)])
            for d in range(1, LINE)
        ]
    else:
        sums = sums.reshape(held, groups, capacity).transpose(1, 0, 2).reshape(groups, -1)
        hidden_grad = hidden_grad.reshape(held, groups, capacity, units).transpose(1, 0, 2, 3)
        returned = lax.all_to_all(sums, "expert", split_axis=0, concat_axis=0, tiled=True)
        returned = [returned.reshape(-1, 128)]
    prob_grad = call(
        functools.partial(prob_kernel, direct, capacity),
        sds((chosen, tokens), F32),
        flat,
        probs,
        *returned,
        keep=False,
    ).T
    finished(count - 1)
    weight_grad = state["grad"]
    return (hidden_grad.reshape(hidden.shape), prob_grad, weight_grad)


def solution(mesh):
    in_specs = (
        P(("dp", "expert"), None),
        P(("dp", "expert"), None),
        P(("dp", "expert"), None),
        P("dp", None, "expert", None, None),
        P("expert", None, None),
    )
    out_specs = (
        P("dp", None, "expert", None, None),
        P(("dp", "expert"), None),
        P("dp", "expert", None),
    )
    return jax.shard_map(body, mesh=mesh, in_specs=in_specs, out_specs=out_specs, check_vma=False)
```

```python
import functools

import jax
import jax.numpy as jnp
from jax import lax
from jax.experimental import pallas as pl
from jax.experimental.pallas import tpu as pltpu
from jax.sharding import PartitionSpec as P

F32, BF16, I32 = jnp.float32, jnp.bfloat16, jnp.int32
VMEM = pl.BlockSpec(memory_space=pltpu.VMEM)
ANY = pl.BlockSpec(memory_space=pl.ANY)
HBM = pl.BlockSpec(memory_space=pltpu.HBM)

LINE, SIDES = 4, 2
BACK = (0, 1, 3, 2)
INFO = 16


def moved(me, places, side):
    return (me // SIDES + places) % LINE * SIDES + (me % SIDES ^ side)


def source_of(me, part):
    return moved(me, LINE - BACK[part % LINE], part // LINE)


class Chain:
    def __init__(self):
        self.last = None

    def __call__(self, kernel, outs, *args, in_specs=None, keep=True, after=(), room=24, **kw):
        in_specs = list(in_specs or [VMEM] * len(args))
        count = len(args)
        body = kernel
        unread = [*after] if self.last is None else [self.last, *after]
        if unread:
            args, in_specs = (*args, *unread), in_specs + [ANY] * len(unread)

            def body(*refs):
                kernel(*refs[:count], *refs[count + len(unread) :])

        made = pl.pallas_call(
            body,
            out_shape=outs,
            in_specs=in_specs,
            compiler_params=pltpu.CompilerParams(vmem_limit_bytes=room * 1024 * 1024),
            cost_estimate=pl.CostEstimate(flops=1, bytes_accessed=1, transcendentals=0),
            **kw,
        )(*args)
        if keep:
            self.last = min(jax.tree.leaves(made), key=lambda x: x.size)
        return made


def gates_of(probs):
    total = jnp.sum(probs, axis=0, keepdims=True)
    gates = probs / total
    return total, gates, gates.astype(BF16).astype(F32)


def slots_of(ids, experts):
    chosen, tokens = ids.shape
    expert = lax.broadcasted_iota(I32, (experts, tokens), 0)
    named = [ids[k : k + 1] == expert for k in range(chosen)]
    hits = functools.reduce(jnp.add, [n.astype(F32) for n in named]).astype(BF16)
    row = lax.broadcasted_iota(I32, (tokens, tokens), 0)
    earlier = (row < lax.broadcasted_iota(I32, (tokens, tokens), 1)).astype(F32).astype(BF16)
    before = jnp.dot(hits, earlier, preferred_element_type=F32)
    return [jnp.sum(jnp.where(n, before, 0.0), axis=0, keepdims=True) for n in named]


def begin_kernel(experts, capacity, ids_ref, probs_ref, rows_ref, flat_ref, out_ref, *scratch):
    ids_got, probs_got, sems = scratch
    chosen, tokens = ids_got.shape
    width = out_ref.shape[1]
    copies = [
        pltpu.make_async_copy(ids_ref, ids_got, sems.at[0]),
        pltpu.make_async_copy(probs_ref, probs_got, sems.at[1]),
        pltpu.make_async_copy(rows_ref.at[:, :width], out_ref.at[:tokens], sems.at[2]),
    ]
    for copy in copies:
        copy.start()
    for copy in copies:
        copy.wait()
    ids = ids_got[...]
    _, _, word = gates_of(probs_got[...])
    slots = slots_of(ids, experts)
    for k in range(chosen):
        flat_ref[k : k + 1, :] = ids[k : k + 1] * capacity + slots[k].astype(I32)
    rest = jnp.zeros((INFO - 3 * chosen, tokens), F32)
    info = jnp.concatenate([ids.astype(F32), *slots, word, rest], axis=0).astype(BF16)
    out_ref[tokens:, :tokens] = info
    if width > tokens:
        out_ref[tokens:, tokens:] = jnp.zeros((INFO, width - tokens), BF16)


def places(held, capacity, chosen, ref, place_ref):
    tokens = place_ref.shape[1]
    rows = held * capacity
    me = lax.axis_index("expert")
    local = lax.broadcasted_iota(I32, (rows, tokens), 0)
    info = ref[tokens:, :tokens].astype(F32)
    flat = (info[:chosen] * capacity + info[chosen : 2 * chosen]).astype(I32)
    word = info[2 * chosen : 3 * chosen]
    for side in range(SIDES):
        slot = local + (me ^ side) * rows
        hits = [jnp.where(flat[k : k + 1] == slot, word[k : k + 1], 0.0) for k in range(chosen)]
        place_ref[side * rows : (side + 1) * rows, :] = functools.reduce(jnp.add, hits).astype(BF16)


def pick(held, capacity, block_refs, place_ref, out_refs):
    tokens = place_ref.shape[2]
    for j, ref in enumerate(block_refs):
        scaled = jnp.dot(place_ref[j], ref[:tokens, :], preferred_element_type=F32).astype(BF16)
        for side, out_ref in enumerate(out_refs):
            for e in range(held):
                at = (side * held + e) * capacity
                out_ref[e, j * capacity : (j + 1) * capacity, :] = scaled[at : at + capacity]


def pick_kernel(held, capacity, chosen, first, count, *refs):
    block_refs, refs = refs[:count], refs[count:]
    if first:
        mine_ref, other_ref, place_ref = refs
        for j, ref in enumerate(block_refs):
            places(held, capacity, chosen, ref, place_ref.at[j])
    else:
        place_ref, mine_ref, other_ref = refs
    pick(held, capacity, block_refs, place_ref, (mine_ref, other_ref))


def turn_kernel(dp, hidden_ref, *refs):
    out_ref, refs = refs[-1], refs[:-1]
    parts, held, _, units = hidden_ref.shape
    share, across = units // dp, dp // 2
    me = lax.axis_index("expert") if parts > 1 else 0
    mine = lax.axis_index("dp")
    row = mine // 2
    for e in range(held):
        sources = [source_of(me, p) if parts > 1 else 0 for p in range(parts)]
        stacked = jnp.concatenate([hidden_ref[source, e] for source in sources], axis=0)
        turned = stacked.T
        for piece in range(dp):
            other = piece % 2
            step = (piece // 2 - row + across) % across
            out_ref[e, other, step] = turned[piece * share : (piece + 1) * share]


def cut_kernel(start, rows_ref, *refs):
    out_refs, sems = refs[:-1], refs[-1]
    copies = []
    for i, ref in enumerate(out_refs):
        at = slice(start, start + ref.shape[1])
        copies.append(pltpu.make_async_copy(rows_ref.at[:, at], ref, sems.at[i]))
        start += ref.shape[1]
    for copy in copies:
        copy.start()
    for copy in copies:
        copy.wait()


def stacked_rows(refs, e):
    return refs[0][e] if len(refs) == 1 else jnp.concatenate([ref[e] for ref in refs], axis=0)


def term_kernel(turned_ref, *refs):
    part_refs, out_ref = refs[:-1], refs[-1]
    held, cores, across, share, slots = turned_ref.shape
    for e in range(held):
        scaled = stacked_rows(part_refs, e)
        for core in range(cores):
            left = turned_ref[e, core].reshape(across * share, slots)
            term = jnp.dot(left, scaled, preferred_element_type=F32).astype(BF16)
            for step in range(across):
                out_ref[core, step, e] = term[step * share : (step + 1) * share]


def pair_kernel(cuts, both_ref, *out_refs):
    out_refs = iter(out_refs)
    for step in range(1, both_ref.shape[1]):
        start = 0
        for rows in cuts:
            at = slice(start, start + rows)
            pair = both_ref[0, step, :, at].astype(F32) + both_ref[1, step, :, at].astype(F32)
            next(out_refs)[...] = pair.astype(BF16)
            start += rows


def last_kernel(cuts, start, both_ref, *refs):
    out_ref, mark_ref, total_ref, sem = refs[-4:]
    mark_ref[...] = jnp.zeros(mark_ref.shape, F32)
    others = len(cuts) * (both_ref.shape[1] - 1)
    for e in range(both_ref.shape[2]):
        row = 0
        for part, rows in enumerate(cuts):
            at = slice(row, row + rows)
            total = both_ref[0, 0, e, at].astype(F32) + both_ref[1, 0, e, at].astype(F32)
            for ref in refs[part : others : len(cuts)]:
                total = total + ref[e].astype(F32)
            total_ref[at, e, :] = total
            row += rows
    copy = pltpu.make_async_copy(
        total_ref, out_ref.at[:, :, start : start + total_ref.shape[2]], sem
    )
    copy.start()
    copy.wait()


def raw_kernel(parts, start, final, weight_ref, *refs):
    part_refs, refs = refs[:parts], refs[parts:]
    if start:
        acc_ref, refs = refs[0], refs[1:]
    width = part_refs[0].shape[2]
    for e in range(weight_ref.shape[0]):
        raw = lax.dot_general(
            stacked_rows(part_refs, e),
            weight_ref[e, :, start : start + width],
            (((1,), (1,)), ((), ())),
            preferred_element_type=F32,
        )
        if start:
            raw = raw + acc_ref[e]
        if not final:
            refs[0][e] = raw
            continue
        hidden_ref, grad_ref, sums_ref = refs
        sources, _, own, units = hidden_ref.shape
        me = lax.axis_index("expert") if sources > 1 else 0
        folds = []
        for part in range(sources):
            source = source_of(me, part) if sources > 1 else 0
            block = raw[part * own : (part + 1) * own]
            grad_ref[source, e] = block.astype(BF16)
            product = block * hidden_ref[source, e].astype(F32)
            folds.append(
                functools.reduce(jnp.add, [product[:, i : i + 128] for i in range(0, units, 128)])
            )
        folded = jnp.concatenate(folds, axis=0) if len(folds) > 1 else folds[0]
        sums_ref[e : e + 1, :] = jnp.sum(folded.T, axis=0, keepdims=True)


def prob_kernel(direct, capacity, flat_ref, probs_ref, *refs):
    out_ref = refs[-1]
    chosen, tokens = flat_ref.shape
    if direct:
        values = []
        for q in range(LINE * SIDES):
            at = (BACK.index(q // SIDES) + LINE * (q % SIDES)) * capacity
            ref = refs[q // SIDES]
            values += [ref[q % SIDES, e : e + 1, at : at + capacity] for e in range(ref.shape[1])]
        lanes = 128 // capacity
        values = jnp.concatenate(
            [
                jnp.concatenate([v.reshape(1, capacity) for v in values[i : i + lanes]], axis=1)
                for i in range(0, len(values), lanes)
            ],
            axis=0,
        )
        me = lax.axis_index("expert")
    else:
        values = refs[0][...]
        me = 0
    lines = values.shape[0]
    spare = jnp.zeros((-lines % 8, 128), F32)
    columns = jnp.concatenate([values, spare], axis=0).T if spare.size else values.T
    total, gates, word = gates_of(probs_ref[...])
    group = lines * 128 // (LINE * SIDES)
    picked = [jnp.zeros((1, tokens), F32) for _ in range(chosen)]
    for line in range(lines):
        at = lax.broadcasted_iota(I32, (128, tokens), 0) + line * 128
        q = at // group
        slot = (moved(me, q // SIDES, q % SIDES) if direct else q) * group + at % group
        for k in range(chosen):
            hit = jnp.where(flat_ref[k : k + 1, :] == slot, columns[:, line : line + 1], 0.0)
            picked[k] += jnp.sum(hit, axis=0, keepdims=True)
    picked = [picked[k] / word[k : k + 1] for k in range(chosen)]
    mixed = functools.reduce(jnp.add, [gates[k : k + 1] * picked[k] for k in range(chosen)])
    for k in range(chosen):
        out_ref[k : k + 1, :] = (picked[k] - mixed) / total


def chunks_of(features):
    unit = features // 16
    return [4 * unit, 6 * unit, 6 * unit]


def cuts_of(share, c):
    first = 16 * (share // 32)
    return [share]


sds = jax.ShapeDtypeStruct


class Relay:
    def __init__(self, call, grad_out, ids, probs, held, capacity, widths):
        tokens, features = grad_out.shape
        self.call, self.held, self.capacity, self.widths = call, held, capacity, widths
        self.tokens, self.chosen, self.place = tokens, ids.shape[0], {}
        self.flat, first = call(
            functools.partial(begin_kernel, LINE * SIDES * held, capacity),
            [sds(ids.shape, I32), sds((tokens + INFO, widths[0]), BF16)],
            ids,
            probs,
            grad_out,
            in_specs=[HBM] * 3,
            scratch_shapes=[
                pltpu.VMEM(ids.shape, I32),
                pltpu.VMEM(probs.shape, F32),
                pltpu.SemaphoreType.DMA((3,)),
            ],
            room=60,
            keep=False,
        )
        rest = call(
            functools.partial(cut_kernel, widths[0]),
            [sds((tokens, w), BF16) for w in widths[1:]],
            grad_out,
            in_specs=[HBM],
            scratch_shapes=[pltpu.SemaphoreType.DMA((len(widths) - 1,))],
            keep=False,
        )
        self.blocks, self.passed = [], []
        for own in [first, *rest]:
            on, back = self.along(own, 1), self.along(own, LINE - 1)
            self.blocks.append([own, on, back])
            self.passed.append(self.along(on, 1))

    def along(self, block, places):
        pairs = [(i, moved(i, places, 0)) for i in range(LINE * SIDES)]
        return lax.ppermute(block, "expert", pairs)

    def pick(self, c, name, blocks):
        held, capacity, count = self.held, self.capacity, len(blocks)
        rows = [sds((held, count * capacity, self.widths[c]), BF16)] * SIDES
        kernel = functools.partial(pick_kernel, held, capacity, self.chosen, c == 0, count)
        if c == 0:
            place = sds((count, SIDES * held * capacity, self.tokens), BF16)
            mine, other, self.place[name] = self.call(kernel, [*rows, place], *blocks)
        else:
            mine, other = self.call(kernel, rows, *blocks, self.place[name])
        return mine, lax.ppermute(other, "expert", [(i, i ^ 1) for i in range(LINE * SIDES)])

    def early(self, c):
        return self.pick(c, "early", self.blocks[c])

    def late(self, c, early):
        late = self.pick(c, "late", [self.passed[c]])
        return [early[0], late[0], early[1], late[1]]


def exchanged(grad_out, ids, probs, groups, held, capacity, widths):
    tokens = grad_out.shape[0]
    experts = groups * held
    slots = experts * capacity
    _, _, word = gates_of(probs)
    flat = ids * capacity + jnp.concatenate(slots_of(ids, experts), axis=0).astype(I32)
    slot = lax.broadcasted_iota(I32, (slots, tokens), 0)
    place = sum(jnp.where(f == slot, w, 0.0) for f, w in zip(flat, word)).astype(BF16)
    arrived, start = [], 0
    for width in widths:
        rows = grad_out[:, start : start + width]
        sent = jnp.dot(place, rows, preferred_element_type=F32).astype(BF16)
        got = lax.all_to_all(
            sent.reshape(groups, held, capacity, width),
            "expert",
            split_axis=0,
            concat_axis=0,
            tiled=True,
        )
        arrived.append([got.transpose(1, 0, 2, 3).reshape(held, groups * capacity, width)])
        start += width
    return flat, arrived


def body(grad_out, route_ids, route_probs, hidden, w_down):
    groups = lax.axis_size("expert")
    dp = lax.axis_size("dp")
    held, units, features = w_down.shape
    capacity = hidden.shape[3]
    slots = groups * held * capacity
    per_expert = slots // held
    tokens, chosen = route_ids.shape
    share, across = units // dp, dp // 2
    direct = groups == LINE * SIDES
    widths = chunks_of(features)
    count = len(widths)

    ids, probs = route_ids.T, route_probs.T
    call = Chain()
    if direct:
        relay = Relay(call, grad_out, ids, probs, held, capacity, widths)
        flat, saved = relay.flat, hidden[0]
    else:
        flat, arrived = exchanged(grad_out, ids, probs, groups, held, capacity, widths)
        saved = hidden[0].transpose(1, 0, 2, 3).reshape(1, held, per_expert, units)
    turned = call(
        functools.partial(turn_kernel, dp),
        sds((held, 2, across, share, per_expert), BF16),
        saved,
    )
    starts = [sum(widths[:c]) for c in range(count)]
    state = {"raw": None, "grad": None}
    summed = []

    def accumulated(c):
        parts, width, final = arrived[c], widths[c], c == count - 1
        if final:
            outs = [sds(saved.shape, BF16), sds((held, per_expert), F32)]
        else:
            outs = [sds((held, per_expert, units), F32)]
        extra = ([state["raw"]] if c else []) + ([saved] if final else [])
        kernel = functools.partial(raw_kernel, len(parts), starts[c], final)
        made = call(
            kernel,
            outs,
            w_down,
            *parts,
            *extra,
        )
        state["raw"] = made if final else made[0]

    def reduced(c):
        parts, width = arrived[c], widths[c]
        piece = sds((2, across, held, share, width), BF16)
        both = lax.all_to_all(
            call(term_kernel, piece, turned, *parts),
            "dp",
            0,
            0,
            axis_index_groups=[[i, i + 1] for i in range(0, dp, 2)],
            tiled=True,
        )
        if c == count - 1:
            accumulated(c)
        cuts = cuts_of(share, c)
        pieces = [sds((held, rows, width), BF16) for rows in cuts]
        pairs = call(functools.partial(pair_kernel, cuts), pieces * (across - 1), both)
        others = []
        for i, pair in enumerate(pairs):
            step = 1 + i // len(cuts)
            shift = [(2 * r + k, 2 * ((r + step) % across) + k) for r in range(across) for k in range(2)]
            others.append(lax.ppermute(pair, "dp", shift))
        summed.append((both, others))

    def finished(c):
        both, others = summed[c]
        before = [] if state["grad"] is None else [state["grad"]]
        count = 1 + len(others)
        state["grad"], _ = call(
            functools.partial(last_kernel, cuts_of(share, c), starts[c]),
            [sds((share, held, features), F32), sds((8, 128), F32)],
            both,
            *others,
            *before,
            in_specs=[VMEM] * count + [ANY] * len(before),
            out_specs=[ANY, VMEM],
            input_output_aliases={count: 0} if before else {},
            scratch_shapes=[
                pltpu.VMEM((share, held, widths[c]), F32),
                pltpu.SemaphoreType.DMA,
            ],
        )

    if direct:
        arrived, early = [], relay.early(0)
    for c in range(count):
        if direct:
            arrived.append(relay.late(c, early))
            if c + 1 < count:
                early = relay.early(c + 1)
        if c >= 1:
            accumulated(c - 1)
        reduced(c)
        if 1 <= c < count - 1:
            finished(c - 1)
    hidden_grad, sums = state["raw"]

    if direct:
        swap = [(i, i ^ 1) for i in range(groups)]
        both = jnp.stack([sums, lax.ppermute(sums, "expert", swap)])
        returned = [both] + [
            lax.ppermute(both, "expert", [(moved(i, d, 0), i) for i in range(groups)])
            for d in range(1, LINE)
        ]
    else:
        sums = sums.reshape(held, groups, capacity).transpose(1, 0, 2).reshape(groups, -1)
        hidden_grad = hidden_grad.reshape(held, groups, capacity, units).transpose(1, 0, 2, 3)
        returned = lax.all_to_all(sums, "expert", split_axis=0, concat_axis=0, tiled=True)
        returned = [returned.reshape(-1, 128)]
    prob_grad = call(
        functools.partial(prob_kernel, direct, capacity),
        sds((chosen, tokens), F32),
        flat,
        probs,
        *returned,
        keep=False,
    ).T
    for c in range(max(0, count - 2), count):
        finished(c)
    weight_grad = state["grad"]
    return (hidden_grad.reshape(hidden.shape), prob_grad, weight_grad)


def solution(mesh):
    in_specs = (
        P(("dp", "expert"), None),
        P(("dp", "expert"), None),
        P(("dp", "expert"), None),
        P("dp", None, "expert", None, None),
        P("expert", None, None),
    )
    out_specs = (
        P("dp", None, "expert", None, None),
        P(("dp", "expert"), None),
        P("dp", "expert", None),
    )
    return jax.shard_map(body, mesh=mesh, in_specs=in_specs, out_specs=out_specs, check_vma=False)
```

```python
import functools

import jax
import jax.numpy as jnp
from jax import lax
from jax.experimental import pallas as pl
from jax.experimental.pallas import tpu as pltpu
from jax.sharding import PartitionSpec as P

F32, BF16, I32 = jnp.float32, jnp.bfloat16, jnp.int32
VMEM = pl.BlockSpec(memory_space=pltpu.VMEM)
ANY = pl.BlockSpec(memory_space=pl.ANY)
HBM = pl.BlockSpec(memory_space=pltpu.HBM)

LINE, SIDES = 4, 2
BACK = (0, 1, 3, 2)
INFO = 16


def moved(me, places, side):
    return (me // SIDES + places) % LINE * SIDES + (me % SIDES ^ side)


def source_of(me, part):
    return moved(me, LINE - BACK[part % LINE], part // LINE)


class Chain:
    def __init__(self):
        self.last = None

    def __call__(self, kernel, outs, *args, in_specs=None, keep=True, after=(), room=24, **kw):
        in_specs = list(in_specs or [VMEM] * len(args))
        count = len(args)
        body = kernel
        unread = [*after] if self.last is None else [self.last, *after]
        if unread:
            args, in_specs = (*args, *unread), in_specs + [ANY] * len(unread)

            def body(*refs):
                kernel(*refs[:count], *refs[count + len(unread) :])

        made = pl.pallas_call(
            body,
            out_shape=outs,
            in_specs=in_specs,
            compiler_params=pltpu.CompilerParams(vmem_limit_bytes=room * 1024 * 1024),
            cost_estimate=pl.CostEstimate(flops=1, bytes_accessed=1, transcendentals=0),
            **kw,
        )(*args)
        if keep:
            self.last = min(jax.tree.leaves(made), key=lambda x: x.size)
        return made


def gates_of(probs):
    total = jnp.sum(probs, axis=0, keepdims=True)
    gates = probs / total
    return total, gates, gates.astype(BF16).astype(F32)


def slots_of(ids, experts):
    chosen, tokens = ids.shape
    expert = lax.broadcasted_iota(I32, (experts, tokens), 0)
    named = [ids[k : k + 1] == expert for k in range(chosen)]
    hits = functools.reduce(jnp.add, [n.astype(F32) for n in named]).astype(BF16)
    row = lax.broadcasted_iota(I32, (tokens, tokens), 0)
    earlier = (row < lax.broadcasted_iota(I32, (tokens, tokens), 1)).astype(F32).astype(BF16)
    before = jnp.dot(hits, earlier, preferred_element_type=F32)
    return [jnp.sum(jnp.where(n, before, 0.0), axis=0, keepdims=True) for n in named]


def begin_kernel(experts, capacity, ids_ref, probs_ref, rows_ref, flat_ref, out_ref, *scratch):
    ids_got, probs_got, sems = scratch
    chosen, tokens = ids_got.shape
    width = out_ref.shape[1]
    copies = [
        pltpu.make_async_copy(ids_ref, ids_got, sems.at[0]),
        pltpu.make_async_copy(probs_ref, probs_got, sems.at[1]),
        pltpu.make_async_copy(rows_ref.at[:, :width], out_ref.at[:tokens], sems.at[2]),
    ]
    for copy in copies:
        copy.start()
    for copy in copies:
        copy.wait()
    ids = ids_got[...]
    _, _, word = gates_of(probs_got[...])
    slots = slots_of(ids, experts)
    for k in range(chosen):
        flat_ref[k : k + 1, :] = ids[k : k + 1] * capacity + slots[k].astype(I32)
    rest = jnp.zeros((INFO - 3 * chosen, tokens), F32)
    info = jnp.concatenate([ids.astype(F32), *slots, word, rest], axis=0).astype(BF16)
    out_ref[tokens:, :tokens] = info
    if width > tokens:
        out_ref[tokens:, tokens:] = jnp.zeros((INFO, width - tokens), BF16)


def places(held, capacity, chosen, ref, place_ref):
    tokens = place_ref.shape[1]
    rows = held * capacity
    me = lax.axis_index("expert")
    local = lax.broadcasted_iota(I32, (rows, tokens), 0)
    info = ref[tokens:, :tokens].astype(F32)
    flat = (info[:chosen] * capacity + info[chosen : 2 * chosen]).astype(I32)
    word = info[2 * chosen : 3 * chosen]
    for side in range(SIDES):
        slot = local + (me ^ side) * rows
        hits = [jnp.where(flat[k : k + 1] == slot, word[k : k + 1], 0.0) for k in range(chosen)]
        place_ref[side * rows : (side + 1) * rows, :] = functools.reduce(jnp.add, hits).astype(BF16)


def pick(held, capacity, block_refs, place_ref, out_refs):
    tokens = place_ref.shape[2]
    for j, ref in enumerate(block_refs):
        scaled = jnp.dot(place_ref[j], ref[:tokens, :], preferred_element_type=F32).astype(BF16)
        for side, out_ref in enumerate(out_refs):
            for e in range(held):
                at = (side * held + e) * capacity
                out_ref[e, j * capacity : (j + 1) * capacity, :] = scaled[at : at + capacity]


def pick_kernel(held, capacity, chosen, first, count, *refs):
    block_refs, refs = refs[:count], refs[count:]
    if first:
        mine_ref, other_ref, place_ref = refs
        for j, ref in enumerate(block_refs):
            places(held, capacity, chosen, ref, place_ref.at[j])
    else:
        place_ref, mine_ref, other_ref = refs
    pick(held, capacity, block_refs, place_ref, (mine_ref, other_ref))


def turn_kernel(dp, hidden_ref, *refs):
    out_ref, refs = refs[-1], refs[:-1]
    parts, held, _, units = hidden_ref.shape
    share, across = units // dp, dp // 2
    me = lax.axis_index("expert") if parts > 1 else 0
    mine = lax.axis_index("dp")
    core, row = mine % 2, mine // 2
    for e in range(held):
        sources = [source_of(me, p) if parts > 1 else 0 for p in range(parts)]
        stacked = jnp.concatenate([hidden_ref[source, e] for source in sources], axis=0)
        turned = stacked.T
        for piece in range(dp):
            other = (piece % 2) ^ core
            step = (piece // 2 - row + across) % across
            out_ref[e, other, step] = turned[piece * share : (piece + 1) * share]


def cut_kernel(start, rows_ref, *refs):
    out_refs, sems = refs[:-1], refs[-1]
    copies = []
    for i, ref in enumerate(out_refs):
        at = slice(start, start + ref.shape[1])
        copies.append(pltpu.make_async_copy(rows_ref.at[:, at], ref, sems.at[i]))
        start += ref.shape[1]
    for copy in copies:
        copy.start()
    for copy in copies:
        copy.wait()


def stacked_rows(refs, e):
    return refs[0][e] if len(refs) == 1 else jnp.concatenate([ref[e] for ref in refs], axis=0)


def term_kernel(turned_ref, *refs):
    part_refs, keep_ref, give_ref = refs[:-2], refs[-2], refs[-1]
    held, _, across, share, slots = turned_ref.shape
    for e in range(held):
        scaled = stacked_rows(part_refs, e)
        for other, ref in ((1, give_ref), (0, keep_ref)):
            left = turned_ref[e, other].reshape(across * share, slots)
            term = jnp.dot(left, scaled, preferred_element_type=F32).astype(BF16)
            for step in range(across):
                ref[step, e] = term[step * share : (step + 1) * share]


def pair_kernel(cuts, keep_ref, got_ref, *out_refs):
    out_refs = iter(out_refs)
    for step in range(1, keep_ref.shape[0]):
        start = 0
        for rows in cuts:
            at = slice(start, start + rows)
            pair = keep_ref[step, :, at].astype(F32) + got_ref[step, :, at].astype(F32)
            next(out_refs)[...] = pair.astype(BF16)
            start += rows


def last_kernel(cuts, start, keep_ref, got_ref, *refs):
    out_ref, mark_ref, total_ref, sem = refs[-4:]
    mark_ref[...] = jnp.zeros(mark_ref.shape, F32)
    others = len(cuts) * (keep_ref.shape[0] - 1)
    for e in range(keep_ref.shape[1]):
        row = 0
        for part, rows in enumerate(cuts):
            at = slice(row, row + rows)
            total = keep_ref[0, e, at].astype(F32) + got_ref[0, e, at].astype(F32)
            for ref in refs[part : others : len(cuts)]:
                total = total + ref[e].astype(F32)
            total_ref[at, e, :] = total
            row += rows
    copy = pltpu.make_async_copy(
        total_ref, out_ref.at[:, :, start : start + total_ref.shape[2]], sem
    )
    copy.start()
    copy.wait()


def raw_kernel(parts, start, final, weight_ref, *refs):
    part_refs, refs = refs[:parts], refs[parts:]
    if start:
        acc_ref, refs = refs[0], refs[1:]
    width = part_refs[0].shape[2]
    for e in range(weight_ref.shape[0]):
        raw = lax.dot_general(
            stacked_rows(part_refs, e),
            weight_ref[e, :, start : start + width],
            (((1,), (1,)), ((), ())),
            preferred_element_type=F32,
        )
        if start:
            raw = raw + acc_ref[e]
        if not final:
            refs[0][e] = raw
            continue
        hidden_ref, grad_ref, sums_ref = refs
        sources, _, own, units = hidden_ref.shape
        me = lax.axis_index("expert") if sources > 1 else 0
        folds = []
        for part in range(sources):
            source = source_of(me, part) if sources > 1 else 0
            block = raw[part * own : (part + 1) * own]
            grad_ref[source, e] = block.astype(BF16)
            product = block * hidden_ref[source, e].astype(F32)
            folds.append(
                functools.reduce(jnp.add, [product[:, i : i + 128] for i in range(0, units, 128)])
            )
        folded = jnp.concatenate(folds, axis=0) if len(folds) > 1 else folds[0]
        sums_ref[e : e + 1, :] = jnp.sum(folded.T, axis=0, keepdims=True)


def prob_kernel(direct, capacity, flat_ref, probs_ref, *refs):
    out_ref = refs[-1]
    chosen, tokens = flat_ref.shape
    if direct:
        values = []
        for q in range(LINE * SIDES):
            at = (BACK.index(q // SIDES) + LINE * (q % SIDES)) * capacity
            ref = refs[q // SIDES]
            values += [ref[q % SIDES, e : e + 1, at : at + capacity] for e in range(ref.shape[1])]
        lanes = 128 // capacity
        values = jnp.concatenate(
            [
                jnp.concatenate([v.reshape(1, capacity) for v in values[i : i + lanes]], axis=1)
                for i in range(0, len(values), lanes)
            ],
            axis=0,
        )
        me = lax.axis_index("expert")
    else:
        values = refs[0][...]
        me = 0
    lines = values.shape[0]
    spare = jnp.zeros((-lines % 8, 128), F32)
    columns = jnp.concatenate([values, spare], axis=0).T if spare.size else values.T
    total, gates, word = gates_of(probs_ref[...])
    group = lines * 128 // (LINE * SIDES)
    picked = [jnp.zeros((1, tokens), F32) for _ in range(chosen)]
    for line in range(lines):
        at = lax.broadcasted_iota(I32, (128, tokens), 0) + line * 128
        q = at // group
        slot = (moved(me, q // SIDES, q % SIDES) if direct else q) * group + at % group
        for k in range(chosen):
            hit = jnp.where(flat_ref[k : k + 1, :] == slot, columns[:, line : line + 1], 0.0)
            picked[k] += jnp.sum(hit, axis=0, keepdims=True)
    picked = [picked[k] / word[k : k + 1] for k in range(chosen)]
    mixed = functools.reduce(jnp.add, [gates[k : k + 1] * picked[k] for k in range(chosen)])
    for k in range(chosen):
        out_ref[k : k + 1, :] = (picked[k] - mixed) / total


def chunks_of(features):
    unit = features // 16
    return [6 * unit, 8 * unit, 2 * unit]


def cuts_of(share, c):
    first = 16 * (share // 32)
    return [first, share - first] if c == 0 else [share]


sds = jax.ShapeDtypeStruct


class Relay:
    def __init__(self, call, grad_out, ids, probs, held, capacity, widths):
        tokens, features = grad_out.shape
        self.call, self.held, self.capacity, self.widths = call, held, capacity, widths
        self.tokens, self.chosen, self.place = tokens, ids.shape[0], {}
        self.flat, first = call(
            functools.partial(begin_kernel, LINE * SIDES * held, capacity),
            [sds(ids.shape, I32), sds((tokens + INFO, widths[0]), BF16)],
            ids,
            probs,
            grad_out,
            in_specs=[HBM] * 3,
            scratch_shapes=[
                pltpu.VMEM(ids.shape, I32),
                pltpu.VMEM(probs.shape, F32),
                pltpu.SemaphoreType.DMA((3,)),
            ],
            room=60,
            keep=False,
        )
        rest = call(
            functools.partial(cut_kernel, widths[0]),
            [sds((tokens, w), BF16) for w in widths[1:]],
            grad_out,
            in_specs=[HBM],
            scratch_shapes=[pltpu.SemaphoreType.DMA((len(widths) - 1,))],
            keep=False,
        )
        self.blocks, self.passed = [], []
        for own in [first, *rest]:
            on, back = self.along(own, 1), self.along(own, LINE - 1)
            self.blocks.append([own, on, back])
            self.passed.append(self.along(on, 1))

    def along(self, block, places):
        pairs = [(i, moved(i, places, 0)) for i in range(LINE * SIDES)]
        return lax.ppermute(block, "expert", pairs)

    def pick(self, c, name, blocks):
        held, capacity, count = self.held, self.capacity, len(blocks)
        rows = [sds((held, count * capacity, self.widths[c]), BF16)] * SIDES
        kernel = functools.partial(pick_kernel, held, capacity, self.chosen, c == 0, count)
        if c == 0:
            place = sds((count, SIDES * held * capacity, self.tokens), BF16)
            mine, other, self.place[name] = self.call(kernel, [*rows, place], *blocks)
        else:
            mine, other = self.call(kernel, rows, *blocks, self.place[name])
        return mine, lax.ppermute(other, "expert", [(i, i ^ 1) for i in range(LINE * SIDES)])

    def early(self, c):
        return self.pick(c, "early", self.blocks[c])

    def late(self, c, early):
        late = self.pick(c, "late", [self.passed[c]])
        return [early[0], late[0], early[1], late[1]]


def exchanged(grad_out, ids, probs, groups, held, capacity, widths):
    tokens = grad_out.shape[0]
    experts = groups * held
    slots = experts * capacity
    _, _, word = gates_of(probs)
    flat = ids * capacity + jnp.concatenate(slots_of(ids, experts), axis=0).astype(I32)
    slot = lax.broadcasted_iota(I32, (slots, tokens), 0)
    place = sum(jnp.where(f == slot, w, 0.0) for f, w in zip(flat, word)).astype(BF16)
    arrived, start = [], 0
    for width in widths:
        rows = grad_out[:, start : start + width]
        sent = jnp.dot(place, rows, preferred_element_type=F32).astype(BF16)
        got = lax.all_to_all(
            sent.reshape(groups, held, capacity, width),
            "expert",
            split_axis=0,
            concat_axis=0,
            tiled=True,
        )
        arrived.append([got.transpose(1, 0, 2, 3).reshape(held, groups * capacity, width)])
        start += width
    return flat, arrived


def body(grad_out, route_ids, route_probs, hidden, w_down):
    groups = lax.axis_size("expert")
    dp = lax.axis_size("dp")
    held, units, features = w_down.shape
    capacity = hidden.shape[3]
    slots = groups * held * capacity
    per_expert = slots // held
    tokens, chosen = route_ids.shape
    share, across = units // dp, dp // 2
    direct = groups == LINE * SIDES
    widths = chunks_of(features)
    count = len(widths)

    ids, probs = route_ids.T, route_probs.T
    call = Chain()
    if direct:
        relay = Relay(call, grad_out, ids, probs, held, capacity, widths)
        flat, saved = relay.flat, hidden[0]
    else:
        flat, arrived = exchanged(grad_out, ids, probs, groups, held, capacity, widths)
        saved = hidden[0].transpose(1, 0, 2, 3).reshape(1, held, per_expert, units)
    turned = call(
        functools.partial(turn_kernel, dp),
        sds((held, 2, across, share, per_expert), BF16),
        saved,
    )
    starts = [sum(widths[:c]) for c in range(count)]
    state = {"raw": None, "grad": None}
    summed = []

    def accumulated(c):
        parts, width, final = arrived[c], widths[c], c == count - 1
        if final:
            outs = [sds(saved.shape, BF16), sds((held, per_expert), F32)]
        else:
            outs = [sds((held, per_expert, units), F32)]
        extra = ([state["raw"]] if c else []) + ([saved] if final else [])
        kernel = functools.partial(raw_kernel, len(parts), starts[c], final)
        made = call(
            kernel,
            outs,
            w_down,
            *parts,
            *extra,
        )
        state["raw"] = made if final else made[0]

    def reduced(c):
        parts, width = arrived[c], widths[c]
        piece = sds((across, held, share, width), BF16)
        after = summed[0][2][:1] if c == 1 else ()
        keep, give = call(term_kernel, [piece, piece], turned, *parts, after=after)
        got = lax.ppermute(give, "dp", [(i, i ^ 1) for i in range(dp)])
        if c == count - 1:
            accumulated(c)
        cuts = cuts_of(share, c)
        pieces = [sds((held, rows, width), BF16) for rows in cuts]
        pairs = call(functools.partial(pair_kernel, cuts), pieces * (across - 1), keep, got)
        others = []
        for i, pair in enumerate(pairs):
            step = 1 + i // len(cuts)
            shift = [(2 * r + k, 2 * ((r + step) % across) + k) for r in range(across) for k in range(2)]
            others.append(lax.ppermute(pair, "dp", shift))
        summed.append((keep, got, others))

    def finished(c):
        keep, got, others = summed[c]
        before = [] if state["grad"] is None else [state["grad"]]
        count = 2 + len(others)
        state["grad"], _ = call(
            functools.partial(last_kernel, cuts_of(share, c), starts[c]),
            [sds((share, held, features), F32), sds((8, 128), F32)],
            keep,
            got,
            *others,
            *before,
            in_specs=[VMEM] * count + [ANY] * len(before),
            out_specs=[ANY, VMEM],
            input_output_aliases={count: 0} if before else {},
            scratch_shapes=[
                pltpu.VMEM((share, held, widths[c]), F32),
                pltpu.SemaphoreType.DMA,
            ],
        )

    if direct:
        arrived = [relay.late(c, relay.early(c)) for c in range(2)]
    for c in range(count):
        if c >= 2:
            if direct:
                arrived.append(relay.late(c, relay.early(c)))
            accumulated(c - 1)
            finished(c - 2)
        reduced(c)
        if c == 1:
            accumulated(0)
    finished(count - 2)
    hidden_grad, sums = state["raw"]

    if direct:
        swap = [(i, i ^ 1) for i in range(groups)]
        both = jnp.stack([sums, lax.ppermute(sums, "expert", swap)])
        returned = [both] + [
            lax.ppermute(both, "expert", [(moved(i, d, 0), i) for i in range(groups)])
            for d in range(1, LINE)
        ]
    else:
        sums = sums.reshape(held, groups, capacity).transpose(1, 0, 2).reshape(groups, -1)
        hidden_grad = hidden_grad.reshape(held, groups, capacity, units).transpose(1, 0, 2, 3)
        returned = lax.all_to_all(sums, "expert", split_axis=0, concat_axis=0, tiled=True)
        returned = [returned.reshape(-1, 128)]
    prob_grad = call(
        functools.partial(prob_kernel, direct, capacity),
        sds((chosen, tokens), F32),
        flat,
        probs,
        *returned,
        keep=False,
    ).T
    finished(count - 1)
    weight_grad = state["grad"]
    return (hidden_grad.reshape(hidden.shape), prob_grad, weight_grad)


def solution(mesh):
    in_specs = (
        P(("dp", "expert"), None),
        P(("dp", "expert"), None),
        P(("dp", "expert"), None),
        P("dp", None, "expert", None, None),
        P("expert", None, None),
    )
    out_specs = (
        P("dp", None, "expert", None, None),
        P(("dp", "expert"), None),
        P("dp", "expert", None),
    )
    return jax.shard_map(body, mesh=mesh, in_specs=in_specs, out_specs=out_specs, check_vma=False)
```

```python
import functools

import jax
import jax.numpy as jnp
from jax import lax
from jax.experimental import pallas as pl
from jax.experimental.pallas import tpu as pltpu
from jax.sharding import PartitionSpec as P

F32, BF16, I32 = jnp.float32, jnp.bfloat16, jnp.int32
VMEM = pl.BlockSpec(memory_space=pltpu.VMEM)
ANY = pl.BlockSpec(memory_space=pl.ANY)
HBM = pl.BlockSpec(memory_space=pltpu.HBM)

LINE, SIDES = 4, 2
BACK = (0, 1, 3, 2)
INFO = 16


def moved(me, places, side):
    return (me // SIDES + places) % LINE * SIDES + (me % SIDES ^ side)


def source_of(me, part):
    return moved(me, LINE - BACK[part % LINE], part // LINE)


class Chain:
    def __init__(self):
        self.last = None

    def __call__(self, kernel, outs, *args, in_specs=None, keep=True, after=(), room=24, **kw):
        in_specs = list(in_specs or [VMEM] * len(args))
        count = len(args)
        body = kernel
        unread = [*after] if self.last is None else [self.last, *after]
        if unread:
            args, in_specs = (*args, *unread), in_specs + [ANY] * len(unread)

            def body(*refs):
                kernel(*refs[:count], *refs[count + len(unread) :])

        made = pl.pallas_call(
            body,
            out_shape=outs,
            in_specs=in_specs,
            compiler_params=pltpu.CompilerParams(vmem_limit_bytes=room * 1024 * 1024),
            cost_estimate=pl.CostEstimate(flops=1, bytes_accessed=1, transcendentals=0),
            **kw,
        )(*args)
        if keep:
            self.last = min(jax.tree.leaves(made), key=lambda x: x.size)
        return made


def gates_of(probs):
    total = jnp.sum(probs, axis=0, keepdims=True)
    gates = probs / total
    return total, gates, gates.astype(BF16).astype(F32)


def slots_of(ids, experts):
    chosen, tokens = ids.shape
    expert = lax.broadcasted_iota(I32, (experts, tokens), 0)
    named = [ids[k : k + 1] == expert for k in range(chosen)]
    hits = functools.reduce(jnp.add, [n.astype(F32) for n in named]).astype(BF16)
    row = lax.broadcasted_iota(I32, (tokens, tokens), 0)
    earlier = (row < lax.broadcasted_iota(I32, (tokens, tokens), 1)).astype(F32).astype(BF16)
    before = jnp.dot(hits, earlier, preferred_element_type=F32)
    return [jnp.sum(jnp.where(n, before, 0.0), axis=0, keepdims=True) for n in named]


def begin_kernel(experts, capacity, ids_ref, probs_ref, rows_ref, flat_ref, out_ref, *scratch):
    ids_got, probs_got, sems = scratch
    chosen, tokens = ids_got.shape
    width = out_ref.shape[1]
    copies = [
        pltpu.make_async_copy(ids_ref, ids_got, sems.at[0]),
        pltpu.make_async_copy(probs_ref, probs_got, sems.at[1]),
        pltpu.make_async_copy(rows_ref.at[:, :width], out_ref.at[:tokens], sems.at[2]),
    ]
    for copy in copies:
        copy.start()
    for copy in copies:
        copy.wait()
    ids = ids_got[...]
    _, _, word = gates_of(probs_got[...])
    slots = slots_of(ids, experts)
    for k in range(chosen):
        flat_ref[k : k + 1, :] = ids[k : k + 1] * capacity + slots[k].astype(I32)
    rest = jnp.zeros((INFO - 3 * chosen, tokens), F32)
    info = jnp.concatenate([ids.astype(F32), *slots, word, rest], axis=0).astype(BF16)
    out_ref[tokens:, :tokens] = info
    if width > tokens:
        out_ref[tokens:, tokens:] = jnp.zeros((INFO, width - tokens), BF16)


def places(held, capacity, chosen, ref, place_ref):
    tokens = place_ref.shape[1]
    rows = held * capacity
    me = lax.axis_index("expert")
    local = lax.broadcasted_iota(I32, (rows, tokens), 0)
    info = ref[tokens:, :tokens].astype(F32)
    flat = (info[:chosen] * capacity + info[chosen : 2 * chosen]).astype(I32)
    word = info[2 * chosen : 3 * chosen]
    for side in range(SIDES):
        slot = local + (me ^ side) * rows
        hits = [jnp.where(flat[k : k + 1] == slot, word[k : k + 1], 0.0) for k in range(chosen)]
        place_ref[side * rows : (side + 1) * rows, :] = functools.reduce(jnp.add, hits).astype(BF16)


def pick(held, capacity, block_refs, place_ref, out_refs):
    tokens = place_ref.shape[2]
    for j, ref in enumerate(block_refs):
        scaled = jnp.dot(place_ref[j], ref[:tokens, :], preferred_element_type=F32).astype(BF16)
        for side, out_ref in enumerate(out_refs):
            for e in range(held):
                at = (side * held + e) * capacity
                out_ref[e, j * capacity : (j + 1) * capacity, :] = scaled[at : at + capacity]


def pick_kernel(held, capacity, chosen, first, count, *refs):
    block_refs, refs = refs[:count], refs[count:]
    if first:
        mine_ref, other_ref, place_ref = refs
        for j, ref in enumerate(block_refs):
            places(held, capacity, chosen, ref, place_ref.at[j])
    else:
        place_ref, mine_ref, other_ref = refs
    pick(held, capacity, block_refs, place_ref, (mine_ref, other_ref))


def turn_kernel(dp, hidden_ref, *refs):
    out_ref, refs = refs[-1], refs[:-1]
    parts, held, _, units = hidden_ref.shape
    share, across = units // dp, dp // 2
    me = lax.axis_index("expert") if parts > 1 else 0
    mine = lax.axis_index("dp")
    core, row = mine % 2, mine // 2
    for e in range(held):
        sources = [source_of(me, p) if parts > 1 else 0 for p in range(parts)]
        stacked = jnp.concatenate([hidden_ref[source, e] for source in sources], axis=0)
        turned = stacked.T
        for piece in range(dp):
            other = (piece % 2) ^ core
            step = (piece // 2 - row + across) % across
            out_ref[e, other, step] = turned[piece * share : (piece + 1) * share]


def cut_kernel(start, rows_ref, *refs):
    out_refs, sems = refs[:-1], refs[-1]
    copies = []
    for i, ref in enumerate(out_refs):
        at = slice(start, start + ref.shape[1])
        copies.append(pltpu.make_async_copy(rows_ref.at[:, at], ref, sems.at[i]))
        start += ref.shape[1]
    for copy in copies:
        copy.start()
    for copy in copies:
        copy.wait()


def stacked_rows(refs, e):
    return refs[0][e] if len(refs) == 1 else jnp.concatenate([ref[e] for ref in refs], axis=0)


def term_kernel(turned_ref, *refs):
    part_refs, keep_ref, give_ref = refs[:-2], refs[-2], refs[-1]
    held, _, across, share, slots = turned_ref.shape
    for e in range(held):
        scaled = stacked_rows(part_refs, e)
        for other, ref in ((1, give_ref), (0, keep_ref)):
            left = turned_ref[e, other].reshape(across * share, slots)
            term = jnp.dot(left, scaled, preferred_element_type=F32).astype(BF16)
            for step in range(across):
                ref[step, e] = term[step * share : (step + 1) * share]


def pair_kernel(keep_ref, got_ref, *out_refs):
    for step, ref in enumerate(out_refs, 1):
        ref[...] = (keep_ref[step].astype(F32) + got_ref[step].astype(F32)).astype(BF16)


def last_kernel(chunks, start, *refs):
    out_ref, mark_ref, total_ref, sem = refs[-4:]
    mark_ref[...] = jnp.zeros(mark_ref.shape, F32)
    across, held = refs[0].shape[:2]
    column = 0
    for chunk in range(chunks):
        keep_ref, got_ref, *other_refs = refs[chunk * (across + 1) : (chunk + 1) * (across + 1)]
        at = slice(column, column + keep_ref.shape[3])
        column = at.stop
        for e in range(held):
            total = keep_ref[0, e].astype(F32) + got_ref[0, e].astype(F32)
            for ref in other_refs:
                total = total + ref[e].astype(F32)
            total_ref[:, e, at] = total
    copy = pltpu.make_async_copy(
        total_ref, out_ref.at[:, :, start : start + total_ref.shape[2]], sem
    )
    copy.start()
    copy.wait()


def raw_kernel(parts, start, final, weight_ref, *refs):
    part_refs, refs = refs[:parts], refs[parts:]
    if start:
        acc_ref, refs = refs[0], refs[1:]
    width = part_refs[0].shape[2]
    for e in range(weight_ref.shape[0]):
        raw = lax.dot_general(
            stacked_rows(part_refs, e),
            weight_ref[e, :, start : start + width],
            (((1,), (1,)), ((), ())),
            preferred_element_type=F32,
        )
        if start:
            raw = raw + acc_ref[e]
        if not final:
            refs[0][e] = raw
            continue
        hidden_ref, grad_ref, sums_ref = refs
        sources, _, own, units = hidden_ref.shape
        me = lax.axis_index("expert") if sources > 1 else 0
        folds = []
        for part in range(sources):
            source = source_of(me, part) if sources > 1 else 0
            block = raw[part * own : (part + 1) * own]
            grad_ref[source, e] = block.astype(BF16)
            product = block * hidden_ref[source, e].astype(F32)
            folds.append(
                functools.reduce(jnp.add, [product[:, i : i + 128] for i in range(0, units, 128)])
            )
        folded = jnp.concatenate(folds, axis=0) if len(folds) > 1 else folds[0]
        sums_ref[e : e + 1, :] = jnp.sum(folded.T, axis=0, keepdims=True)


def prob_kernel(direct, capacity, flat_ref, probs_ref, *refs):
    out_ref = refs[-1]
    chosen, tokens = flat_ref.shape
    if direct:
        values = []
        for q in range(LINE * SIDES):
            at = (BACK.index(q // SIDES) + LINE * (q % SIDES)) * capacity
            ref = refs[q // SIDES]
            values += [ref[q % SIDES, e : e + 1, at : at + capacity] for e in range(ref.shape[1])]
        lanes = 128 // capacity
        values = jnp.concatenate(
            [
                jnp.concatenate([v.reshape(1, capacity) for v in values[i : i + lanes]], axis=1)
                for i in range(0, len(values), lanes)
            ],
            axis=0,
        )
        me = lax.axis_index("expert")
    else:
        values = refs[0][...]
        me = 0
    lines = values.shape[0]
    spare = jnp.zeros((-lines % 8, 128), F32)
    columns = jnp.concatenate([values, spare], axis=0).T if spare.size else values.T
    total, gates, word = gates_of(probs_ref[...])
    group = lines * 128 // (LINE * SIDES)
    picked = [jnp.zeros((1, tokens), F32) for _ in range(chosen)]
    for line in range(lines):
        at = lax.broadcasted_iota(I32, (128, tokens), 0) + line * 128
        q = at // group
        slot = (moved(me, q // SIDES, q % SIDES) if direct else q) * group + at % group
        for k in range(chosen):
            hit = jnp.where(flat_ref[k : k + 1, :] == slot, columns[:, line : line + 1], 0.0)
            picked[k] += jnp.sum(hit, axis=0, keepdims=True)
    picked = [picked[k] / word[k : k + 1] for k in range(chosen)]
    mixed = functools.reduce(jnp.add, [gates[k : k + 1] * picked[k] for k in range(chosen)])
    for k in range(chosen):
        out_ref[k : k + 1, :] = (picked[k] - mixed) / total


def chunks_of(features):
    unit = features // 16
    return [5 * unit, 8 * unit, 3 * unit]


sds = jax.ShapeDtypeStruct


class Relay:
    def __init__(self, call, grad_out, ids, probs, held, capacity, widths):
        tokens, features = grad_out.shape
        self.call, self.held, self.capacity, self.widths = call, held, capacity, widths
        self.tokens, self.chosen, self.place = tokens, ids.shape[0], {}
        self.flat, first = call(
            functools.partial(begin_kernel, LINE * SIDES * held, capacity),
            [sds(ids.shape, I32), sds((tokens + INFO, widths[0]), BF16)],
            ids,
            probs,
            grad_out,
            in_specs=[HBM] * 3,
            scratch_shapes=[
                pltpu.VMEM(ids.shape, I32),
                pltpu.VMEM(probs.shape, F32),
                pltpu.SemaphoreType.DMA((3,)),
            ],
            room=60,
            keep=False,
        )
        rest = call(
            functools.partial(cut_kernel, widths[0]),
            [sds((tokens, w), BF16) for w in widths[1:]],
            grad_out,
            in_specs=[HBM],
            scratch_shapes=[pltpu.SemaphoreType.DMA((len(widths) - 1,))],
            keep=False,
        )
        self.blocks, self.passed = [], []
        for own in [first, *rest]:
            on, back = self.along(own, 1), self.along(own, LINE - 1)
            self.blocks.append([own, on, back])
            self.passed.append(self.along(on, 1))

    def along(self, block, places):
        pairs = [(i, moved(i, places, 0)) for i in range(LINE * SIDES)]
        return lax.ppermute(block, "expert", pairs)

    def pick(self, c, name, blocks):
        held, capacity, count = self.held, self.capacity, len(blocks)
        rows = [sds((held, count * capacity, self.widths[c]), BF16)] * SIDES
        kernel = functools.partial(pick_kernel, held, capacity, self.chosen, c == 0, count)
        if c == 0:
            place = sds((count, SIDES * held * capacity, self.tokens), BF16)
            mine, other, self.place[name] = self.call(kernel, [*rows, place], *blocks)
        else:
            mine, other = self.call(kernel, rows, *blocks, self.place[name])
        return mine, lax.ppermute(other, "expert", [(i, i ^ 1) for i in range(LINE * SIDES)])

    def early(self, c):
        return self.pick(c, "early", self.blocks[c])

    def late(self, c, early):
        late = self.pick(c, "late", [self.passed[c]])
        return [early[0], late[0], early[1], late[1]]


def exchanged(grad_out, ids, probs, groups, held, capacity, widths):
    tokens = grad_out.shape[0]
    experts = groups * held
    slots = experts * capacity
    _, _, word = gates_of(probs)
    flat = ids * capacity + jnp.concatenate(slots_of(ids, experts), axis=0).astype(I32)
    slot = lax.broadcasted_iota(I32, (slots, tokens), 0)
    place = sum(jnp.where(f == slot, w, 0.0) for f, w in zip(flat, word)).astype(BF16)
    arrived, start = [], 0
    for width in widths:
        rows = grad_out[:, start : start + width]
        sent = jnp.dot(place, rows, preferred_element_type=F32).astype(BF16)
        got = lax.all_to_all(
            sent.reshape(groups, held, capacity, width),
            "expert",
            split_axis=0,
            concat_axis=0,
            tiled=True,
        )
        arrived.append([got.transpose(1, 0, 2, 3).reshape(held, groups * capacity, width)])
        start += width
    return flat, arrived


def body(grad_out, route_ids, route_probs, hidden, w_down):
    groups = lax.axis_size("expert")
    dp = lax.axis_size("dp")
    held, units, features = w_down.shape
    capacity = hidden.shape[3]
    slots = groups * held * capacity
    per_expert = slots // held
    tokens, chosen = route_ids.shape
    share, across = units // dp, dp // 2
    direct = groups == LINE * SIDES
    widths = chunks_of(features)
    count = len(widths)

    ids, probs = route_ids.T, route_probs.T
    call = Chain()
    if direct:
        relay = Relay(call, grad_out, ids, probs, held, capacity, widths)
        flat, saved = relay.flat, hidden[0]
    else:
        flat, arrived = exchanged(grad_out, ids, probs, groups, held, capacity, widths)
        saved = hidden[0].transpose(1, 0, 2, 3).reshape(1, held, per_expert, units)
    turned = call(
        functools.partial(turn_kernel, dp),
        sds((held, 2, across, share, per_expert), BF16),
        saved,
    )
    starts = [sum(widths[:c]) for c in range(count)]
    state = {"raw": None, "grad": None}
    summed = []

    def accumulated(c):
        parts, width, final = arrived[c], widths[c], c == count - 1
        if final:
            outs = [sds(saved.shape, BF16), sds((held, per_expert), F32)]
        else:
            outs = [sds((held, per_expert, units), F32)]
        extra = ([state["raw"]] if c else []) + ([saved] if final else [])
        kernel = functools.partial(raw_kernel, len(parts), starts[c], final)
        made = call(
            kernel,
            outs,
            w_down,
            *parts,
            *extra,
        )
        state["raw"] = made if final else made[0]

    def reduced(c):
        parts, width = arrived[c], widths[c]
        piece = sds((across, held, share, width), BF16)
        after = summed[-1][2][:1] if c else ()
        keep, give = call(term_kernel, [piece, piece], turned, *parts, after=after)
        got = lax.ppermute(give, "dp", [(i, i ^ 1) for i in range(dp)])
        if c == count - 1:
            accumulated(c)
        pairs = call(pair_kernel, [sds((held, share, width), BF16)] * (across - 1), keep, got)
        others = []
        for step, pair in enumerate(pairs, 1):
            shift = [(2 * r + k, 2 * ((r + step) % across) + k) for r in range(across) for k in range(2)]
            others.append(lax.ppermute(pair, "dp", shift))
        summed.append((keep, got, others))

    def finished(chunks):
        before = [] if state["grad"] is None else [state["grad"]]
        args = [x for c in chunks for x in (*summed[c][:2], *summed[c][2])]
        state["grad"], _ = call(
            functools.partial(last_kernel, len(chunks), starts[chunks[0]]),
            [sds((share, held, features), F32), sds((8, 128), F32)],
            *args,
            *before,
            in_specs=[VMEM] * len(args) + [ANY] * len(before),
            out_specs=[ANY, VMEM],
            input_output_aliases={len(args): 0} if before else {},
            scratch_shapes=[
                pltpu.VMEM((share, held, sum(widths[c] for c in chunks)), F32),
                pltpu.SemaphoreType.DMA,
            ],
        )

    if direct:
        arrived, early = [], relay.early(0)
    for c in range(count):
        if direct:
            arrived.append(relay.late(c, early))
            if c == 0:
                early = relay.early(1)
        if c >= 1:
            accumulated(c - 1)
        reduced(c)
        if direct and 1 <= c < count - 1:
            early = relay.early(c + 1)
        if 1 <= c < count - 1:
            finished([c - 1])
    hidden_grad, sums = state["raw"]

    if direct:
        swap = [(i, i ^ 1) for i in range(groups)]
        both = jnp.stack([sums, lax.ppermute(sums, "expert", swap)])
        returned = [both] + [
            lax.ppermute(both, "expert", [(moved(i, d, 0), i) for i in range(groups)])
            for d in range(1, LINE)
        ]
    else:
        sums = sums.reshape(held, groups, capacity).transpose(1, 0, 2).reshape(groups, -1)
        hidden_grad = hidden_grad.reshape(held, groups, capacity, units).transpose(1, 0, 2, 3)
        returned = lax.all_to_all(sums, "expert", split_axis=0, concat_axis=0, tiled=True)
        returned = [returned.reshape(-1, 128)]
    prob_grad = call(
        functools.partial(prob_kernel, direct, capacity),
        sds((chosen, tokens), F32),
        flat,
        probs,
        *returned,
        keep=False,
    ).T
    finished([count - 2, count - 1])
    weight_grad = state["grad"]
    return (hidden_grad.reshape(hidden.shape), prob_grad, weight_grad)


def solution(mesh):
    in_specs = (
        P(("dp", "expert"), None),
        P(("dp", "expert"), None),
        P(("dp", "expert"), None),
        P("dp", None, "expert", None, None),
        P("expert", None, None),
    )
    out_specs = (
        P("dp", None, "expert", None, None),
        P(("dp", "expert"), None),
        P("dp", "expert", None),
    )
    return jax.shard_map(body, mesh=mesh, in_specs=in_specs, out_specs=out_specs, check_vma=False)
```

```python
import functools

import jax
import jax.numpy as jnp
from jax import lax
from jax.experimental import pallas as pl
from jax.experimental.pallas import tpu as pltpu
from jax.sharding import PartitionSpec as P

F32, BF16, I32 = jnp.float32, jnp.bfloat16, jnp.int32
VMEM = pl.BlockSpec(memory_space=pltpu.VMEM)
ANY = pl.BlockSpec(memory_space=pl.ANY)
HBM = pl.BlockSpec(memory_space=pltpu.HBM)

LINE, SIDES = 4, 2
BACK = (0, 1, 3, 2)
INFO = 16


def moved(me, places, side):
    return (me // SIDES + places) % LINE * SIDES + (me % SIDES ^ side)


def source_of(me, part):
    return moved(me, LINE - BACK[part % LINE], part // LINE)


class Chain:
    def __init__(self):
        self.last = None

    def __call__(self, kernel, outs, *args, in_specs=None, keep=True, after=(), room=24, **kw):
        in_specs = list(in_specs or [VMEM] * len(args))
        count = len(args)
        body = kernel
        unread = [*after] if self.last is None else [self.last, *after]
        if unread:
            args, in_specs = (*args, *unread), in_specs + [ANY] * len(unread)

            def body(*refs):
                kernel(*refs[:count], *refs[count + len(unread) :])

        made = pl.pallas_call(
            body,
            out_shape=outs,
            in_specs=in_specs,
            compiler_params=pltpu.CompilerParams(vmem_limit_bytes=room * 1024 * 1024),
            cost_estimate=pl.CostEstimate(flops=1, bytes_accessed=1, transcendentals=0),
            **kw,
        )(*args)
        if keep:
            self.last = min(jax.tree.leaves(made), key=lambda x: x.size)
        return made


def gates_of(probs):
    total = jnp.sum(probs, axis=0, keepdims=True)
    gates = probs / total
    return total, gates, gates.astype(BF16).astype(F32)


def slots_of(ids, experts):
    chosen, tokens = ids.shape
    expert = lax.broadcasted_iota(I32, (experts, tokens), 0)
    named = [ids[k : k + 1] == expert for k in range(chosen)]
    hits = functools.reduce(jnp.add, [n.astype(F32) for n in named]).astype(BF16)
    row = lax.broadcasted_iota(I32, (tokens, tokens), 0)
    earlier = (row < lax.broadcasted_iota(I32, (tokens, tokens), 1)).astype(F32).astype(BF16)
    before = jnp.dot(hits, earlier, preferred_element_type=F32)
    return [jnp.sum(jnp.where(n, before, 0.0), axis=0, keepdims=True) for n in named]


def begin_kernel(experts, capacity, ids_ref, probs_ref, rows_ref, flat_ref, out_ref, *scratch):
    ids_got, probs_got, sems = scratch
    chosen, tokens = ids_got.shape
    width = out_ref.shape[1]
    copies = [
        pltpu.make_async_copy(ids_ref, ids_got, sems.at[0]),
        pltpu.make_async_copy(probs_ref, probs_got, sems.at[1]),
        pltpu.make_async_copy(rows_ref.at[:, :width], out_ref.at[:tokens], sems.at[2]),
    ]
    for copy in copies:
        copy.start()
    for copy in copies:
        copy.wait()
    ids = ids_got[...]
    _, _, word = gates_of(probs_got[...])
    slots = slots_of(ids, experts)
    for k in range(chosen):
        flat_ref[k : k + 1, :] = ids[k : k + 1] * capacity + slots[k].astype(I32)
    rest = jnp.zeros((INFO - 3 * chosen, tokens), F32)
    info = jnp.concatenate([ids.astype(F32), *slots, word, rest], axis=0).astype(BF16)
    out_ref[tokens:, :tokens] = info
    if width > tokens:
        out_ref[tokens:, tokens:] = jnp.zeros((INFO, width - tokens), BF16)


def places(held, capacity, chosen, ref, place_ref):
    tokens = place_ref.shape[1]
    rows = held * capacity
    me = lax.axis_index("expert")
    local = lax.broadcasted_iota(I32, (rows, tokens), 0)
    info = ref[tokens:, :tokens].astype(F32)
    flat = (info[:chosen] * capacity + info[chosen : 2 * chosen]).astype(I32)
    word = info[2 * chosen : 3 * chosen]
    for side in range(SIDES):
        slot = local + (me ^ side) * rows
        hits = [jnp.where(flat[k : k + 1] == slot, word[k : k + 1], 0.0) for k in range(chosen)]
        place_ref[side * rows : (side + 1) * rows, :] = functools.reduce(jnp.add, hits).astype(BF16)


def pick(held, capacity, block_refs, place_ref, out_refs):
    tokens = place_ref.shape[2]
    for j, ref in enumerate(block_refs):
        scaled = jnp.dot(place_ref[j], ref[:tokens, :], preferred_element_type=F32).astype(BF16)
        for side, out_ref in enumerate(out_refs):
            for e in range(held):
                at = (side * held + e) * capacity
                out_ref[e, j * capacity : (j + 1) * capacity, :] = scaled[at : at + capacity]


def pick_kernel(held, capacity, chosen, first, count, *refs):
    block_refs, refs = refs[:count], refs[count:]
    if first:
        mine_ref, other_ref, place_ref = refs
        for j, ref in enumerate(block_refs):
            places(held, capacity, chosen, ref, place_ref.at[j])
    else:
        place_ref, mine_ref, other_ref = refs
    pick(held, capacity, block_refs, place_ref, (mine_ref, other_ref))


def turn_kernel(dp, hidden_ref, *refs):
    out_ref, refs = refs[-1], refs[:-1]
    parts, held, _, units = hidden_ref.shape
    share, across = units // dp, dp // 2
    me = lax.axis_index("expert") if parts > 1 else 0
    mine = lax.axis_index("dp")
    core, row = mine % 2, mine // 2
    for e in range(held):
        sources = [source_of(me, p) if parts > 1 else 0 for p in range(parts)]
        stacked = jnp.concatenate([hidden_ref[source, e] for source in sources], axis=0)
        turned = stacked.T
        for piece in range(dp):
            other = (piece % 2) ^ core
            step = (piece // 2 - row + across) % across
            out_ref[e, other, step] = turned[piece * share : (piece + 1) * share]


def cut_kernel(start, rows_ref, *refs):
    out_refs, sems = refs[:-1], refs[-1]
    copies = []
    for i, ref in enumerate(out_refs):
        at = slice(start, start + ref.shape[1])
        copies.append(pltpu.make_async_copy(rows_ref.at[:, at], ref, sems.at[i]))
        start += ref.shape[1]
    for copy in copies:
        copy.start()
    for copy in copies:
        copy.wait()


def stacked_rows(refs, e, at):
    rows = [ref[e, :, at] for ref in refs]
    return rows[0] if len(rows) == 1 else jnp.concatenate(rows, axis=0)


def term_kernel(start, turned_ref, *refs):
    part_refs, keep_ref, give_ref = refs[:-2], refs[-2], refs[-1]
    held, _, across, share, slots = turned_ref.shape
    at = slice(start, start + keep_ref.shape[3])
    for e in range(held):
        scaled = stacked_rows(part_refs, e, at)
        for other, ref in ((1, give_ref), (0, keep_ref)):
            left = turned_ref[e, other].reshape(across * share, slots)
            term = jnp.dot(left, scaled, preferred_element_type=F32).astype(BF16)
            for step in range(across):
                ref[step, e] = term[step * share : (step + 1) * share]


def pair_kernel(cuts, keep_ref, got_ref, *out_refs):
    out_refs = iter(out_refs)
    for step in range(1, keep_ref.shape[0]):
        start = 0
        for rows in cuts:
            at = slice(start, start + rows)
            pair = keep_ref[step, :, at].astype(F32) + got_ref[step, :, at].astype(F32)
            next(out_refs)[...] = pair.astype(BF16)
            start += rows


def last_kernel(cuts, start, *refs):
    out_ref, mark_ref, total_ref, sem = refs[-4:]
    mark_ref[...] = jnp.zeros(mark_ref.shape, F32)
    column = 0
    for rows_of in cuts:
        keep_ref, got_ref, *refs = refs
        across, held, _, width = keep_ref.shape
        others, refs = refs[: len(rows_of) * (across - 1)], refs[len(rows_of) * (across - 1) :]
        columns = slice(column, column + width)
        column += width
        for e in range(held):
            row = 0
            for cut, rows in enumerate(rows_of):
                at = slice(row, row + rows)
                total = keep_ref[0, e, at].astype(F32) + got_ref[0, e, at].astype(F32)
                for ref in others[cut :: len(rows_of)]:
                    total = total + ref[e].astype(F32)
                total_ref[at, e, columns] = total
                row += rows
    copy = pltpu.make_async_copy(
        total_ref, out_ref.at[:, :, start : start + total_ref.shape[2]], sem
    )
    copy.start()
    copy.wait()


def raw_kernel(parts, start, final, weight_ref, *refs):
    part_refs, refs = refs[:parts], refs[parts:]
    if start:
        acc_ref, refs = refs[0], refs[1:]
    width = part_refs[0].shape[2]
    for e in range(weight_ref.shape[0]):
        raw = lax.dot_general(
            stacked_rows(part_refs, e, slice(None)),
            weight_ref[e, :, start : start + width],
            (((1,), (1,)), ((), ())),
            preferred_element_type=F32,
        )
        if start:
            raw = raw + acc_ref[e]
        if not final:
            refs[0][e] = raw
            continue
        hidden_ref, grad_ref, sums_ref = refs
        sources, _, own, units = hidden_ref.shape
        me = lax.axis_index("expert") if sources > 1 else 0
        folds = []
        for part in range(sources):
            source = source_of(me, part) if sources > 1 else 0
            block = raw[part * own : (part + 1) * own]
            grad_ref[source, e] = block.astype(BF16)
            product = block * hidden_ref[source, e].astype(F32)
            folds.append(
                functools.reduce(jnp.add, [product[:, i : i + 128] for i in range(0, units, 128)])
            )
        folded = jnp.concatenate(folds, axis=0) if len(folds) > 1 else folds[0]
        sums_ref[e : e + 1, :] = jnp.sum(folded.T, axis=0, keepdims=True)


def prob_kernel(direct, capacity, flat_ref, probs_ref, *refs):
    out_ref = refs[-1]
    chosen, tokens = flat_ref.shape
    if direct:
        values = []
        for q in range(LINE * SIDES):
            at = (BACK.index(q // SIDES) + LINE * (q % SIDES)) * capacity
            ref = refs[q // SIDES]
            values += [ref[q % SIDES, e : e + 1, at : at + capacity] for e in range(ref.shape[1])]
        lanes = 128 // capacity
        values = jnp.concatenate(
            [
                jnp.concatenate([v.reshape(1, capacity) for v in values[i : i + lanes]], axis=1)
                for i in range(0, len(values), lanes)
            ],
            axis=0,
        )
        me = lax.axis_index("expert")
    else:
        values = refs[0][...]
        me = 0
    lines = values.shape[0]
    spare = jnp.zeros((-lines % 8, 128), F32)
    columns = jnp.concatenate([values, spare], axis=0).T if spare.size else values.T
    total, gates, word = gates_of(probs_ref[...])
    group = lines * 128 // (LINE * SIDES)
    picked = [jnp.zeros((1, tokens), F32) for _ in range(chosen)]
    for line in range(lines):
        at = lax.broadcasted_iota(I32, (128, tokens), 0) + line * 128
        q = at // group
        slot = (moved(me, q // SIDES, q % SIDES) if direct else q) * group + at % group
        for k in range(chosen):
            hit = jnp.where(flat_ref[k : k + 1, :] == slot, columns[:, line : line + 1], 0.0)
            picked[k] += jnp.sum(hit, axis=0, keepdims=True)
    picked = [picked[k] / word[k : k + 1] for k in range(chosen)]
    mixed = functools.reduce(jnp.add, [gates[k : k + 1] * picked[k] for k in range(chosen)])
    for k in range(chosen):
        out_ref[k : k + 1, :] = (picked[k] - mixed) / total


def chunks_of(features):
    unit = features // 16
    return [[7 * unit], [5 * unit, 4 * unit]]


def cuts_of(share, first):
    return [share // 3] * 3 if first else [share]


sds = jax.ShapeDtypeStruct


class Relay:
    def __init__(self, call, grad_out, ids, probs, held, capacity, widths):
        tokens, features = grad_out.shape
        self.call, self.held, self.capacity, self.widths = call, held, capacity, widths
        self.tokens, self.chosen, self.place = tokens, ids.shape[0], {}
        self.flat, first = call(
            functools.partial(begin_kernel, LINE * SIDES * held, capacity),
            [sds(ids.shape, I32), sds((tokens + INFO, widths[0]), BF16)],
            ids,
            probs,
            grad_out,
            in_specs=[HBM] * 3,
            scratch_shapes=[
                pltpu.VMEM(ids.shape, I32),
                pltpu.VMEM(probs.shape, F32),
                pltpu.SemaphoreType.DMA((3,)),
            ],
            room=60,
            keep=False,
        )
        rest = call(
            functools.partial(cut_kernel, widths[0]),
            [sds((tokens, w), BF16) for w in widths[1:]],
            grad_out,
            in_specs=[HBM],
            scratch_shapes=[pltpu.SemaphoreType.DMA((len(widths) - 1,))],
            keep=False,
        )
        self.blocks, self.passed = [], []
        for own in [first, *rest]:
            on, back = self.along(own, 1), self.along(own, LINE - 1)
            self.blocks.append([own, on, back])
            self.passed.append(self.along(on, 1))

    def along(self, block, places):
        pairs = [(i, moved(i, places, 0)) for i in range(LINE * SIDES)]
        return lax.ppermute(block, "expert", pairs)

    def pick(self, c, name, blocks):
        held, capacity, count = self.held, self.capacity, len(blocks)
        rows = [sds((held, count * capacity, self.widths[c]), BF16)] * SIDES
        kernel = functools.partial(pick_kernel, held, capacity, self.chosen, c == 0, count)
        if c == 0:
            place = sds((count, SIDES * held * capacity, self.tokens), BF16)
            mine, other, self.place[name] = self.call(kernel, [*rows, place], *blocks)
        else:
            mine, other = self.call(kernel, rows, *blocks, self.place[name])
        return mine, lax.ppermute(other, "expert", [(i, i ^ 1) for i in range(LINE * SIDES)])

    def early(self, c):
        return self.pick(c, "early", self.blocks[c])

    def late(self, c, early):
        late = self.pick(c, "late", [self.passed[c]])
        return [early[0], late[0], early[1], late[1]]


def exchanged(grad_out, ids, probs, groups, held, capacity, widths):
    tokens = grad_out.shape[0]
    experts = groups * held
    slots = experts * capacity
    _, _, word = gates_of(probs)
    flat = ids * capacity + jnp.concatenate(slots_of(ids, experts), axis=0).astype(I32)
    slot = lax.broadcasted_iota(I32, (slots, tokens), 0)
    place = sum(jnp.where(f == slot, w, 0.0) for f, w in zip(flat, word)).astype(BF16)
    arrived, start = [], 0
    for width in widths:
        rows = grad_out[:, start : start + width]
        sent = jnp.dot(place, rows, preferred_element_type=F32).astype(BF16)
        got = lax.all_to_all(
            sent.reshape(groups, held, capacity, width),
            "expert",
            split_axis=0,
            concat_axis=0,
            tiled=True,
        )
        arrived.append([got.transpose(1, 0, 2, 3).reshape(held, groups * capacity, width)])
        start += width
    return flat, arrived


def body(grad_out, route_ids, route_probs, hidden, w_down):
    groups = lax.axis_size("expert")
    dp = lax.axis_size("dp")
    held, units, features = w_down.shape
    capacity = hidden.shape[3]
    slots = groups * held * capacity
    per_expert = slots // held
    tokens, chosen = route_ids.shape
    share, across = units // dp, dp // 2
    direct = groups == LINE * SIDES
    chunks = chunks_of(features)
    widths = [sum(chunk) for chunk in chunks]
    count = len(widths)

    ids, probs = route_ids.T, route_probs.T
    call = Chain()
    if direct:
        relay = Relay(call, grad_out, ids, probs, held, capacity, widths)
        flat, saved = relay.flat, hidden[0]
    else:
        flat, arrived = exchanged(grad_out, ids, probs, groups, held, capacity, widths)
        saved = hidden[0].transpose(1, 0, 2, 3).reshape(1, held, per_expert, units)
    turned = call(
        functools.partial(turn_kernel, dp),
        sds((held, 2, across, share, per_expert), BF16),
        saved,
    )
    starts = [sum(widths[:c]) for c in range(count)]
    state = {"raw": None, "grad": None}
    summed = []

    def accumulated(c):
        parts, width, final = arrived[c], widths[c], c == count - 1
        if final:
            outs = [sds(saved.shape, BF16), sds((held, per_expert), F32)]
        else:
            outs = [sds((held, per_expert, units), F32)]
        extra = ([state["raw"]] if c else []) + ([saved] if final else [])
        kernel = functools.partial(raw_kernel, len(parts), starts[c], final)
        made = call(
            kernel,
            outs,
            w_down,
            *parts,
            *extra,
        )
        state["raw"] = made if final else made[0]

    def reduced(c, at, width):
        piece = sds((across, held, share, width), BF16)
        after = summed[0][2][:2] if len(summed) == 1 else ()
        kernel = functools.partial(term_kernel, at)
        keep, give = call(kernel, [piece, piece], turned, *arrived[c], after=after)
        got = lax.ppermute(give, "dp", [(i, i ^ 1) for i in range(dp)])
        if c == count - 1 and at == 0:
            accumulated(c)
        cuts = cuts_of(share, not summed)
        pieces = [sds((held, rows, width), BF16) for rows in cuts]
        pairs = call(functools.partial(pair_kernel, cuts), pieces * (across - 1), keep, got)
        others = []
        for i, pair in enumerate(pairs):
            step = 1 + i // len(cuts)
            shift = [(2 * r + k, 2 * ((r + step) % across) + k) for r in range(across) for k in range(2)]
            others.append(lax.ppermute(pair, "dp", shift))
        summed.append((keep, got, others, starts[c] + at))

    def finished(first, last):
        before = [] if state["grad"] is None else [state["grad"]]
        done = summed[first:last]
        args = [x for keep, got, others, _ in done for x in (keep, got, *others)]
        cuts = [cuts_of(share, j == 0) for j in range(first, last)]
        state["grad"], _ = call(
            functools.partial(last_kernel, cuts, done[0][3]),
            [sds((share, held, features), F32), sds((8, 128), F32)],
            *args,
            *before,
            in_specs=[VMEM] * len(args) + [ANY] * len(before),
            out_specs=[ANY, VMEM],
            input_output_aliases={len(args): 0} if before else {},
            scratch_shapes=[
                pltpu.VMEM((share, held, sum(keep.shape[3] for keep, *_ in done)), F32),
                pltpu.SemaphoreType.DMA,
            ],
        )

    if direct:
        arrived, early = [], relay.early(0)
    for c, chunk in enumerate(chunks):
        if direct:
            arrived.append(relay.late(c, early))
            if c + 1 < count:
                early = relay.early(c + 1)
        if c >= 1:
            accumulated(c - 1)
        at = 0
        for width in chunk:
            reduced(c, at, width)
            at += width
            if len(summed) > 1:
                finished(len(summed) - 2, len(summed) - 1)
    hidden_grad, sums = state["raw"]

    if direct:
        swap = [(i, i ^ 1) for i in range(groups)]
        both = jnp.stack([sums, lax.ppermute(sums, "expert", swap)])
        returned = [both] + [
            lax.ppermute(both, "expert", [(moved(i, d, 0), i) for i in range(groups)])
            for d in range(1, LINE)
        ]
    else:
        sums = sums.reshape(held, groups, capacity).transpose(1, 0, 2).reshape(groups, -1)
        hidden_grad = hidden_grad.reshape(held, groups, capacity, units).transpose(1, 0, 2, 3)
        returned = lax.all_to_all(sums, "expert", split_axis=0, concat_axis=0, tiled=True)
        returned = [returned.reshape(-1, 128)]
    prob_grad = call(
        functools.partial(prob_kernel, direct, capacity),
        sds((chosen, tokens), F32),
        flat,
        probs,
        *returned,
        keep=False,
    ).T
    finished(len(summed) - 1, len(summed))
    weight_grad = state["grad"]
    return (hidden_grad.reshape(hidden.shape), prob_grad, weight_grad)


def solution(mesh):
    in_specs = (
        P(("dp", "expert"), None),
        P(("dp", "expert"), None),
        P(("dp", "expert"), None),
        P("dp", None, "expert", None, None),
        P("expert", None, None),
    )
    out_specs = (
        P("dp", None, "expert", None, None),
        P(("dp", "expert"), None),
        P("dp", "expert", None),
    )
    return jax.shard_map(body, mesh=mesh, in_specs=in_specs, out_specs=out_specs, check_vma=False)
```

```python
import functools

import jax
import jax.numpy as jnp
from jax import lax
from jax.experimental import pallas as pl
from jax.experimental.pallas import tpu as pltpu
from jax.sharding import PartitionSpec as P

F32, BF16, I32 = jnp.float32, jnp.bfloat16, jnp.int32
VMEM = pl.BlockSpec(memory_space=pltpu.VMEM)
ANY = pl.BlockSpec(memory_space=pl.ANY)
HBM = pl.BlockSpec(memory_space=pltpu.HBM)

LINE, SIDES = 4, 2
BACK = (0, 1, 3, 2)
INFO = 16


def moved(me, places, side):
    return (me // SIDES + places) % LINE * SIDES + (me % SIDES ^ side)


def source_of(me, part):
    return moved(me, LINE - BACK[part % LINE], part // LINE)


class Chain:
    def __init__(self):
        self.last = None

    def __call__(self, kernel, outs, *args, in_specs=None, keep=True, after=(), room=24, **kw):
        in_specs = list(in_specs or [VMEM] * len(args))
        count = len(args)
        body = kernel
        unread = [*after] if self.last is None else [self.last, *after]
        if unread:
            args, in_specs = (*args, *unread), in_specs + [ANY] * len(unread)

            def body(*refs):
                kernel(*refs[:count], *refs[count + len(unread) :])

        made = pl.pallas_call(
            body,
            out_shape=outs,
            in_specs=in_specs,
            compiler_params=pltpu.CompilerParams(vmem_limit_bytes=room * 1024 * 1024),
            cost_estimate=pl.CostEstimate(flops=1, bytes_accessed=1, transcendentals=0),
            **kw,
        )(*args)
        if keep:
            self.last = min(jax.tree.leaves(made), key=lambda x: x.size)
        return made


def gates_of(probs):
    total = jnp.sum(probs, axis=0, keepdims=True)
    gates = probs / total
    return total, gates, gates.astype(BF16).astype(F32)


def slots_of(ids, experts):
    chosen, tokens = ids.shape
    expert = lax.broadcasted_iota(I32, (experts, tokens), 0)
    named = [ids[k : k + 1] == expert for k in range(chosen)]
    hits = functools.reduce(jnp.add, [n.astype(F32) for n in named]).astype(BF16)
    row = lax.broadcasted_iota(I32, (tokens, tokens), 0)
    earlier = (row < lax.broadcasted_iota(I32, (tokens, tokens), 1)).astype(F32).astype(BF16)
    before = jnp.dot(hits, earlier, preferred_element_type=F32)
    return [jnp.sum(jnp.where(n, before, 0.0), axis=0, keepdims=True) for n in named]


def begin_kernel(experts, capacity, ids_ref, probs_ref, rows_ref, flat_ref, out_ref, *scratch):
    ids_got, probs_got, sems = scratch
    chosen, tokens = ids_got.shape
    width = out_ref.shape[1]
    copies = [
        pltpu.make_async_copy(ids_ref, ids_got, sems.at[0]),
        pltpu.make_async_copy(probs_ref, probs_got, sems.at[1]),
        pltpu.make_async_copy(rows_ref.at[:, :width], out_ref.at[:tokens], sems.at[2]),
    ]
    for copy in copies:
        copy.start()
    for copy in copies:
        copy.wait()
    ids = ids_got[...]
    _, _, word = gates_of(probs_got[...])
    slots = slots_of(ids, experts)
    for k in range(chosen):
        flat_ref[k : k + 1, :] = ids[k : k + 1] * capacity + slots[k].astype(I32)
    rest = jnp.zeros((INFO - 3 * chosen, tokens), F32)
    info = jnp.concatenate([ids.astype(F32), *slots, word, rest], axis=0).astype(BF16)
    out_ref[tokens:, :tokens] = info
    if width > tokens:
        out_ref[tokens:, tokens:] = jnp.zeros((INFO, width - tokens), BF16)


def places(held, capacity, chosen, ref, place_ref):
    tokens = place_ref.shape[1]
    rows = held * capacity
    me = lax.axis_index("expert")
    local = lax.broadcasted_iota(I32, (rows, tokens), 0)
    info = ref[tokens:, :tokens].astype(F32)
    flat = (info[:chosen] * capacity + info[chosen : 2 * chosen]).astype(I32)
    word = info[2 * chosen : 3 * chosen]
    for side in range(SIDES):
        slot = local + (me ^ side) * rows
        hits = [jnp.where(flat[k : k + 1] == slot, word[k : k + 1], 0.0) for k in range(chosen)]
        place_ref[side * rows : (side + 1) * rows, :] = functools.reduce(jnp.add, hits).astype(BF16)


def pick(held, capacity, begin, block_refs, place_ref, out_refs):
    tokens = place_ref.shape[2]
    for j, ref in enumerate(block_refs):
        scaled = jnp.dot(place_ref[begin + j], ref[:tokens, :], preferred_element_type=F32).astype(BF16)
        for side, out_ref in enumerate(out_refs):
            for e in range(held):
                at = (side * held + e) * capacity
                out_ref[e, j * capacity : (j + 1) * capacity, :] = scaled[at : at + capacity]


def pick_kernel(held, capacity, chosen, first, at, count, *refs):
    block_refs, refs = refs[:count], refs[count:]
    if first:
        mine_ref, other_ref, place_ref = refs
        for j, ref in enumerate(block_refs):
            places(held, capacity, chosen, ref, place_ref.at[j])
    else:
        place_ref, mine_ref, other_ref = refs
    pick(held, capacity, at, block_refs, place_ref, (mine_ref, other_ref))


def turn_kernel(dp, hidden_ref, *refs):
    out_ref, refs = refs[-1], refs[:-1]
    parts, held, _, units = hidden_ref.shape
    share, across = units // dp, dp // 2
    me = lax.axis_index("expert") if parts > 1 else 0
    mine = lax.axis_index("dp")
    core, row = mine % 2, mine // 2
    for e in range(held):
        sources = [source_of(me, p) if parts > 1 else 0 for p in range(parts)]
        stacked = jnp.concatenate([hidden_ref[source, e] for source in sources], axis=0)
        turned = stacked.T
        for piece in range(dp):
            other = (piece % 2) ^ core
            step = (piece // 2 - row + across) % across
            out_ref[e, other, step] = turned[piece * share : (piece + 1) * share]


def cut_kernel(start, rows_ref, *refs):
    out_refs, sems = refs[:-1], refs[-1]
    copies = []
    for i, ref in enumerate(out_refs):
        at = slice(start, start + ref.shape[1])
        copies.append(pltpu.make_async_copy(rows_ref.at[:, at], ref, sems.at[i]))
        start += ref.shape[1]
    for copy in copies:
        copy.start()
    for copy in copies:
        copy.wait()


def stacked_rows(refs, e, at):
    rows = [ref[e, :, at] for ref in refs]
    return rows[0] if len(rows) == 1 else jnp.concatenate(rows, axis=0)


def term_kernel(start, turned_ref, *refs):
    part_refs, keep_ref, give_ref = refs[:-2], refs[-2], refs[-1]
    held, _, across, share, slots = turned_ref.shape
    at = slice(start, start + keep_ref.shape[3])
    for e in range(held):
        scaled = stacked_rows(part_refs, e, at)
        for other, ref in ((1, give_ref), (0, keep_ref)):
            left = turned_ref[e, other].reshape(across * share, slots)
            term = jnp.dot(left, scaled, preferred_element_type=F32).astype(BF16)
            for step in range(across):
                ref[step, e] = term[step * share : (step + 1) * share]


def pair_kernel(cuts, keep_ref, got_ref, *out_refs):
    out_refs = iter(out_refs)
    for step in range(1, keep_ref.shape[0]):
        start = 0
        for rows in cuts:
            at = slice(start, start + rows)
            pair = keep_ref[step, :, at].astype(F32) + got_ref[step, :, at].astype(F32)
            next(out_refs)[...] = pair.astype(BF16)
            start += rows


def last_kernel(cuts, start, *refs):
    out_ref, mark_ref, total_ref, sem = refs[-4:]
    mark_ref[...] = jnp.zeros(mark_ref.shape, F32)
    column = 0
    for rows_of in cuts:
        keep_ref, got_ref, *refs = refs
        across, held, _, width = keep_ref.shape
        others, refs = refs[: len(rows_of) * (across - 1)], refs[len(rows_of) * (across - 1) :]
        columns = slice(column, column + width)
        column += width
        for e in range(held):
            row = 0
            for cut, rows in enumerate(rows_of):
                at = slice(row, row + rows)
                total = keep_ref[0, e, at].astype(F32) + got_ref[0, e, at].astype(F32)
                for ref in others[cut :: len(rows_of)]:
                    total = total + ref[e].astype(F32)
                total_ref[at, e, columns] = total
                row += rows
    copy = pltpu.make_async_copy(
        total_ref, out_ref.at[:, :, start : start + total_ref.shape[2]], sem
    )
    copy.start()
    copy.wait()


def raw_kernel(parts, start, final, weight_ref, *refs):
    part_refs, refs = refs[:parts], refs[parts:]
    if start:
        acc_ref, refs = refs[0], refs[1:]
    width = part_refs[0].shape[2]
    for e in range(weight_ref.shape[0]):
        raw = lax.dot_general(
            stacked_rows(part_refs, e, slice(None)),
            weight_ref[e, :, start : start + width],
            (((1,), (1,)), ((), ())),
            preferred_element_type=F32,
        )
        if start:
            raw = raw + acc_ref[e]
        if not final:
            refs[0][e] = raw
            continue
        hidden_ref, grad_ref, sums_ref = refs
        sources, _, own, units = hidden_ref.shape
        me = lax.axis_index("expert") if sources > 1 else 0
        folds = []
        for part in range(sources):
            source = source_of(me, part) if sources > 1 else 0
            block = raw[part * own : (part + 1) * own]
            grad_ref[source, e] = block.astype(BF16)
            product = block * hidden_ref[source, e].astype(F32)
            folds.append(
                functools.reduce(jnp.add, [product[:, i : i + 128] for i in range(0, units, 128)])
            )
        folded = jnp.concatenate(folds, axis=0) if len(folds) > 1 else folds[0]
        sums_ref[e : e + 1, :] = jnp.sum(folded.T, axis=0, keepdims=True)


def prob_kernel(direct, capacity, flat_ref, probs_ref, *refs):
    out_ref = refs[-1]
    chosen, tokens = flat_ref.shape
    if direct:
        values = []
        for q in range(LINE * SIDES):
            at = (BACK.index(q // SIDES) + LINE * (q % SIDES)) * capacity
            ref = refs[q // SIDES]
            values += [ref[q % SIDES, e : e + 1, at : at + capacity] for e in range(ref.shape[1])]
        lanes = 128 // capacity
        values = jnp.concatenate(
            [
                jnp.concatenate([v.reshape(1, capacity) for v in values[i : i + lanes]], axis=1)
                for i in range(0, len(values), lanes)
            ],
            axis=0,
        )
        me = lax.axis_index("expert")
    else:
        values = refs[0][...]
        me = 0
    lines = values.shape[0]
    spare = jnp.zeros((-lines % 8, 128), F32)
    columns = jnp.concatenate([values, spare], axis=0).T if spare.size else values.T
    total, gates, word = gates_of(probs_ref[...])
    group = lines * 128 // (LINE * SIDES)
    picked = [jnp.zeros((1, tokens), F32) for _ in range(chosen)]
    for line in range(lines):
        at = lax.broadcasted_iota(I32, (128, tokens), 0) + line * 128
        q = at // group
        slot = (moved(me, q // SIDES, q % SIDES) if direct else q) * group + at % group
        for k in range(chosen):
            hit = jnp.where(flat_ref[k : k + 1, :] == slot, columns[:, line : line + 1], 0.0)
            picked[k] += jnp.sum(hit, axis=0, keepdims=True)
    picked = [picked[k] / word[k : k + 1] for k in range(chosen)]
    mixed = functools.reduce(jnp.add, [gates[k : k + 1] * picked[k] for k in range(chosen)])
    for k in range(chosen):
        out_ref[k : k + 1, :] = (picked[k] - mixed) / total


def chunks_of(features):
    unit = features // 16
    return [[7 * unit], [5 * unit, 4 * unit]]


def cuts_of(share, first):
    return [share // 3] * 3 if first else [share]


sds = jax.ShapeDtypeStruct


class Relay:
    def __init__(self, call, grad_out, ids, probs, held, capacity, widths):
        tokens, features = grad_out.shape
        self.call, self.held, self.capacity, self.widths = call, held, capacity, widths
        self.tokens, self.chosen, self.place = tokens, ids.shape[0], {}
        self.flat, first = call(
            functools.partial(begin_kernel, LINE * SIDES * held, capacity),
            [sds(ids.shape, I32), sds((tokens + INFO, widths[0]), BF16)],
            ids,
            probs,
            grad_out,
            in_specs=[HBM] * 3,
            scratch_shapes=[
                pltpu.VMEM(ids.shape, I32),
                pltpu.VMEM(probs.shape, F32),
                pltpu.SemaphoreType.DMA((3,)),
            ],
            room=60,
            keep=False,
        )
        rest = call(
            functools.partial(cut_kernel, widths[0]),
            [sds((tokens, w), BF16) for w in widths[1:]],
            grad_out,
            in_specs=[HBM],
            scratch_shapes=[pltpu.SemaphoreType.DMA((len(widths) - 1,))],
            keep=False,
        )
        self.blocks, self.passed = [], []
        for own in [first, *rest]:
            on, back = self.along(own, 1), self.along(own, LINE - 1)
            self.blocks.append([own, on, back])
            self.passed.append(self.along(on, 1))

    def along(self, block, places):
        pairs = [(i, moved(i, places, 0)) for i in range(LINE * SIDES)]
        return lax.ppermute(block, "expert", pairs)

    def pick(self, c, name, blocks, at=0):
        held, capacity, count = self.held, self.capacity, len(blocks)
        rows = [sds((held, count * capacity, self.widths[c]), BF16)] * SIDES
        kernel = functools.partial(pick_kernel, held, capacity, self.chosen, c == 0, at, count)
        if c == 0:
            place = sds((count, SIDES * held * capacity, self.tokens), BF16)
            mine, other, self.place[name] = self.call(kernel, [*rows, place], *blocks)
        else:
            mine, other = self.call(kernel, rows, *blocks, self.place[name])
        return mine, lax.ppermute(other, "expert", [(i, i ^ 1) for i in range(LINE * SIDES)])

    def early(self, c):
        if c == 0:
            return [self.pick(c, "early", self.blocks[c])]
        own = self.pick(c, "early", self.blocks[c][:1])
        return [own, self.pick(c, "early", self.blocks[c][1:], 1)]

    def late(self, c, early):
        picked = [*early, self.pick(c, "late", [self.passed[c]])]
        return [mine for mine, _ in picked] + [other for _, other in picked]


def exchanged(grad_out, ids, probs, groups, held, capacity, widths):
    tokens = grad_out.shape[0]
    experts = groups * held
    slots = experts * capacity
    _, _, word = gates_of(probs)
    flat = ids * capacity + jnp.concatenate(slots_of(ids, experts), axis=0).astype(I32)
    slot = lax.broadcasted_iota(I32, (slots, tokens), 0)
    place = sum(jnp.where(f == slot, w, 0.0) for f, w in zip(flat, word)).astype(BF16)
    arrived, start = [], 0
    for width in widths:
        rows = grad_out[:, start : start + width]
        sent = jnp.dot(place, rows, preferred_element_type=F32).astype(BF16)
        got = lax.all_to_all(
            sent.reshape(groups, held, capacity, width),
            "expert",
            split_axis=0,
            concat_axis=0,
            tiled=True,
        )
        arrived.append([got.transpose(1, 0, 2, 3).reshape(held, groups * capacity, width)])
        start += width
    return flat, arrived


def body(grad_out, route_ids, route_probs, hidden, w_down):
    groups = lax.axis_size("expert")
    dp = lax.axis_size("dp")
    held, units, features = w_down.shape
    capacity = hidden.shape[3]
    slots = groups * held * capacity
    per_expert = slots // held
    tokens, chosen = route_ids.shape
    share, across = units // dp, dp // 2
    direct = groups == LINE * SIDES
    chunks = chunks_of(features)
    widths = [sum(chunk) for chunk in chunks]
    count = len(widths)

    ids, probs = route_ids.T, route_probs.T
    call = Chain()
    if direct:
        relay = Relay(call, grad_out, ids, probs, held, capacity, widths)
        flat, saved = relay.flat, hidden[0]
    else:
        flat, arrived = exchanged(grad_out, ids, probs, groups, held, capacity, widths)
        saved = hidden[0].transpose(1, 0, 2, 3).reshape(1, held, per_expert, units)
    turned = call(
        functools.partial(turn_kernel, dp),
        sds((held, 2, across, share, per_expert), BF16),
        saved,
    )
    starts = [sum(widths[:c]) for c in range(count)]
    state = {"raw": None, "grad": None}
    summed = []

    def accumulated(c):
        parts, width, final = arrived[c], widths[c], c == count - 1
        if final:
            outs = [sds(saved.shape, BF16), sds((held, per_expert), F32)]
        else:
            outs = [sds((held, per_expert, units), F32)]
        extra = ([state["raw"]] if c else []) + ([saved] if final else [])
        kernel = functools.partial(raw_kernel, len(parts), starts[c], final)
        made = call(
            kernel,
            outs,
            w_down,
            *parts,
            *extra,
        )
        state["raw"] = made if final else made[0]

    def termed(c, at, width):
        piece = sds((across, held, share, width), BF16)
        after = summed[0][2][:2] if summed and at == 0 else ()
        if direct and not c:
            after = [early[0][1]]
        kernel = functools.partial(term_kernel, at)
        keep, give = call(kernel, [piece, piece], turned, *arrived[c], after=after)
        got = lax.ppermute(give, "dp", [(i, i ^ 1) for i in range(dp)])
        return keep, got, starts[c] + at

    def paired(keep, got, start):
        cuts = cuts_of(share, not summed)
        pieces = [sds((held, rows, keep.shape[3]), BF16) for rows in cuts]
        pairs = call(functools.partial(pair_kernel, cuts), pieces * (across - 1), keep, got)
        others = []
        for i, pair in enumerate(pairs):
            step = 1 + i // len(cuts)
            shift = [(2 * r + k, 2 * ((r + step) % across) + k) for r in range(across) for k in range(2)]
            others.append(lax.ppermute(pair, "dp", shift))
        summed.append((keep, got, others, start))

    def finished(first, last):
        before = [] if state["grad"] is None else [state["grad"]]
        done = summed[first:last]
        args = [x for keep, got, others, _ in done for x in (keep, got, *others)]
        cuts = [cuts_of(share, j == 0) for j in range(first, last)]
        state["grad"], _ = call(
            functools.partial(last_kernel, cuts, done[0][3]),
            [sds((share, held, features), F32), sds((8, 128), F32)],
            *args,
            *before,
            in_specs=[VMEM] * len(args) + [ANY] * len(before),
            out_specs=[ANY, VMEM],
            input_output_aliases={len(args): 0} if before else {},
            scratch_shapes=[
                pltpu.VMEM((share, held, sum(keep.shape[3] for keep, *_ in done)), F32),
                pltpu.SemaphoreType.DMA,
            ],
        )

    if direct:
        arrived, early = [], relay.early(0)
    for c, chunk in enumerate(chunks):
        if direct:
            arrived.append(relay.late(c, early))
            if c + 1 < count:
                early = relay.early(c + 1)
        if c >= 1:
            accumulated(c - 1)
        terms = [termed(c, sum(chunk[:i]), width) for i, width in enumerate(chunk)]
        if c == count - 1:
            accumulated(c)
        for term in terms:
            paired(*term)
    for j in range(1, len(summed)):
        finished(j, j + 1)
    hidden_grad, sums = state["raw"]

    if direct:
        swap = [(i, i ^ 1) for i in range(groups)]
        both = jnp.stack([sums, lax.ppermute(sums, "expert", swap)])
        returned = [both] + [
            lax.ppermute(both, "expert", [(moved(i, d, 0), i) for i in range(groups)])
            for d in range(1, LINE)
        ]
    else:
        sums = sums.reshape(held, groups, capacity).transpose(1, 0, 2).reshape(groups, -1)
        hidden_grad = hidden_grad.reshape(held, groups, capacity, units).transpose(1, 0, 2, 3)
        returned = lax.all_to_all(sums, "expert", split_axis=0, concat_axis=0, tiled=True)
        returned = [returned.reshape(-1, 128)]
    prob_grad = call(
        functools.partial(prob_kernel, direct, capacity),
        sds((chosen, tokens), F32),
        flat,
        probs,
        *returned,
    ).T
    finished(0, 1)
    weight_grad = state["grad"]
    return (hidden_grad.reshape(hidden.shape), prob_grad, weight_grad)


def solution(mesh):
    in_specs = (
        P(("dp", "expert"), None),
        P(("dp", "expert"), None),
        P(("dp", "expert"), None),
        P("dp", None, "expert", None, None),
        P("expert", None, None),
    )
    out_specs = (
        P("dp", None, "expert", None, None),
        P(("dp", "expert"), None),
        P("dp", "expert", None),
    )
    return jax.shard_map(body, mesh=mesh, in_specs=in_specs, out_specs=out_specs, check_vma=False)
```

```python
import functools

import jax
import jax.numpy as jnp
from jax import lax
from jax.experimental import pallas as pl
from jax.experimental.pallas import tpu as pltpu
from jax.sharding import PartitionSpec as P

F32, BF16, I32 = jnp.float32, jnp.bfloat16, jnp.int32
VMEM = pl.BlockSpec(memory_space=pltpu.VMEM)
ANY = pl.BlockSpec(memory_space=pl.ANY)
HBM = pl.BlockSpec(memory_space=pltpu.HBM)

LINE, SIDES = 4, 2
BACK = (0, 1, 3, 2)
INFO = 16


def moved(me, places, side):
    return (me // SIDES + places) % LINE * SIDES + (me % SIDES ^ side)


def source_of(me, part):
    return moved(me, LINE - BACK[part % LINE], part // LINE)


class Chain:
    def __init__(self):
        self.last = None

    def __call__(self, kernel, outs, *args, in_specs=None, keep=True, after=(), room=24, **kw):
        in_specs = list(in_specs or [VMEM] * len(args))
        count = len(args)
        body = kernel
        unread = [*after] if self.last is None else [self.last, *after]
        if unread:
            args, in_specs = (*args, *unread), in_specs + [ANY] * len(unread)

            def body(*refs):
                kernel(*refs[:count], *refs[count + len(unread) :])

        made = pl.pallas_call(
            body,
            out_shape=outs,
            in_specs=in_specs,
            compiler_params=pltpu.CompilerParams(vmem_limit_bytes=room * 1024 * 1024),
            cost_estimate=pl.CostEstimate(flops=1, bytes_accessed=1, transcendentals=0),
            **kw,
        )(*args)
        if keep:
            self.last = min(jax.tree.leaves(made), key=lambda x: x.size)
        return made


def gates_of(probs):
    total = jnp.sum(probs, axis=0, keepdims=True)
    gates = probs / total
    return total, gates, gates.astype(BF16).astype(F32)


def slots_of(ids, experts):
    chosen, tokens = ids.shape
    expert = lax.broadcasted_iota(I32, (experts, tokens), 0)
    named = [ids[k : k + 1] == expert for k in range(chosen)]
    hits = functools.reduce(jnp.add, [n.astype(F32) for n in named]).astype(BF16)
    row = lax.broadcasted_iota(I32, (tokens, tokens), 0)
    earlier = (row < lax.broadcasted_iota(I32, (tokens, tokens), 1)).astype(F32).astype(BF16)
    before = jnp.dot(hits, earlier, preferred_element_type=F32)
    return [jnp.sum(jnp.where(n, before, 0.0), axis=0, keepdims=True) for n in named]


def begin_kernel(experts, capacity, ids_ref, probs_ref, rows_ref, flat_ref, out_ref, *scratch):
    ids_got, probs_got, sems = scratch
    chosen, tokens = ids_got.shape
    width = out_ref.shape[1]
    copies = [
        pltpu.make_async_copy(ids_ref, ids_got, sems.at[0]),
        pltpu.make_async_copy(probs_ref, probs_got, sems.at[1]),
        pltpu.make_async_copy(rows_ref.at[:, :width], out_ref.at[:tokens], sems.at[2]),
    ]
    for copy in copies:
        copy.start()
    for copy in copies:
        copy.wait()
    ids = ids_got[...]
    _, _, word = gates_of(probs_got[...])
    slots = slots_of(ids, experts)
    for k in range(chosen):
        flat_ref[k : k + 1, :] = ids[k : k + 1] * capacity + slots[k].astype(I32)
    rest = jnp.zeros((INFO - 3 * chosen, tokens), F32)
    info = jnp.concatenate([ids.astype(F32), *slots, word, rest], axis=0).astype(BF16)
    out_ref[tokens:, :tokens] = info
    if width > tokens:
        out_ref[tokens:, tokens:] = jnp.zeros((INFO, width - tokens), BF16)


def places(held, capacity, chosen, ref, place_ref):
    tokens = place_ref.shape[1]
    rows = held * capacity
    me = lax.axis_index("expert")
    local = lax.broadcasted_iota(I32, (rows, tokens), 0)
    info = ref[tokens:, :tokens].astype(F32)
    flat = (info[:chosen] * capacity + info[chosen : 2 * chosen]).astype(I32)
    word = info[2 * chosen : 3 * chosen]
    for side in range(SIDES):
        slot = local + (me ^ side) * rows
        hits = [jnp.where(flat[k : k + 1] == slot, word[k : k + 1], 0.0) for k in range(chosen)]
        place_ref[side * rows : (side + 1) * rows, :] = functools.reduce(jnp.add, hits).astype(BF16)


def pick(held, capacity, begin, block_refs, place_ref, out_refs):
    tokens = place_ref.shape[2]
    for j, ref in enumerate(block_refs):
        scaled = jnp.dot(place_ref[begin + j], ref[:tokens, :], preferred_element_type=F32).astype(BF16)
        for side, out_ref in enumerate(out_refs):
            for e in range(held):
                at = (side * held + e) * capacity
                out_ref[e, j * capacity : (j + 1) * capacity, :] = scaled[at : at + capacity]


def pick_kernel(held, capacity, chosen, first, at, count, *refs):
    block_refs, refs = refs[:count], refs[count:]
    if first:
        mine_ref, other_ref, place_ref = refs
        for j, ref in enumerate(block_refs):
            places(held, capacity, chosen, ref, place_ref.at[j])
    else:
        place_ref, mine_ref, other_ref = refs
    pick(held, capacity, at, block_refs, place_ref, (mine_ref, other_ref))


def turn_kernel(dp, hidden_ref, *refs):
    out_ref, refs = refs[-1], refs[:-1]
    parts, held, _, units = hidden_ref.shape
    share, across = units // dp, dp // 2
    me = lax.axis_index("expert") if parts > 1 else 0
    mine = lax.axis_index("dp")
    core, row = mine % 2, mine // 2
    for e in range(held):
        sources = [source_of(me, p) if parts > 1 else 0 for p in range(parts)]
        stacked = jnp.concatenate([hidden_ref[source, e] for source in sources], axis=0)
        turned = stacked.T
        for piece in range(dp):
            other = (piece % 2) ^ core
            step = (piece // 2 - row + across) % across
            out_ref[e, other, step] = turned[piece * share : (piece + 1) * share]


def cut_kernel(start, rows_ref, *refs):
    out_refs, sems = refs[:-1], refs[-1]
    copies = []
    for i, ref in enumerate(out_refs):
        at = slice(start, start + ref.shape[1])
        copies.append(pltpu.make_async_copy(rows_ref.at[:, at], ref, sems.at[i]))
        start += ref.shape[1]
    for copy in copies:
        copy.start()
    for copy in copies:
        copy.wait()


def stacked_rows(refs, e, at):
    rows = [ref[e, :, at] for ref in refs]
    return rows[0] if len(rows) == 1 else jnp.concatenate(rows, axis=0)


def term_kernel(start, turned_ref, *refs):
    part_refs, keep_ref, give_ref = refs[:-2], refs[-2], refs[-1]
    held, _, across, share, slots = turned_ref.shape
    at = slice(start, start + keep_ref.shape[3])
    for e in range(held):
        scaled = stacked_rows(part_refs, e, at)
        for other, ref in ((1, give_ref), (0, keep_ref)):
            left = turned_ref[e, other].reshape(across * share, slots)
            term = jnp.dot(left, scaled, preferred_element_type=F32).astype(BF16)
            for step in range(across):
                ref[step, e] = term[step * share : (step + 1) * share]


def pair_kernel(cuts, keep_ref, got_ref, *out_refs):
    out_refs = iter(out_refs)
    for step in range(1, keep_ref.shape[0]):
        start = 0
        for rows in cuts:
            at = slice(start, start + rows)
            pair = keep_ref[step, :, at].astype(F32) + got_ref[step, :, at].astype(F32)
            next(out_refs)[...] = pair.astype(BF16)
            start += rows


def last_kernel(cuts, start, *refs):
    out_ref, mark_ref, total_ref, sem = refs[-4:]
    mark_ref[...] = jnp.zeros(mark_ref.shape, F32)
    column = 0
    for rows_of in cuts:
        keep_ref, got_ref, *refs = refs
        across, held, _, width = keep_ref.shape
        others, refs = refs[: len(rows_of) * (across - 1)], refs[len(rows_of) * (across - 1) :]
        columns = slice(column, column + width)
        column += width
        for e in range(held):
            row = 0
            for cut, rows in enumerate(rows_of):
                at = slice(row, row + rows)
                total = keep_ref[0, e, at].astype(F32) + got_ref[0, e, at].astype(F32)
                for ref in others[cut :: len(rows_of)]:
                    total = total + ref[e].astype(F32)
                total_ref[at, e, columns] = total
                row += rows
    copy = pltpu.make_async_copy(
        total_ref, out_ref.at[:, :, start : start + total_ref.shape[2]], sem
    )
    copy.start()
    copy.wait()


def raw_kernel(parts, start, final, weight_ref, *refs):
    part_refs, refs = refs[:parts], refs[parts:]
    if start:
        acc_ref, refs = refs[0], refs[1:]
    width = part_refs[0].shape[2]
    for e in range(weight_ref.shape[0]):
        raw = lax.dot_general(
            stacked_rows(part_refs, e, slice(None)),
            weight_ref[e, :, start : start + width],
            (((1,), (1,)), ((), ())),
            preferred_element_type=F32,
        )
        if start:
            raw = raw + acc_ref[e]
        if not final:
            refs[0][e] = raw
            continue
        hidden_ref, grad_ref, sums_ref = refs
        sources, _, own, units = hidden_ref.shape
        me = lax.axis_index("expert") if sources > 1 else 0
        folds = []
        for part in range(sources):
            source = source_of(me, part) if sources > 1 else 0
            block = raw[part * own : (part + 1) * own]
            grad_ref[source, e] = block.astype(BF16)
            product = block * hidden_ref[source, e].astype(F32)
            folds.append(
                functools.reduce(jnp.add, [product[:, i : i + 128] for i in range(0, units, 128)])
            )
        folded = jnp.concatenate(folds, axis=0) if len(folds) > 1 else folds[0]
        sums_ref[e : e + 1, :] = jnp.sum(folded.T, axis=0, keepdims=True)


def prob_kernel(direct, capacity, flat_ref, probs_ref, *refs):
    out_ref = refs[-1]
    chosen, tokens = flat_ref.shape
    if direct:
        values = []
        for q in range(LINE * SIDES):
            at = (BACK.index(q // SIDES) + LINE * (q % SIDES)) * capacity
            ref = refs[q // SIDES]
            values += [ref[q % SIDES, e : e + 1, at : at + capacity] for e in range(ref.shape[1])]
        lanes = 128 // capacity
        values = jnp.concatenate(
            [
                jnp.concatenate([v.reshape(1, capacity) for v in values[i : i + lanes]], axis=1)
                for i in range(0, len(values), lanes)
            ],
            axis=0,
        )
        me = lax.axis_index("expert")
    else:
        values = refs[0][...]
        me = 0
    lines = values.shape[0]
    spare = jnp.zeros((-lines % 8, 128), F32)
    columns = jnp.concatenate([values, spare], axis=0).T if spare.size else values.T
    total, gates, word = gates_of(probs_ref[...])
    group = lines * 128 // (LINE * SIDES)
    picked = [jnp.zeros((1, tokens), F32) for _ in range(chosen)]
    for line in range(lines):
        at = lax.broadcasted_iota(I32, (128, tokens), 0) + line * 128
        q = at // group
        slot = (moved(me, q // SIDES, q % SIDES) if direct else q) * group + at % group
        for k in range(chosen):
            hit = jnp.where(flat_ref[k : k + 1, :] == slot, columns[:, line : line + 1], 0.0)
            picked[k] += jnp.sum(hit, axis=0, keepdims=True)
    picked = [picked[k] / word[k : k + 1] for k in range(chosen)]
    mixed = functools.reduce(jnp.add, [gates[k : k + 1] * picked[k] for k in range(chosen)])
    for k in range(chosen):
        out_ref[k : k + 1, :] = (picked[k] - mixed) / total


def chunks_of(features):
    unit = features // 16
    return [[7 * unit], [5 * unit, 4 * unit]]


def cuts_of(share, first):
    return [share // 3] * 3 if first else [share]


sds = jax.ShapeDtypeStruct


class Relay:
    def __init__(self, call, grad_out, ids, probs, held, capacity, widths):
        tokens, features = grad_out.shape
        self.call, self.held, self.capacity, self.widths = call, held, capacity, widths
        self.tokens, self.chosen, self.place = tokens, ids.shape[0], {}
        self.flat, first = call(
            functools.partial(begin_kernel, LINE * SIDES * held, capacity),
            [sds(ids.shape, I32), sds((tokens + INFO, widths[0]), BF16)],
            ids,
            probs,
            grad_out,
            in_specs=[HBM] * 3,
            scratch_shapes=[
                pltpu.VMEM(ids.shape, I32),
                pltpu.VMEM(probs.shape, F32),
                pltpu.SemaphoreType.DMA((3,)),
            ],
            room=60,
            keep=False,
        )
        rest = call(
            functools.partial(cut_kernel, widths[0]),
            [sds((tokens, w), BF16) for w in widths[1:]],
            grad_out,
            in_specs=[HBM],
            scratch_shapes=[pltpu.SemaphoreType.DMA((len(widths) - 1,))],
            keep=False,
        )
        self.blocks, self.passed = [], []
        for own in [first, *rest]:
            on, back = self.along(own, 1), self.along(own, LINE - 1)
            self.blocks.append([own, on, back])
            self.passed.append(self.along(on, 1))

    def along(self, block, places):
        pairs = [(i, moved(i, places, 0)) for i in range(LINE * SIDES)]
        return lax.ppermute(block, "expert", pairs)

    def pick(self, c, name, blocks, at=0):
        held, capacity, count = self.held, self.capacity, len(blocks)
        rows = [sds((held, count * capacity, self.widths[c]), BF16)] * SIDES
        kernel = functools.partial(pick_kernel, held, capacity, self.chosen, c == 0, at, count)
        if c == 0:
            place = sds((count, SIDES * held * capacity, self.tokens), BF16)
            mine, other, self.place[name] = self.call(kernel, [*rows, place], *blocks)
        else:
            mine, other = self.call(kernel, rows, *blocks, self.place[name])
        return mine, lax.ppermute(other, "expert", [(i, i ^ 1) for i in range(LINE * SIDES)])

    def early(self, c):
        if c == 0:
            return [self.pick(c, "early", self.blocks[c])]
        own = self.pick(c, "early", self.blocks[c][:1])
        return [own, self.pick(c, "early", self.blocks[c][1:], 1)]

    def late(self, c, early):
        picked = [*early, self.pick(c, "late", [self.passed[c]])]
        return [mine for mine, _ in picked] + [other for _, other in picked]


def exchanged(grad_out, ids, probs, groups, held, capacity, widths):
    tokens = grad_out.shape[0]
    experts = groups * held
    slots = experts * capacity
    _, _, word = gates_of(probs)
    flat = ids * capacity + jnp.concatenate(slots_of(ids, experts), axis=0).astype(I32)
    slot = lax.broadcasted_iota(I32, (slots, tokens), 0)
    place = sum(jnp.where(f == slot, w, 0.0) for f, w in zip(flat, word)).astype(BF16)
    arrived, start = [], 0
    for width in widths:
        rows = grad_out[:, start : start + width]
        sent = jnp.dot(place, rows, preferred_element_type=F32).astype(BF16)
        got = lax.all_to_all(
            sent.reshape(groups, held, capacity, width),
            "expert",
            split_axis=0,
            concat_axis=0,
            tiled=True,
        )
        arrived.append([got.transpose(1, 0, 2, 3).reshape(held, groups * capacity, width)])
        start += width
    return flat, arrived


def body(grad_out, route_ids, route_probs, hidden, w_down):
    groups = lax.axis_size("expert")
    dp = lax.axis_size("dp")
    held, units, features = w_down.shape
    capacity = hidden.shape[3]
    slots = groups * held * capacity
    per_expert = slots // held
    tokens, chosen = route_ids.shape
    share, across = units // dp, dp // 2
    direct = groups == LINE * SIDES
    chunks = chunks_of(features)
    widths = [sum(chunk) for chunk in chunks]
    count = len(widths)

    ids, probs = route_ids.T, route_probs.T
    call = Chain()
    if direct:
        relay = Relay(call, grad_out, ids, probs, held, capacity, widths)
        flat, saved = relay.flat, hidden[0]
    else:
        flat, arrived = exchanged(grad_out, ids, probs, groups, held, capacity, widths)
        saved = hidden[0].transpose(1, 0, 2, 3).reshape(1, held, per_expert, units)
    turned = call(
        functools.partial(turn_kernel, dp),
        sds((held, 2, across, share, per_expert), BF16),
        saved,
    )
    starts = [sum(widths[:c]) for c in range(count)]
    state = {"raw": None, "grad": None}
    summed = []

    def accumulated(c):
        parts, width, final = arrived[c], widths[c], c == count - 1
        if final:
            outs = [sds(saved.shape, BF16), sds((held, per_expert), F32)]
        else:
            outs = [sds((held, per_expert, units), F32)]
        extra = ([state["raw"]] if c else []) + ([saved] if final else [])
        kernel = functools.partial(raw_kernel, len(parts), starts[c], final)
        made = call(
            kernel,
            outs,
            w_down,
            *parts,
            *extra,
        )
        state["raw"] = made if final else made[0]

    def termed(c, at, width):
        piece = sds((across, held, share, width), BF16)
        after = summed[0][2] if summed and at == 0 and direct else ()
        if direct and not c:
            after = [early[0][1]]
        kernel = functools.partial(term_kernel, at)
        keep, give = call(kernel, [piece, piece], turned, *arrived[c], after=after)
        got = lax.ppermute(give, "dp", [(i, i ^ 1) for i in range(dp)])
        return keep, got, starts[c] + at

    def paired(keep, got, start):
        cuts = cuts_of(share, not summed)
        pieces = [sds((held, rows, keep.shape[3]), BF16) for rows in cuts]
        pairs = call(functools.partial(pair_kernel, cuts), pieces * (across - 1), keep, got)
        others = []
        for i, pair in enumerate(pairs):
            step = 1 + i // len(cuts)
            shift = [(2 * r + k, 2 * ((r + step) % across) + k) for r in range(across) for k in range(2)]
            others.append(lax.ppermute(pair, "dp", shift))
        summed.append((keep, got, others, start))

    def finished(first, last):
        before = [] if state["grad"] is None else [state["grad"]]
        done = summed[first:last]
        args = [x for keep, got, others, _ in done for x in (keep, got, *others)]
        cuts = [cuts_of(share, j == 0) for j in range(first, last)]
        state["grad"], _ = call(
            functools.partial(last_kernel, cuts, done[0][3]),
            [sds((share, held, features), F32), sds((8, 128), F32)],
            *args,
            *before,
            in_specs=[VMEM] * len(args) + [ANY] * len(before),
            out_specs=[ANY, VMEM],
            input_output_aliases={len(args): 0} if before else {},
            scratch_shapes=[
                pltpu.VMEM((share, held, sum(keep.shape[3] for keep, *_ in done)), F32),
                pltpu.SemaphoreType.DMA,
            ],
        )

    if direct:
        arrived, early = [], relay.early(0)
    for c, chunk in enumerate(chunks):
        if direct:
            arrived.append(relay.late(c, early))
            if c + 1 < count:
                early = relay.early(c + 1)
        if c >= 1:
            accumulated(c - 1)
        terms = [termed(c, sum(chunk[:i]), width) for i, width in enumerate(chunk)]
        for term in terms:
            paired(*term)
    accumulated(count - 1)
    for j in range(len(summed) - 1):
        finished(j, j + 1)
    hidden_grad, sums = state["raw"]

    if direct:
        swap = [(i, i ^ 1) for i in range(groups)]
        both = jnp.stack([sums, lax.ppermute(sums, "expert", swap)])
        returned = [both] + [
            lax.ppermute(both, "expert", [(moved(i, d, 0), i) for i in range(groups)])
            for d in range(1, LINE)
        ]
    else:
        sums = sums.reshape(held, groups, capacity).transpose(1, 0, 2).reshape(groups, -1)
        hidden_grad = hidden_grad.reshape(held, groups, capacity, units).transpose(1, 0, 2, 3)
        returned = lax.all_to_all(sums, "expert", split_axis=0, concat_axis=0, tiled=True)
        returned = [returned.reshape(-1, 128)]
    prob_grad = call(
        functools.partial(prob_kernel, direct, capacity),
        sds((chosen, tokens), F32),
        flat,
        probs,
        *returned,
    ).T
    finished(len(summed) - 1, len(summed))
    weight_grad = state["grad"]
    return (hidden_grad.reshape(hidden.shape), prob_grad, weight_grad)


def solution(mesh):
    in_specs = (
        P(("dp", "expert"), None),
        P(("dp", "expert"), None),
        P(("dp", "expert"), None),
        P("dp", None, "expert", None, None),
        P("expert", None, None),
    )
    out_specs = (
        P("dp", None, "expert", None, None),
        P(("dp", "expert"), None),
        P("dp", "expert", None),
    )
    return jax.shard_map(body, mesh=mesh, in_specs=in_specs, out_specs=out_specs, check_vma=False)
```

```python
import functools

import jax
import jax.numpy as jnp
from jax import lax
from jax.experimental import pallas as pl
from jax.experimental.pallas import tpu as pltpu
from jax.sharding import PartitionSpec as P

F32, BF16, I32 = jnp.float32, jnp.bfloat16, jnp.int32
VMEM = pl.BlockSpec(memory_space=pltpu.VMEM)
ANY = pl.BlockSpec(memory_space=pl.ANY)
HBM = pl.BlockSpec(memory_space=pltpu.HBM)

LINE, SIDES = 4, 2
BACK = (0, 1, 3, 2)
INFO = 16


def moved(me, places, side):
    return (me // SIDES + places) % LINE * SIDES + (me % SIDES ^ side)


def source_of(me, part):
    return moved(me, LINE - BACK[part % LINE], part // LINE)


class Chain:
    def __init__(self):
        self.last = None

    def __call__(self, kernel, outs, *args, in_specs=None, keep=True, after=(), room=24, **kw):
        in_specs = list(in_specs or [VMEM] * len(args))
        count = len(args)
        body = kernel
        unread = [*after] if self.last is None else [self.last, *after]
        if unread:
            args, in_specs = (*args, *unread), in_specs + [ANY] * len(unread)

            def body(*refs):
                kernel(*refs[:count], *refs[count + len(unread) :])

        made = pl.pallas_call(
            body,
            out_shape=outs,
            in_specs=in_specs,
            compiler_params=pltpu.CompilerParams(vmem_limit_bytes=room * 1024 * 1024),
            cost_estimate=pl.CostEstimate(flops=1, bytes_accessed=1, transcendentals=0),
            **kw,
        )(*args)
        if keep:
            self.last = min(jax.tree.leaves(made), key=lambda x: x.size)
        return made


def gates_of(probs):
    total = jnp.sum(probs, axis=0, keepdims=True)
    gates = probs / total
    return total, gates, gates.astype(BF16).astype(F32)


def slots_of(ids, experts):
    chosen, tokens = ids.shape
    expert = lax.broadcasted_iota(I32, (experts, tokens), 0)
    named = [ids[k : k + 1] == expert for k in range(chosen)]
    hits = functools.reduce(jnp.add, [n.astype(F32) for n in named]).astype(BF16)
    row = lax.broadcasted_iota(I32, (tokens, tokens), 0)
    earlier = (row < lax.broadcasted_iota(I32, (tokens, tokens), 1)).astype(F32).astype(BF16)
    before = jnp.dot(hits, earlier, preferred_element_type=F32)
    return [jnp.sum(jnp.where(n, before, 0.0), axis=0, keepdims=True) for n in named]


def begin_kernel(experts, capacity, ids_ref, probs_ref, rows_ref, flat_ref, out_ref, *scratch):
    ids_got, probs_got, sems = scratch
    chosen, tokens = ids_got.shape
    width = out_ref.shape[1]
    copies = [
        pltpu.make_async_copy(ids_ref, ids_got, sems.at[0]),
        pltpu.make_async_copy(probs_ref, probs_got, sems.at[1]),
        pltpu.make_async_copy(rows_ref.at[:, :width], out_ref.at[:tokens], sems.at[2]),
    ]
    for copy in copies:
        copy.start()
    for copy in copies:
        copy.wait()
    ids = ids_got[...]
    _, _, word = gates_of(probs_got[...])
    slots = slots_of(ids, experts)
    for k in range(chosen):
        flat_ref[k : k + 1, :] = ids[k : k + 1] * capacity + slots[k].astype(I32)
    rest = jnp.zeros((INFO - 3 * chosen, tokens), F32)
    info = jnp.concatenate([ids.astype(F32), *slots, word, rest], axis=0).astype(BF16)
    out_ref[tokens:, :tokens] = info
    if width > tokens:
        out_ref[tokens:, tokens:] = jnp.zeros((INFO, width - tokens), BF16)


def places(held, capacity, chosen, ref, place_ref):
    tokens = place_ref.shape[1]
    rows = held * capacity
    me = lax.axis_index("expert")
    local = lax.broadcasted_iota(I32, (rows, tokens), 0)
    info = ref[tokens:, :tokens].astype(F32)
    flat = (info[:chosen] * capacity + info[chosen : 2 * chosen]).astype(I32)
    word = info[2 * chosen : 3 * chosen]
    for side in range(SIDES):
        slot = local + (me ^ side) * rows
        hits = [jnp.where(flat[k : k + 1] == slot, word[k : k + 1], 0.0) for k in range(chosen)]
        place_ref[side * rows : (side + 1) * rows, :] = functools.reduce(jnp.add, hits).astype(BF16)


def pick(held, capacity, begin, block_refs, place_ref, out_refs):
    tokens = place_ref.shape[2]
    for j, ref in enumerate(block_refs):
        scaled = jnp.dot(place_ref[begin + j], ref[:tokens, :], preferred_element_type=F32).astype(BF16)
        for side, out_ref in enumerate(out_refs):
            for e in range(held):
                at = (side * held + e) * capacity
                out_ref[e, j * capacity : (j + 1) * capacity, :] = scaled[at : at + capacity]


def pick_kernel(held, capacity, chosen, first, at, count, *refs):
    block_refs, refs = refs[:count], refs[count:]
    if first:
        mine_ref, other_ref, place_ref = refs
        for j, ref in enumerate(block_refs):
            places(held, capacity, chosen, ref, place_ref.at[j])
    else:
        place_ref, mine_ref, other_ref = refs
    pick(held, capacity, at, block_refs, place_ref, (mine_ref, other_ref))


def turn_kernel(dp, hidden_ref, *refs):
    out_ref, refs = refs[-1], refs[:-1]
    parts, held, _, units = hidden_ref.shape
    share, across = units // dp, dp // 2
    me = lax.axis_index("expert") if parts > 1 else 0
    mine = lax.axis_index("dp")
    core, row = mine % 2, mine // 2
    for e in range(held):
        sources = [source_of(me, p) if parts > 1 else 0 for p in range(parts)]
        stacked = jnp.concatenate([hidden_ref[source, e] for source in sources], axis=0)
        turned = stacked.T
        for piece in range(dp):
            other = (piece % 2) ^ core
            step = (piece // 2 - row + across) % across
            out_ref[e, other, step] = turned[piece * share : (piece + 1) * share]


def cut_kernel(start, rows_ref, *refs):
    out_refs, sems = refs[:-1], refs[-1]
    copies = []
    for i, ref in enumerate(out_refs):
        at = slice(start, start + ref.shape[1])
        copies.append(pltpu.make_async_copy(rows_ref.at[:, at], ref, sems.at[i]))
        start += ref.shape[1]
    for copy in copies:
        copy.start()
    for copy in copies:
        copy.wait()


def stacked_rows(refs, e, at):
    rows = [ref[e, :, at] for ref in refs]
    return rows[0] if len(rows) == 1 else jnp.concatenate(rows, axis=0)


def term_kernel(start, turned_ref, *refs):
    part_refs, keep_ref, give_ref = refs[:-2], refs[-2], refs[-1]
    held, _, across, share, slots = turned_ref.shape
    at = slice(start, start + keep_ref.shape[3])
    for e in range(held):
        scaled = stacked_rows(part_refs, e, at)
        for other, ref in ((1, give_ref), (0, keep_ref)):
            left = turned_ref[e, other].reshape(across * share, slots)
            term = jnp.dot(left, scaled, preferred_element_type=F32).astype(BF16)
            for step in range(across):
                ref[step, e] = term[step * share : (step + 1) * share]


def pair_kernel(cuts, keep_ref, got_ref, *out_refs):
    out_refs = iter(out_refs)
    for step in range(1, keep_ref.shape[0]):
        start = 0
        for rows in cuts:
            at = slice(start, start + rows)
            pair = keep_ref[step, :, at].astype(F32) + got_ref[step, :, at].astype(F32)
            next(out_refs)[...] = pair.astype(BF16)
            start += rows


def last_kernel(cuts, start, *refs):
    out_ref, mark_ref, total_ref, sem = refs[-4:]
    mark_ref[...] = jnp.zeros(mark_ref.shape, F32)
    column = 0
    for rows_of in cuts:
        keep_ref, got_ref, *refs = refs
        across, held, _, width = keep_ref.shape
        others, refs = refs[: len(rows_of) * (across - 1)], refs[len(rows_of) * (across - 1) :]
        columns = slice(column, column + width)
        column += width
        for e in range(held):
            row = 0
            for cut, rows in enumerate(rows_of):
                at = slice(row, row + rows)
                total = keep_ref[0, e, at].astype(F32) + got_ref[0, e, at].astype(F32)
                for ref in others[cut :: len(rows_of)]:
                    total = total + ref[e].astype(F32)
                total_ref[at, e, columns] = total
                row += rows
    copy = pltpu.make_async_copy(
        total_ref, out_ref.at[:, :, start : start + total_ref.shape[2]], sem
    )
    copy.start()
    copy.wait()


def raw_kernel(parts, start, final, weight_ref, *refs):
    part_refs, refs = refs[:parts], refs[parts:]
    if start:
        acc_ref, refs = refs[0], refs[1:]
    width = part_refs[0].shape[2]
    for e in range(weight_ref.shape[0]):
        raw = lax.dot_general(
            stacked_rows(part_refs, e, slice(None)),
            weight_ref[e, :, start : start + width],
            (((1,), (1,)), ((), ())),
            preferred_element_type=F32,
        )
        if start:
            raw = raw + acc_ref[e]
        if not final:
            refs[0][e] = raw
            continue
        hidden_ref, grad_ref, sums_ref = refs
        sources, _, own, units = hidden_ref.shape
        me = lax.axis_index("expert") if sources > 1 else 0
        folds = []
        for part in range(sources):
            source = source_of(me, part) if sources > 1 else 0
            block = raw[part * own : (part + 1) * own]
            grad_ref[source, e] = block.astype(BF16)
            product = block * hidden_ref[source, e].astype(F32)
            folds.append(
                functools.reduce(jnp.add, [product[:, i : i + 128] for i in range(0, units, 128)])
            )
        folded = jnp.concatenate(folds, axis=0) if len(folds) > 1 else folds[0]
        sums_ref[e : e + 1, :] = jnp.sum(folded.T, axis=0, keepdims=True)


def prob_kernel(direct, capacity, flat_ref, probs_ref, *refs):
    out_ref, mark_ref = refs[-2:]
    mark_ref[...] = jnp.zeros(mark_ref.shape, F32)
    chosen, tokens = flat_ref.shape
    if direct:
        values = []
        for q in range(LINE * SIDES):
            at = (BACK.index(q // SIDES) + LINE * (q % SIDES)) * capacity
            ref = refs[q // SIDES]
            values += [ref[q % SIDES, e : e + 1, at : at + capacity] for e in range(ref.shape[1])]
        lanes = 128 // capacity
        values = jnp.concatenate(
            [
                jnp.concatenate([v.reshape(1, capacity) for v in values[i : i + lanes]], axis=1)
                for i in range(0, len(values), lanes)
            ],
            axis=0,
        )
        me = lax.axis_index("expert")
    else:
        values = refs[0][...]
        me = 0
    lines = values.shape[0]
    spare = jnp.zeros((-lines % 8, 128), F32)
    columns = jnp.concatenate([values, spare], axis=0).T if spare.size else values.T
    total, gates, word = gates_of(probs_ref[...])
    group = lines * 128 // (LINE * SIDES)
    picked = [jnp.zeros((1, tokens), F32) for _ in range(chosen)]
    for line in range(lines):
        at = lax.broadcasted_iota(I32, (128, tokens), 0) + line * 128
        q = at // group
        slot = (moved(me, q // SIDES, q % SIDES) if direct else q) * group + at % group
        for k in range(chosen):
            hit = jnp.where(flat_ref[k : k + 1, :] == slot, columns[:, line : line + 1], 0.0)
            picked[k] += jnp.sum(hit, axis=0, keepdims=True)
    picked = [picked[k] / word[k : k + 1] for k in range(chosen)]
    mixed = functools.reduce(jnp.add, [gates[k : k + 1] * picked[k] for k in range(chosen)])
    for k in range(chosen):
        out_ref[k : k + 1, :] = (picked[k] - mixed) / total


def chunks_of(features):
    unit = features // 16
    return [[6 * unit], [6 * unit, 4 * unit]]


def cuts_of(share, first):
    return [share // 3] * 3 if first else [share]


sds = jax.ShapeDtypeStruct


class Relay:
    def __init__(self, call, grad_out, ids, probs, held, capacity, widths):
        tokens, features = grad_out.shape
        self.call, self.held, self.capacity, self.widths = call, held, capacity, widths
        self.tokens, self.chosen, self.place = tokens, ids.shape[0], {}
        self.flat, first = call(
            functools.partial(begin_kernel, LINE * SIDES * held, capacity),
            [sds(ids.shape, I32), sds((tokens + INFO, widths[0]), BF16)],
            ids,
            probs,
            grad_out,
            in_specs=[HBM] * 3,
            scratch_shapes=[
                pltpu.VMEM(ids.shape, I32),
                pltpu.VMEM(probs.shape, F32),
                pltpu.SemaphoreType.DMA((3,)),
            ],
            room=60,
            keep=False,
        )
        self.blocks, self.passed = [], []
        self.leave(first)
        rest = call(
            functools.partial(cut_kernel, widths[0]),
            [sds((tokens, w), BF16) for w in widths[1:]],
            grad_out,
            in_specs=[HBM],
            scratch_shapes=[pltpu.SemaphoreType.DMA((len(widths) - 1,))],
            after=[self.blocks[0][1]],
        )
        for own in rest:
            self.leave(own)

    def leave(self, own):
        on, back = self.along(own, 1), self.along(own, LINE - 1)
        self.blocks.append([own, on, back])
        self.passed.append(self.along(on, 1))

    def along(self, block, places):
        pairs = [(i, moved(i, places, 0)) for i in range(LINE * SIDES)]
        return lax.ppermute(block, "expert", pairs)

    def pick(self, c, name, blocks, at=0):
        held, capacity, count = self.held, self.capacity, len(blocks)
        rows = [sds((held, count * capacity, self.widths[c]), BF16)] * SIDES
        kernel = functools.partial(pick_kernel, held, capacity, self.chosen, c == 0, at, count)
        if c == 0:
            place = sds((count, SIDES * held * capacity, self.tokens), BF16)
            mine, other, self.place[name] = self.call(kernel, [*rows, place], *blocks)
        else:
            mine, other = self.call(kernel, rows, *blocks, self.place[name])
        return mine, lax.ppermute(other, "expert", [(i, i ^ 1) for i in range(LINE * SIDES)])

    def early(self, c):
        if c == 0:
            return [self.pick(c, "early", self.blocks[c])]
        own = self.pick(c, "early", self.blocks[c][:1])
        return [own, self.pick(c, "early", self.blocks[c][1:], 1)]

    def late(self, c, early):
        picked = [*early, self.pick(c, "late", [self.passed[c]])]
        return [mine for mine, _ in picked] + [other for _, other in picked]


def exchanged(grad_out, ids, probs, groups, held, capacity, widths):
    tokens = grad_out.shape[0]
    experts = groups * held
    slots = experts * capacity
    _, _, word = gates_of(probs)
    flat = ids * capacity + jnp.concatenate(slots_of(ids, experts), axis=0).astype(I32)
    slot = lax.broadcasted_iota(I32, (slots, tokens), 0)
    place = sum(jnp.where(f == slot, w, 0.0) for f, w in zip(flat, word)).astype(BF16)
    arrived, start = [], 0
    for width in widths:
        rows = grad_out[:, start : start + width]
        sent = jnp.dot(place, rows, preferred_element_type=F32).astype(BF16)
        got = lax.all_to_all(
            sent.reshape(groups, held, capacity, width),
            "expert",
            split_axis=0,
            concat_axis=0,
            tiled=True,
        )
        arrived.append([got.transpose(1, 0, 2, 3).reshape(held, groups * capacity, width)])
        start += width
    return flat, arrived


def body(grad_out, route_ids, route_probs, hidden, w_down):
    groups = lax.axis_size("expert")
    dp = lax.axis_size("dp")
    held, units, features = w_down.shape
    capacity = hidden.shape[3]
    slots = groups * held * capacity
    per_expert = slots // held
    tokens, chosen = route_ids.shape
    share, across = units // dp, dp // 2
    direct = groups == LINE * SIDES
    chunks = chunks_of(features)
    widths = [sum(chunk) for chunk in chunks]
    count = len(widths)

    ids, probs = route_ids.T, route_probs.T
    call = Chain()
    if direct:
        relay = Relay(call, grad_out, ids, probs, held, capacity, widths)
        flat, saved = relay.flat, hidden[0]
    else:
        flat, arrived = exchanged(grad_out, ids, probs, groups, held, capacity, widths)
        saved = hidden[0].transpose(1, 0, 2, 3).reshape(1, held, per_expert, units)
    turned = call(
        functools.partial(turn_kernel, dp),
        sds((held, 2, across, share, per_expert), BF16),
        saved,
    )
    starts = [sum(widths[:c]) for c in range(count)]
    state = {"raw": None, "grad": None}
    summed = []

    def accumulated(c):
        parts, width, final = arrived[c], widths[c], c == count - 1
        if final:
            outs = [sds(saved.shape, BF16), sds((held, per_expert), F32)]
        else:
            outs = [sds((held, per_expert, units), F32)]
        extra = ([state["raw"]] if c else []) + ([saved] if final else [])
        kernel = functools.partial(raw_kernel, len(parts), starts[c], final)
        made = call(
            kernel,
            outs,
            w_down,
            *parts,
            *extra,
        )
        state["raw"] = made if final else made[0]

    def termed(c, at, width):
        piece = sds((across, held, share, width), BF16)
        after = summed[0][2] if summed and at == 0 and direct else ()
        if direct and not c:
            after = [early[0][1]]
        kernel = functools.partial(term_kernel, at)
        keep, give = call(kernel, [piece, piece], turned, *arrived[c], after=after)
        got = lax.ppermute(give, "dp", [(i, i ^ 1) for i in range(dp)])
        return keep, got, starts[c] + at

    def paired(keep, got, start):
        cuts = cuts_of(share, not summed)
        pieces = [sds((held, rows, keep.shape[3]), BF16) for rows in cuts]
        pairs = call(functools.partial(pair_kernel, cuts), pieces * (across - 1), keep, got)
        others = []
        for i, pair in enumerate(pairs):
            step = 1 + i // len(cuts)
            shift = [(2 * r + k, 2 * ((r + step) % across) + k) for r in range(across) for k in range(2)]
            others.append(lax.ppermute(pair, "dp", shift))
        summed.append((keep, got, others, start))

    def finished(first, last):
        before = [] if state["grad"] is None else [state["grad"]]
        done = summed[first:last]
        args = [x for keep, got, others, _ in done for x in (keep, got, *others)]
        cuts = [cuts_of(share, j == 0) for j in range(first, last)]
        state["grad"], _ = call(
            functools.partial(last_kernel, cuts, done[0][3]),
            [sds((share, held, features), F32), sds((8, 128), F32)],
            *args,
            *before,
            in_specs=[VMEM] * len(args) + [ANY] * len(before),
            out_specs=[ANY, VMEM],
            input_output_aliases={len(args): 0} if before else {},
            scratch_shapes=[
                pltpu.VMEM((share, held, sum(keep.shape[3] for keep, *_ in done)), F32),
                pltpu.SemaphoreType.DMA,
            ],
        )

    if direct:
        arrived, early = [], relay.early(0)
    for c, chunk in enumerate(chunks):
        if direct:
            arrived.append(relay.late(c, early))
            if c + 1 < count:
                early = relay.early(c + 1)
        if c >= 1:
            accumulated(c - 1)
        terms = [termed(c, sum(chunk[:i]), width) for i, width in enumerate(chunk)]
        for term in terms:
            paired(*term)
    accumulated(count - 1)
    for j in range(len(summed) - 1):
        finished(j, j + 1)
    hidden_grad, sums = state["raw"]

    if direct:
        swap = [(i, i ^ 1) for i in range(groups)]
        both = jnp.stack([sums, lax.ppermute(sums, "expert", swap)])
        returned = [both] + [
            lax.ppermute(both, "expert", [(moved(i, d, 0), i) for i in range(groups)])
            for d in range(1, LINE)
        ]
    else:
        sums = sums.reshape(held, groups, capacity).transpose(1, 0, 2).reshape(groups, -1)
        hidden_grad = hidden_grad.reshape(held, groups, capacity, units).transpose(1, 0, 2, 3)
        returned = lax.all_to_all(sums, "expert", split_axis=0, concat_axis=0, tiled=True)
        returned = [returned.reshape(-1, 128)]
    prob_grad, call.last = call(
        functools.partial(prob_kernel, direct, capacity),
        [sds((chosen, tokens), F32), sds((8, 128), F32)],
        flat,
        probs,
        *returned,
    )
    prob_grad = prob_grad.T
    finished(len(summed) - 1, len(summed))
    weight_grad = state["grad"]
    return (hidden_grad.reshape(hidden.shape), prob_grad, weight_grad)


def solution(mesh):
    in_specs = (
        P(("dp", "expert"), None),
        P(("dp", "expert"), None),
        P(("dp", "expert"), None),
        P("dp", None, "expert", None, None),
        P("expert", None, None),
    )
    out_specs = (
        P("dp", None, "expert", None, None),
        P(("dp", "expert"), None),
        P("dp", "expert", None),
    )
    return jax.shard_map(body, mesh=mesh, in_specs=in_specs, out_specs=out_specs, check_vma=False)
```

```python
import functools

import jax
import jax.numpy as jnp
from jax import lax
from jax.experimental import pallas as pl
from jax.experimental.pallas import tpu as pltpu
from jax.sharding import PartitionSpec as P

F32, BF16, I32 = jnp.float32, jnp.bfloat16, jnp.int32
VMEM = pl.BlockSpec(memory_space=pltpu.VMEM)
ANY = pl.BlockSpec(memory_space=pl.ANY)
HBM = pl.BlockSpec(memory_space=pltpu.HBM)

LINE, SIDES = 4, 2
BACK = (0, 1, 3, 2)
INFO = 16


def moved(me, places, side):
    return (me // SIDES + places) % LINE * SIDES + (me % SIDES ^ side)


def source_of(me, part):
    return moved(me, LINE - BACK[part % LINE], part // LINE)


class Chain:
    def __init__(self):
        self.last = None

    def __call__(self, kernel, outs, *args, in_specs=None, keep=True, after=(), room=24, **kw):
        in_specs = list(in_specs or [VMEM] * len(args))
        count = len(args)
        body = kernel
        unread = [*after] if self.last is None else [self.last, *after]
        if unread:
            args, in_specs = (*args, *unread), in_specs + [ANY] * len(unread)

            def body(*refs):
                kernel(*refs[:count], *refs[count + len(unread) :])

        made = pl.pallas_call(
            body,
            out_shape=outs,
            in_specs=in_specs,
            compiler_params=pltpu.CompilerParams(vmem_limit_bytes=room * 1024 * 1024),
            cost_estimate=pl.CostEstimate(flops=1, bytes_accessed=1, transcendentals=0),
            **kw,
        )(*args)
        if keep:
            self.last = min(jax.tree.leaves(made), key=lambda x: x.size)
        return made


def gates_of(probs):
    total = jnp.sum(probs, axis=0, keepdims=True)
    gates = probs / total
    return total, gates, gates.astype(BF16).astype(F32)


def slots_of(ids, experts):
    chosen, tokens = ids.shape
    expert = lax.broadcasted_iota(I32, (experts, tokens), 0)
    named = [ids[k : k + 1] == expert for k in range(chosen)]
    hits = functools.reduce(jnp.add, [n.astype(F32) for n in named]).astype(BF16)
    row = lax.broadcasted_iota(I32, (tokens, tokens), 0)
    earlier = (row < lax.broadcasted_iota(I32, (tokens, tokens), 1)).astype(F32).astype(BF16)
    before = jnp.dot(hits, earlier, preferred_element_type=F32)
    return [jnp.sum(jnp.where(n, before, 0.0), axis=0, keepdims=True) for n in named]


def begin_kernel(experts, capacity, ids_ref, probs_ref, rows_ref, flat_ref, out_ref, *scratch):
    ids_got, probs_got, sems = scratch
    chosen, tokens = ids_got.shape
    width = out_ref.shape[1]
    copies = [
        pltpu.make_async_copy(ids_ref, ids_got, sems.at[0]),
        pltpu.make_async_copy(probs_ref, probs_got, sems.at[1]),
        pltpu.make_async_copy(rows_ref.at[:, :width], out_ref.at[:tokens], sems.at[2]),
    ]
    for copy in copies:
        copy.start()
    for copy in copies:
        copy.wait()
    ids = ids_got[...]
    _, _, word = gates_of(probs_got[...])
    slots = slots_of(ids, experts)
    for k in range(chosen):
        flat_ref[k : k + 1, :] = ids[k : k + 1] * capacity + slots[k].astype(I32)
    rest = jnp.zeros((INFO - 3 * chosen, tokens), F32)
    info = jnp.concatenate([ids.astype(F32), *slots, word, rest], axis=0).astype(BF16)
    out_ref[tokens:, :tokens] = info
    if width > tokens:
        out_ref[tokens:, tokens:] = jnp.zeros((INFO, width - tokens), BF16)


def places(held, capacity, chosen, ref, place_ref):
    tokens = place_ref.shape[1]
    rows = held * capacity
    me = lax.axis_index("expert")
    local = lax.broadcasted_iota(I32, (rows, tokens), 0)
    info = ref[tokens:, :tokens].astype(F32)
    flat = (info[:chosen] * capacity + info[chosen : 2 * chosen]).astype(I32)
    word = info[2 * chosen : 3 * chosen]
    for side in range(SIDES):
        slot = local + (me ^ side) * rows
        hits = [jnp.where(flat[k : k + 1] == slot, word[k : k + 1], 0.0) for k in range(chosen)]
        place_ref[side * rows : (side + 1) * rows, :] = functools.reduce(jnp.add, hits).astype(BF16)


def pick(held, capacity, begin, block_refs, place_ref, out_refs):
    tokens = place_ref.shape[2]
    for j, ref in enumerate(block_refs):
        scaled = jnp.dot(place_ref[begin + j], ref[:tokens, :], preferred_element_type=F32).astype(BF16)
        for side, out_ref in enumerate(out_refs):
            for e in range(held):
                at = (side * held + e) * capacity
                out_ref[e, j * capacity : (j + 1) * capacity, :] = scaled[at : at + capacity]


def pick_kernel(held, capacity, chosen, first, at, count, *refs):
    block_refs, refs = refs[:count], refs[count:]
    if first:
        mine_ref, other_ref, place_ref = refs
        for j, ref in enumerate(block_refs):
            places(held, capacity, chosen, ref, place_ref.at[j])
    else:
        place_ref, mine_ref, other_ref = refs
    pick(held, capacity, at, block_refs, place_ref, (mine_ref, other_ref))


def turn_kernel(dp, hidden_ref, *refs):
    out_ref, refs = refs[-1], refs[:-1]
    parts, held, _, units = hidden_ref.shape
    share, across = units // dp, dp // 2
    me = lax.axis_index("expert") if parts > 1 else 0
    mine = lax.axis_index("dp")
    core, row = mine % 2, mine // 2
    for e in range(held):
        sources = [source_of(me, p) if parts > 1 else 0 for p in range(parts)]
        stacked = jnp.concatenate([hidden_ref[source, e] for source in sources], axis=0)
        turned = stacked.T
        for piece in range(dp):
            other = (piece % 2) ^ core
            step = (piece // 2 - row + across) % across
            out_ref[e, other, step] = turned[piece * share : (piece + 1) * share]


def cut_kernel(start, rows_ref, *refs):
    out_refs, sems = refs[:-1], refs[-1]
    copies = []
    for i, ref in enumerate(out_refs):
        at = slice(start, start + ref.shape[1])
        copies.append(pltpu.make_async_copy(rows_ref.at[:, at], ref, sems.at[i]))
        start += ref.shape[1]
    for copy in copies:
        copy.start()
    for copy in copies:
        copy.wait()


def stacked_rows(refs, e, at):
    rows = [ref[e, :, at] for ref in refs]
    return rows[0] if len(rows) == 1 else jnp.concatenate(rows, axis=0)


def term_kernel(start, turned_ref, *refs):
    part_refs, keep_ref, give_ref = refs[:-2], refs[-2], refs[-1]
    held, _, across, share, slots = turned_ref.shape
    at = slice(start, start + keep_ref.shape[3])
    for e in range(held):
        scaled = stacked_rows(part_refs, e, at)
        for other, ref in ((1, give_ref), (0, keep_ref)):
            left = turned_ref[e, other].reshape(across * share, slots)
            term = jnp.dot(left, scaled, preferred_element_type=F32).astype(BF16)
            for step in range(across):
                ref[step, e] = term[step * share : (step + 1) * share]


def pair_kernel(cuts, keep_ref, got_ref, *out_refs):
    out_refs = iter(out_refs)
    for step in range(1, keep_ref.shape[0]):
        start = 0
        for rows in cuts:
            at = slice(start, start + rows)
            pair = keep_ref[step, :, at].astype(F32) + got_ref[step, :, at].astype(F32)
            next(out_refs)[...] = pair.astype(BF16)
            start += rows


def last_kernel(cuts, start, *refs):
    out_ref, mark_ref, total_ref, sem = refs[-4:]
    mark_ref[...] = jnp.zeros(mark_ref.shape, F32)
    column = 0
    for rows_of in cuts:
        keep_ref, got_ref, *refs = refs
        across, held, _, width = keep_ref.shape
        others, refs = refs[: len(rows_of) * (across - 1)], refs[len(rows_of) * (across - 1) :]
        columns = slice(column, column + width)
        column += width
        for e in range(held):
            row = 0
            for cut, rows in enumerate(rows_of):
                at = slice(row, row + rows)
                total = keep_ref[0, e, at].astype(F32) + got_ref[0, e, at].astype(F32)
                for ref in others[cut :: len(rows_of)]:
                    total = total + ref[e].astype(F32)
                total_ref[at, e, columns] = total
                row += rows
    copy = pltpu.make_async_copy(
        total_ref, out_ref.at[:, :, start : start + total_ref.shape[2]], sem
    )
    copy.start()
    copy.wait()


def raw_kernel(parts, start, final, weight_ref, *refs):
    part_refs, refs = refs[:parts], refs[parts:]
    if start:
        acc_ref, refs = refs[0], refs[1:]
    width = part_refs[0].shape[2]
    for e in range(weight_ref.shape[0]):
        raw = lax.dot_general(
            stacked_rows(part_refs, e, slice(None)),
            weight_ref[e, :, start : start + width],
            (((1,), (1,)), ((), ())),
            preferred_element_type=F32,
        )
        if start:
            raw = raw + acc_ref[e]
        if not final:
            refs[0][e] = raw
            continue
        hidden_ref, grad_ref, sums_ref = refs
        sources, _, own, units = hidden_ref.shape
        me = lax.axis_index("expert") if sources > 1 else 0
        folds = []
        for part in range(sources):
            source = source_of(me, part) if sources > 1 else 0
            block = raw[part * own : (part + 1) * own]
            grad_ref[source, e] = block.astype(BF16)
            product = block * hidden_ref[source, e].astype(F32)
            folds.append(
                functools.reduce(jnp.add, [product[:, i : i + 128] for i in range(0, units, 128)])
            )
        folded = jnp.concatenate(folds, axis=0) if len(folds) > 1 else folds[0]
        sums_ref[e : e + 1, :] = jnp.sum(folded.T, axis=0, keepdims=True)


def prob_kernel(direct, capacity, flat_ref, probs_ref, *refs):
    out_ref, mark_ref = refs[-2:]
    mark_ref[...] = jnp.zeros(mark_ref.shape, F32)
    chosen, tokens = flat_ref.shape
    if direct:
        values = []
        for q in range(LINE * SIDES):
            at = (BACK.index(q // SIDES) + LINE * (q % SIDES)) * capacity
            ref = refs[q // SIDES]
            values += [ref[q % SIDES, e : e + 1, at : at + capacity] for e in range(ref.shape[1])]
        lanes = 128 // capacity
        values = jnp.concatenate(
            [
                jnp.concatenate([v.reshape(1, capacity) for v in values[i : i + lanes]], axis=1)
                for i in range(0, len(values), lanes)
            ],
            axis=0,
        )
        me = lax.axis_index("expert")
    else:
        values = refs[0][...]
        me = 0
    lines = values.shape[0]
    spare = jnp.zeros((-lines % 8, 128), F32)
    columns = jnp.concatenate([values, spare], axis=0).T if spare.size else values.T
    total, gates, word = gates_of(probs_ref[...])
    group = lines * 128 // (LINE * SIDES)
    picked = [jnp.zeros((1, tokens), F32) for _ in range(chosen)]
    for line in range(lines):
        at = lax.broadcasted_iota(I32, (128, tokens), 0) + line * 128
        q = at // group
        slot = (moved(me, q // SIDES, q % SIDES) if direct else q) * group + at % group
        for k in range(chosen):
            hit = jnp.where(flat_ref[k : k + 1, :] == slot, columns[:, line : line + 1], 0.0)
            picked[k] += jnp.sum(hit, axis=0, keepdims=True)
    picked = [picked[k] / word[k : k + 1] for k in range(chosen)]
    mixed = functools.reduce(jnp.add, [gates[k : k + 1] * picked[k] for k in range(chosen)])
    for k in range(chosen):
        out_ref[k : k + 1, :] = (picked[k] - mixed) / total


def chunks_of(features):
    unit = features // 16
    return [[6 * unit], [3 * unit, 7 * unit]]


def cuts_of(share, first):
    return [share // 3] * 3 if first else [share]


sds = jax.ShapeDtypeStruct


class Relay:
    def __init__(self, call, grad_out, ids, probs, held, capacity, widths):
        tokens, features = grad_out.shape
        self.call, self.held, self.capacity, self.widths = call, held, capacity, widths
        self.tokens, self.chosen, self.place = tokens, ids.shape[0], {}
        self.flat, first = call(
            functools.partial(begin_kernel, LINE * SIDES * held, capacity),
            [sds(ids.shape, I32), sds((tokens + INFO, widths[0]), BF16)],
            ids,
            probs,
            grad_out,
            in_specs=[HBM] * 3,
            scratch_shapes=[
                pltpu.VMEM(ids.shape, I32),
                pltpu.VMEM(probs.shape, F32),
                pltpu.SemaphoreType.DMA((3,)),
            ],
            room=60,
            keep=False,
        )
        self.blocks, self.passed = [], []
        self.leave(first)
        rest = call(
            functools.partial(cut_kernel, widths[0]),
            [sds((tokens, w), BF16) for w in widths[1:]],
            grad_out,
            in_specs=[HBM],
            scratch_shapes=[pltpu.SemaphoreType.DMA((len(widths) - 1,))],
            after=[self.blocks[0][1]],
        )
        for own in rest:
            self.leave(own)

    def leave(self, own):
        on, back = self.along(own, 1), self.along(own, LINE - 1)
        self.blocks.append([own, on, back])
        self.passed.append(self.along(on, 1))

    def along(self, block, places):
        pairs = [(i, moved(i, places, 0)) for i in range(LINE * SIDES)]
        return lax.ppermute(block, "expert", pairs)

    def pick(self, c, name, blocks, at=0):
        held, capacity, count = self.held, self.capacity, len(blocks)
        rows = [sds((held, count * capacity, self.widths[c]), BF16)] * SIDES
        kernel = functools.partial(pick_kernel, held, capacity, self.chosen, c == 0, at, count)
        if c == 0:
            place = sds((count, SIDES * held * capacity, self.tokens), BF16)
            mine, other, self.place[name] = self.call(kernel, [*rows, place], *blocks)
        else:
            mine, other = self.call(kernel, rows, *blocks, self.place[name])
        return mine, lax.ppermute(other, "expert", [(i, i ^ 1) for i in range(LINE * SIDES)])

    def early(self, c):
        if c == 0:
            return [self.pick(c, "early", self.blocks[c])]
        own = self.pick(c, "early", self.blocks[c][:1])
        return [own, self.pick(c, "early", self.blocks[c][1:], 1)]

    def late(self, c, early):
        picked = [*early, self.pick(c, "late", [self.passed[c]])]
        return [mine for mine, _ in picked] + [other for _, other in picked]


def exchanged(grad_out, ids, probs, groups, held, capacity, widths):
    tokens = grad_out.shape[0]
    experts = groups * held
    slots = experts * capacity
    _, _, word = gates_of(probs)
    flat = ids * capacity + jnp.concatenate(slots_of(ids, experts), axis=0).astype(I32)
    slot = lax.broadcasted_iota(I32, (slots, tokens), 0)
    place = sum(jnp.where(f == slot, w, 0.0) for f, w in zip(flat, word)).astype(BF16)
    arrived, start = [], 0
    for width in widths:
        rows = grad_out[:, start : start + width]
        sent = jnp.dot(place, rows, preferred_element_type=F32).astype(BF16)
        got = lax.all_to_all(
            sent.reshape(groups, held, capacity, width),
            "expert",
            split_axis=0,
            concat_axis=0,
            tiled=True,
        )
        arrived.append([got.transpose(1, 0, 2, 3).reshape(held, groups * capacity, width)])
        start += width
    return flat, arrived


def body(grad_out, route_ids, route_probs, hidden, w_down):
    groups = lax.axis_size("expert")
    dp = lax.axis_size("dp")
    held, units, features = w_down.shape
    capacity = hidden.shape[3]
    slots = groups * held * capacity
    per_expert = slots // held
    tokens, chosen = route_ids.shape
    share, across = units // dp, dp // 2
    direct = groups == LINE * SIDES
    chunks = chunks_of(features)
    widths = [sum(chunk) for chunk in chunks]
    count = len(widths)

    ids, probs = route_ids.T, route_probs.T
    call = Chain()
    if direct:
        relay = Relay(call, grad_out, ids, probs, held, capacity, widths)
        flat, saved = relay.flat, hidden[0]
    else:
        flat, arrived = exchanged(grad_out, ids, probs, groups, held, capacity, widths)
        saved = hidden[0].transpose(1, 0, 2, 3).reshape(1, held, per_expert, units)
    turned = call(
        functools.partial(turn_kernel, dp),
        sds((held, 2, across, share, per_expert), BF16),
        saved,
    )
    starts = [sum(widths[:c]) for c in range(count)]
    state = {"raw": None, "grad": None}
    summed = []

    def accumulated(c):
        parts, width, final = arrived[c], widths[c], c == count - 1
        if final:
            outs = [sds(saved.shape, BF16), sds((held, per_expert), F32)]
        else:
            outs = [sds((held, per_expert, units), F32)]
        extra = ([state["raw"]] if c else []) + ([saved] if final else [])
        kernel = functools.partial(raw_kernel, len(parts), starts[c], final)
        made = call(
            kernel,
            outs,
            w_down,
            *parts,
            *extra,
        )
        state["raw"] = made if final else made[0]

    def termed(c, at, width):
        piece = sds((across, held, share, width), BF16)
        after = summed[0][2] if summed and at == 0 and direct else ()
        if direct and not c:
            after = [early[0][1]]
        kernel = functools.partial(term_kernel, at)
        keep, give = call(kernel, [piece, piece], turned, *arrived[c], after=after)
        got = lax.ppermute(give, "dp", [(i, i ^ 1) for i in range(dp)])
        return keep, got, starts[c] + at

    def paired(keep, got, start):
        cuts = cuts_of(share, not summed)
        pieces = [sds((held, rows, keep.shape[3]), BF16) for rows in cuts]
        pairs = call(functools.partial(pair_kernel, cuts), pieces * (across - 1), keep, got)
        others = []
        for i, pair in enumerate(pairs):
            step = 1 + i // len(cuts)
            shift = [(2 * r + k, 2 * ((r + step) % across) + k) for r in range(across) for k in range(2)]
            others.append(lax.ppermute(pair, "dp", shift))
        summed.append((keep, got, others, start))

    def finished(first, last):
        before = [] if state["grad"] is None else [state["grad"]]
        done = summed[first:last]
        args = [x for keep, got, others, _ in done for x in (keep, got, *others)]
        cuts = [cuts_of(share, j == 0) for j in range(first, last)]
        state["grad"], _ = call(
            functools.partial(last_kernel, cuts, done[0][3]),
            [sds((share, held, features), F32), sds((8, 128), F32)],
            *args,
            *before,
            in_specs=[VMEM] * len(args) + [ANY] * len(before),
            out_specs=[ANY, VMEM],
            input_output_aliases={len(args): 0} if before else {},
            scratch_shapes=[
                pltpu.VMEM((share, held, sum(keep.shape[3] for keep, *_ in done)), F32),
                pltpu.SemaphoreType.DMA,
            ],
        )

    if direct:
        arrived, early = [], relay.early(0)
    for c, chunk in enumerate(chunks):
        if direct:
            arrived.append(relay.late(c, early))
            if c + 1 < count:
                early = relay.early(c + 1)
        if c >= 1:
            accumulated(c - 1)
        terms = [termed(c, sum(chunk[:i]), width) for i, width in enumerate(chunk)]
        for term in terms:
            paired(*term)
    accumulated(count - 1)
    for j in range(len(summed) - 1):
        finished(j, j + 1)
    hidden_grad, sums = state["raw"]

    if direct:
        swap = [(i, i ^ 1) for i in range(groups)]
        both = jnp.stack([sums, lax.ppermute(sums, "expert", swap)])
        returned = [both] + [
            lax.ppermute(both, "expert", [(moved(i, d, 0), i) for i in range(groups)])
            for d in range(1, LINE)
        ]
    else:
        sums = sums.reshape(held, groups, capacity).transpose(1, 0, 2).reshape(groups, -1)
        hidden_grad = hidden_grad.reshape(held, groups, capacity, units).transpose(1, 0, 2, 3)
        returned = lax.all_to_all(sums, "expert", split_axis=0, concat_axis=0, tiled=True)
        returned = [returned.reshape(-1, 128)]
    prob_grad, call.last = call(
        functools.partial(prob_kernel, direct, capacity),
        [sds((chosen, tokens), F32), sds((8, 128), F32)],
        flat,
        probs,
        *returned,
    )
    prob_grad = prob_grad.T
    finished(len(summed) - 1, len(summed))
    weight_grad = state["grad"]
    return (hidden_grad.reshape(hidden.shape), prob_grad, weight_grad)


def solution(mesh):
    in_specs = (
        P(("dp", "expert"), None),
        P(("dp", "expert"), None),
        P(("dp", "expert"), None),
        P("dp", None, "expert", None, None),
        P("expert", None, None),
    )
    out_specs = (
        P("dp", None, "expert", None, None),
        P(("dp", "expert"), None),
        P("dp", "expert", None),
    )
    return jax.shard_map(body, mesh=mesh, in_specs=in_specs, out_specs=out_specs, check_vma=False)
```

```python
import functools

import jax
import jax.numpy as jnp
from jax import lax
from jax.experimental import pallas as pl
from jax.experimental.pallas import tpu as pltpu
from jax.sharding import PartitionSpec as P

F32, BF16, I32 = jnp.float32, jnp.bfloat16, jnp.int32
VMEM = pl.BlockSpec(memory_space=pltpu.VMEM)
ANY = pl.BlockSpec(memory_space=pl.ANY)
HBM = pl.BlockSpec(memory_space=pltpu.HBM)

LINE, SIDES = 4, 2
BACK = (0, 1, 3, 2)
INFO = 16


def moved(me, places, side):
    return (me // SIDES + places) % LINE * SIDES + (me % SIDES ^ side)


def source_of(me, part):
    return moved(me, LINE - BACK[part % LINE], part // LINE)


class Chain:
    def __init__(self):
        self.last = None

    def __call__(self, kernel, outs, *args, in_specs=None, keep=True, after=(), room=24, **kw):
        in_specs = list(in_specs or [VMEM] * len(args))
        count = len(args)
        body = kernel
        unread = [*after] if self.last is None else [self.last, *after]
        if unread:
            args, in_specs = (*args, *unread), in_specs + [ANY] * len(unread)

            def body(*refs):
                kernel(*refs[:count], *refs[count + len(unread) :])

        made = pl.pallas_call(
            body,
            out_shape=outs,
            in_specs=in_specs,
            compiler_params=pltpu.CompilerParams(vmem_limit_bytes=room * 1024 * 1024),
            cost_estimate=pl.CostEstimate(flops=1, bytes_accessed=1, transcendentals=0),
            **kw,
        )(*args)
        if keep:
            self.last = min(jax.tree.leaves(made), key=lambda x: x.size)
        return made


def gates_of(probs):
    total = jnp.sum(probs, axis=0, keepdims=True)
    gates = probs / total
    return total, gates, gates.astype(BF16).astype(F32)


def slots_of(ids, experts):
    chosen, tokens = ids.shape
    expert = lax.broadcasted_iota(I32, (experts, tokens), 0)
    named = [ids[k : k + 1] == expert for k in range(chosen)]
    hits = functools.reduce(jnp.add, [n.astype(F32) for n in named]).astype(BF16)
    row = lax.broadcasted_iota(I32, (tokens, tokens), 0)
    earlier = (row < lax.broadcasted_iota(I32, (tokens, tokens), 1)).astype(F32).astype(BF16)
    before = jnp.dot(hits, earlier, preferred_element_type=F32)
    return [jnp.sum(jnp.where(n, before, 0.0), axis=0, keepdims=True) for n in named]


def begin_kernel(experts, capacity, ids_ref, probs_ref, rows_ref, flat_ref, *refs):
    out_refs, (ids_got, probs_got, sems) = refs[:-3], refs[-3:]
    chosen, tokens = ids_got.shape
    out_ref, width = out_refs[0], out_refs[0].shape[1]
    copies = [
        pltpu.make_async_copy(ids_ref, ids_got, sems.at[0]),
        pltpu.make_async_copy(probs_ref, probs_got, sems.at[1]),
    ]
    start = 0
    for i, ref in enumerate(out_refs):
        rows = rows_ref.at[:, start : start + ref.shape[1]]
        copies.append(pltpu.make_async_copy(rows, ref.at[:tokens], sems.at[2 + i]))
        start += ref.shape[1]
    for copy in copies:
        copy.start()
    for copy in copies:
        copy.wait()
    ids = ids_got[...]
    _, _, word = gates_of(probs_got[...])
    slots = slots_of(ids, experts)
    for k in range(chosen):
        flat_ref[k : k + 1, :] = ids[k : k + 1] * capacity + slots[k].astype(I32)
    rest = jnp.zeros((INFO - 3 * chosen, tokens), F32)
    info = jnp.concatenate([ids.astype(F32), *slots, word, rest], axis=0).astype(BF16)
    out_ref[tokens:, :tokens] = info
    if width > tokens:
        out_ref[tokens:, tokens:] = jnp.zeros((INFO, width - tokens), BF16)


def places(held, capacity, chosen, ref, place_ref):
    tokens = place_ref.shape[1]
    rows = held * capacity
    me = lax.axis_index("expert")
    local = lax.broadcasted_iota(I32, (rows, tokens), 0)
    info = ref[tokens:, :tokens].astype(F32)
    flat = (info[:chosen] * capacity + info[chosen : 2 * chosen]).astype(I32)
    word = info[2 * chosen : 3 * chosen]
    for side in range(SIDES):
        slot = local + (me ^ side) * rows
        hits = [jnp.where(flat[k : k + 1] == slot, word[k : k + 1], 0.0) for k in range(chosen)]
        place_ref[side * rows : (side + 1) * rows, :] = functools.reduce(jnp.add, hits).astype(BF16)


def pick(held, capacity, begin, block_refs, place_ref, out_refs):
    tokens = place_ref.shape[2]
    for j, ref in enumerate(block_refs):
        scaled = jnp.dot(place_ref[begin + j], ref[:tokens, :], preferred_element_type=F32).astype(BF16)
        for side, out_ref in enumerate(out_refs):
            for e in range(held):
                at = (side * held + e) * capacity
                out_ref[e, j * capacity : (j + 1) * capacity, :] = scaled[at : at + capacity]


def pick_kernel(held, capacity, chosen, first, at, count, *refs):
    block_refs, refs = refs[:count], refs[count:]
    if first:
        mine_ref, other_ref, place_ref = refs
        for j, ref in enumerate(block_refs):
            places(held, capacity, chosen, ref, place_ref.at[j])
    else:
        place_ref, mine_ref, other_ref = refs
    pick(held, capacity, at, block_refs, place_ref, (mine_ref, other_ref))


def turn_kernel(dp, hidden_ref, *refs):
    out_ref, refs = refs[-1], refs[:-1]
    parts, held, _, units = hidden_ref.shape
    share, across = units // dp, dp // 2
    me = lax.axis_index("expert") if parts > 1 else 0
    mine = lax.axis_index("dp")
    core, row = mine % 2, mine // 2
    for e in range(held):
        sources = [source_of(me, p) if parts > 1 else 0 for p in range(parts)]
        stacked = jnp.concatenate([hidden_ref[source, e] for source in sources], axis=0)
        turned = stacked.T
        for piece in range(dp):
            other = (piece % 2) ^ core
            step = (piece // 2 - row + across) % across
            out_ref[e, other, step] = turned[piece * share : (piece + 1) * share]


def stacked_rows(refs, e, at):
    rows = [ref[e, :, at] for ref in refs]
    return rows[0] if len(rows) == 1 else jnp.concatenate(rows, axis=0)


def term_kernel(start, turned_ref, *refs):
    part_refs, keep_ref, give_ref = refs[:-2], refs[-2], refs[-1]
    held, _, across, share, slots = turned_ref.shape
    at = slice(start, start + keep_ref.shape[3])
    for e in range(held):
        scaled = stacked_rows(part_refs, e, at)
        for other, ref in ((1, give_ref), (0, keep_ref)):
            left = turned_ref[e, other].reshape(across * share, slots)
            term = jnp.dot(left, scaled, preferred_element_type=F32).astype(BF16)
            for step in range(across):
                ref[step, e] = term[step * share : (step + 1) * share]


def pair_kernel(cuts, keep_ref, got_ref, *out_refs):
    out_refs = iter(out_refs)
    for step in range(1, keep_ref.shape[0]):
        start = 0
        for rows in cuts:
            at = slice(start, start + rows)
            pair = keep_ref[step, :, at].astype(F32) + got_ref[step, :, at].astype(F32)
            next(out_refs)[...] = pair.astype(BF16)
            start += rows


def last_kernel(cuts, start, *refs):
    out_ref, mark_ref, total_ref, sem = refs[-4:]
    mark_ref[...] = jnp.zeros(mark_ref.shape, F32)
    column = 0
    for rows_of in cuts:
        keep_ref, got_ref, *refs = refs
        across, held, _, width = keep_ref.shape
        others, refs = refs[: len(rows_of) * (across - 1)], refs[len(rows_of) * (across - 1) :]
        columns = slice(column, column + width)
        column += width
        for e in range(held):
            row = 0
            for cut, rows in enumerate(rows_of):
                at = slice(row, row + rows)
                total = keep_ref[0, e, at].astype(F32) + got_ref[0, e, at].astype(F32)
                for ref in others[cut :: len(rows_of)]:
                    total = total + ref[e].astype(F32)
                total_ref[at, e, columns] = total
                row += rows
    copy = pltpu.make_async_copy(
        total_ref, out_ref.at[:, :, start : start + total_ref.shape[2]], sem
    )
    copy.start()
    copy.wait()


def raw_kernel(parts, start, final, weight_ref, *refs):
    part_refs, refs = refs[:parts], refs[parts:]
    if start:
        acc_ref, refs = refs[0], refs[1:]
    width = part_refs[0].shape[2]
    for e in range(weight_ref.shape[0]):
        raw = lax.dot_general(
            stacked_rows(part_refs, e, slice(None)),
            weight_ref[e, :, start : start + width],
            (((1,), (1,)), ((), ())),
            preferred_element_type=F32,
        )
        if start:
            raw = raw + acc_ref[e]
        if not final:
            refs[0][e] = raw
            continue
        hidden_ref, grad_ref, sums_ref = refs
        sources, _, own, units = hidden_ref.shape
        me = lax.axis_index("expert") if sources > 1 else 0
        folds = []
        for part in range(sources):
            source = source_of(me, part) if sources > 1 else 0
            block = raw[part * own : (part + 1) * own]
            grad_ref[source, e] = block.astype(BF16)
            product = block * hidden_ref[source, e].astype(F32)
            folds.append(
                functools.reduce(jnp.add, [product[:, i : i + 128] for i in range(0, units, 128)])
            )
        folded = jnp.concatenate(folds, axis=0) if len(folds) > 1 else folds[0]
        sums_ref[e : e + 1, :] = jnp.sum(folded.T, axis=0, keepdims=True)


def prob_kernel(direct, capacity, flat_ref, probs_ref, *refs):
    out_ref, mark_ref = refs[-2:]
    mark_ref[...] = jnp.zeros(mark_ref.shape, F32)
    chosen, tokens = flat_ref.shape
    if direct:
        values = []
        for q in range(LINE * SIDES):
            at = (BACK.index(q // SIDES) + LINE * (q % SIDES)) * capacity
            ref = refs[q // SIDES]
            values += [ref[q % SIDES, e : e + 1, at : at + capacity] for e in range(ref.shape[1])]
        lanes = 128 // capacity
        values = jnp.concatenate(
            [
                jnp.concatenate([v.reshape(1, capacity) for v in values[i : i + lanes]], axis=1)
                for i in range(0, len(values), lanes)
            ],
            axis=0,
        )
        me = lax.axis_index("expert")
    else:
        values = refs[0][...]
        me = 0
    lines = values.shape[0]
    spare = jnp.zeros((-lines % 8, 128), F32)
    columns = jnp.concatenate([values, spare], axis=0).T if spare.size else values.T
    total, gates, word = gates_of(probs_ref[...])
    group = lines * 128 // (LINE * SIDES)
    picked = [jnp.zeros((1, tokens), F32) for _ in range(chosen)]
    for line in range(lines):
        at = lax.broadcasted_iota(I32, (128, tokens), 0) + line * 128
        q = at // group
        slot = (moved(me, q // SIDES, q % SIDES) if direct else q) * group + at % group
        for k in range(chosen):
            hit = jnp.where(flat_ref[k : k + 1, :] == slot, columns[:, line : line + 1], 0.0)
            picked[k] += jnp.sum(hit, axis=0, keepdims=True)
    picked = [picked[k] / word[k : k + 1] for k in range(chosen)]
    mixed = functools.reduce(jnp.add, [gates[k : k + 1] * picked[k] for k in range(chosen)])
    for k in range(chosen):
        out_ref[k : k + 1, :] = (picked[k] - mixed) / total


def chunks_of(features):
    unit = features // 16
    return [[6 * unit], [7 * unit, 3 * unit]]


def cuts_of(share, first):
    return [share // 3] * 3 if first else [share]


sds = jax.ShapeDtypeStruct


class Relay:
    def __init__(self, call, grad_out, ids, probs, held, capacity, widths):
        tokens, features = grad_out.shape
        self.call, self.held, self.capacity, self.widths = call, held, capacity, widths
        self.tokens, self.chosen, self.place = tokens, ids.shape[0], {}
        self.flat, *owns = call(
            functools.partial(begin_kernel, LINE * SIDES * held, capacity),
            [sds(ids.shape, I32)]
            + [sds((tokens + (0 if c else INFO), w), BF16) for c, w in enumerate(widths)],
            ids,
            probs,
            grad_out,
            in_specs=[HBM] * 3,
            scratch_shapes=[
                pltpu.VMEM(ids.shape, I32),
                pltpu.VMEM(probs.shape, F32),
                pltpu.SemaphoreType.DMA((2 + len(widths),)),
            ],
            room=60,
            keep=False,
        )
        self.blocks, self.passed = [], []
        for own in owns:
            self.leave(own)

    def leave(self, own):
        on, back = self.along(own, 1), self.along(own, LINE - 1)
        self.blocks.append([own, on, back])
        self.passed.append(self.along(on, 1))

    def along(self, block, places):
        pairs = [(i, moved(i, places, 0)) for i in range(LINE * SIDES)]
        return lax.ppermute(block, "expert", pairs)

    def pick(self, c, name, blocks, at=0):
        held, capacity, count = self.held, self.capacity, len(blocks)
        rows = [sds((held, count * capacity, self.widths[c]), BF16)] * SIDES
        kernel = functools.partial(pick_kernel, held, capacity, self.chosen, c == 0, at, count)
        if c == 0:
            place = sds((count, SIDES * held * capacity, self.tokens), BF16)
            mine, other, self.place[name] = self.call(kernel, [*rows, place], *blocks)
        else:
            mine, other = self.call(kernel, rows, *blocks, self.place[name])
        return mine, lax.ppermute(other, "expert", [(i, i ^ 1) for i in range(LINE * SIDES)])

    def early(self, c):
        if c == 0:
            return [self.pick(c, "early", self.blocks[c])]
        own = self.pick(c, "early", self.blocks[c][:1])
        return [own, self.pick(c, "early", self.blocks[c][1:], 1)]

    def late(self, c, early):
        picked = [*early, self.pick(c, "late", [self.passed[c]])]
        return [mine for mine, _ in picked] + [other for _, other in picked]


def exchanged(grad_out, ids, probs, groups, held, capacity, widths):
    tokens = grad_out.shape[0]
    experts = groups * held
    slots = experts * capacity
    _, _, word = gates_of(probs)
    flat = ids * capacity + jnp.concatenate(slots_of(ids, experts), axis=0).astype(I32)
    slot = lax.broadcasted_iota(I32, (slots, tokens), 0)
    place = sum(jnp.where(f == slot, w, 0.0) for f, w in zip(flat, word)).astype(BF16)
    arrived, start = [], 0
    for width in widths:
        rows = grad_out[:, start : start + width]
        sent = jnp.dot(place, rows, preferred_element_type=F32).astype(BF16)
        got = lax.all_to_all(
            sent.reshape(groups, held, capacity, width),
            "expert",
            split_axis=0,
            concat_axis=0,
            tiled=True,
        )
        arrived.append([got.transpose(1, 0, 2, 3).reshape(held, groups * capacity, width)])
        start += width
    return flat, arrived


def body(grad_out, route_ids, route_probs, hidden, w_down):
    groups = lax.axis_size("expert")
    dp = lax.axis_size("dp")
    held, units, features = w_down.shape
    capacity = hidden.shape[3]
    slots = groups * held * capacity
    per_expert = slots // held
    tokens, chosen = route_ids.shape
    share, across = units // dp, dp // 2
    direct = groups == LINE * SIDES
    chunks = chunks_of(features)
    widths = [sum(chunk) for chunk in chunks]
    count = len(widths)

    ids, probs = route_ids.T, route_probs.T
    call = Chain()
    if direct:
        relay = Relay(call, grad_out, ids, probs, held, capacity, widths)
        flat, saved = relay.flat, hidden[0]
    else:
        flat, arrived = exchanged(grad_out, ids, probs, groups, held, capacity, widths)
        saved = hidden[0].transpose(1, 0, 2, 3).reshape(1, held, per_expert, units)
    turned = call(
        functools.partial(turn_kernel, dp),
        sds((held, 2, across, share, per_expert), BF16),
        saved,
    )
    starts = [sum(widths[:c]) for c in range(count)]
    state = {"raw": None, "grad": None}
    summed = []

    def accumulated(c):
        parts, width, final = arrived[c], widths[c], c == count - 1
        if final:
            outs = [sds(saved.shape, BF16), sds((held, per_expert), F32)]
        else:
            outs = [sds((held, per_expert, units), F32)]
        extra = ([state["raw"]] if c else []) + ([saved] if final else [])
        kernel = functools.partial(raw_kernel, len(parts), starts[c], final)
        made = call(
            kernel,
            outs,
            w_down,
            *parts,
            *extra,
        )
        state["raw"] = made if final else made[0]

    def termed(c, at, width):
        piece = sds((across, held, share, width), BF16)
        after = summed[0][2] if summed and at == 0 and direct else ()
        if direct and not c:
            after = [early[0][1]]
        kernel = functools.partial(term_kernel, at)
        keep, give = call(kernel, [piece, piece], turned, *arrived[c], after=after)
        got = lax.ppermute(give, "dp", [(i, i ^ 1) for i in range(dp)])
        return keep, got, starts[c] + at

    def paired(keep, got, start):
        cuts = cuts_of(share, not summed)
        pieces = [sds((held, rows, keep.shape[3]), BF16) for rows in cuts]
        pairs = call(functools.partial(pair_kernel, cuts), pieces * (across - 1), keep, got)
        others = []
        for i, pair in enumerate(pairs):
            step = 1 + i // len(cuts)
            shift = [(2 * r + k, 2 * ((r + step) % across) + k) for r in range(across) for k in range(2)]
            others.append(lax.ppermute(pair, "dp", shift))
        summed.append((keep, got, others, start))

    def finished(first, last):
        before = [] if state["grad"] is None else [state["grad"]]
        done = summed[first:last]
        args = [x for keep, got, others, _ in done for x in (keep, got, *others)]
        cuts = [cuts_of(share, j == 0) for j in range(first, last)]
        state["grad"], _ = call(
            functools.partial(last_kernel, cuts, done[0][3]),
            [sds((share, held, features), F32), sds((8, 128), F32)],
            *args,
            *before,
            in_specs=[VMEM] * len(args) + [ANY] * len(before),
            out_specs=[ANY, VMEM],
            input_output_aliases={len(args): 0} if before else {},
            scratch_shapes=[
                pltpu.VMEM((share, held, sum(keep.shape[3] for keep, *_ in done)), F32),
                pltpu.SemaphoreType.DMA,
            ],
        )

    if direct:
        arrived, early = [], relay.early(0)
    for c, chunk in enumerate(chunks):
        if direct:
            arrived.append(relay.late(c, early))
            if c + 1 < count:
                early = relay.early(c + 1)
        if c >= 1:
            accumulated(c - 1)
        terms = [termed(c, sum(chunk[:i]), width) for i, width in enumerate(chunk)]
        for term in terms:
            paired(*term)
    accumulated(count - 1)
    for j in range(len(summed) - 1):
        finished(j, j + 1)
    hidden_grad, sums = state["raw"]

    if direct:
        swap = [(i, i ^ 1) for i in range(groups)]
        both = jnp.stack([sums, lax.ppermute(sums, "expert", swap)])
        returned = [both] + [
            lax.ppermute(both, "expert", [(moved(i, d, 0), i) for i in range(groups)])
            for d in range(1, LINE)
        ]
    else:
        sums = sums.reshape(held, groups, capacity).transpose(1, 0, 2).reshape(groups, -1)
        hidden_grad = hidden_grad.reshape(held, groups, capacity, units).transpose(1, 0, 2, 3)
        returned = lax.all_to_all(sums, "expert", split_axis=0, concat_axis=0, tiled=True)
        returned = [returned.reshape(-1, 128)]
    prob_grad, call.last = call(
        functools.partial(prob_kernel, direct, capacity),
        [sds((chosen, tokens), F32), sds((8, 128), F32)],
        flat,
        probs,
        *returned,
    )
    prob_grad = prob_grad.T
    finished(len(summed) - 1, len(summed))
    weight_grad = state["grad"]
    return (hidden_grad.reshape(hidden.shape), prob_grad, weight_grad)


def solution(mesh):
    in_specs = (
        P(("dp", "expert"), None),
        P(("dp", "expert"), None),
        P(("dp", "expert"), None),
        P("dp", None, "expert", None, None),
        P("expert", None, None),
    )
    out_specs = (
        P("dp", None, "expert", None, None),
        P(("dp", "expert"), None),
        P("dp", "expert", None),
    )
    return jax.shard_map(body, mesh=mesh, in_specs=in_specs, out_specs=out_specs, check_vma=False)
```

```python
import functools

import jax
import jax.numpy as jnp
from jax import lax
from jax.experimental import pallas as pl
from jax.experimental.pallas import tpu as pltpu
from jax.sharding import PartitionSpec as P

F32, BF16, I32 = jnp.float32, jnp.bfloat16, jnp.int32
VMEM = pl.BlockSpec(memory_space=pltpu.VMEM)
ANY = pl.BlockSpec(memory_space=pl.ANY)
HBM = pl.BlockSpec(memory_space=pltpu.HBM)

LINE, SIDES = 4, 2
BACK = (0, 1, 3, 2)
INFO = 16


def moved(me, places, side):
    return (me // SIDES + places) % LINE * SIDES + (me % SIDES ^ side)


def source_of(me, part):
    return moved(me, LINE - BACK[part % LINE], part // LINE)


class Chain:
    def __init__(self):
        self.last = None

    def __call__(self, kernel, outs, *args, in_specs=None, keep=True, after=(), room=24, **kw):
        in_specs = list(in_specs or [VMEM] * len(args))
        count = len(args)
        body = kernel
        unread = [*after] if self.last is None else [self.last, *after]
        if unread:
            args, in_specs = (*args, *unread), in_specs + [ANY] * len(unread)

            def body(*refs):
                kernel(*refs[:count], *refs[count + len(unread) :])

        made = pl.pallas_call(
            body,
            out_shape=outs,
            in_specs=in_specs,
            compiler_params=pltpu.CompilerParams(vmem_limit_bytes=room * 1024 * 1024),
            cost_estimate=pl.CostEstimate(flops=1, bytes_accessed=1, transcendentals=0),
            **kw,
        )(*args)
        if keep:
            self.last = min(jax.tree.leaves(made), key=lambda x: x.size)
        return made


def gates_of(probs):
    total = jnp.sum(probs, axis=0, keepdims=True)
    gates = probs / total
    return total, gates, gates.astype(BF16).astype(F32)


def slots_of(ids, experts):
    chosen, tokens = ids.shape
    expert = lax.broadcasted_iota(I32, (experts, tokens), 0)
    named = [ids[k : k + 1] == expert for k in range(chosen)]
    hits = functools.reduce(jnp.add, [n.astype(F32) for n in named]).astype(BF16)
    row = lax.broadcasted_iota(I32, (tokens, tokens), 0)
    earlier = (row < lax.broadcasted_iota(I32, (tokens, tokens), 1)).astype(F32).astype(BF16)
    before = jnp.dot(hits, earlier, preferred_element_type=F32)
    return [jnp.sum(jnp.where(n, before, 0.0), axis=0, keepdims=True) for n in named]


def begin_kernel(experts, capacity, ids_ref, probs_ref, rows_ref, flat_ref, out_ref, *scratch):
    ids_got, probs_got, sems = scratch
    chosen, tokens = ids_got.shape
    width = out_ref.shape[1]
    copies = [
        pltpu.make_async_copy(ids_ref, ids_got, sems.at[0]),
        pltpu.make_async_copy(probs_ref, probs_got, sems.at[1]),
        pltpu.make_async_copy(rows_ref.at[:, :width], out_ref.at[:tokens], sems.at[2]),
    ]
    for copy in copies:
        copy.start()
    for copy in copies:
        copy.wait()
    ids = ids_got[...]
    _, _, word = gates_of(probs_got[...])
    slots = slots_of(ids, experts)
    for k in range(chosen):
        flat_ref[k : k + 1, :] = ids[k : k + 1] * capacity + slots[k].astype(I32)
    rest = jnp.zeros((INFO - 3 * chosen, tokens), F32)
    info = jnp.concatenate([ids.astype(F32), *slots, word, rest], axis=0).astype(BF16)
    out_ref[tokens:, :tokens] = info
    if width > tokens:
        out_ref[tokens:, tokens:] = jnp.zeros((INFO, width - tokens), BF16)


def places(held, capacity, chosen, ref, place_ref):
    tokens = place_ref.shape[1]
    rows = held * capacity
    me = lax.axis_index("expert")
    local = lax.broadcasted_iota(I32, (rows, tokens), 0)
    info = ref[tokens:, :tokens].astype(F32)
    flat = (info[:chosen] * capacity + info[chosen : 2 * chosen]).astype(I32)
    word = info[2 * chosen : 3 * chosen]
    for side in range(SIDES):
        slot = local + (me ^ side) * rows
        hits = [jnp.where(flat[k : k + 1] == slot, word[k : k + 1], 0.0) for k in range(chosen)]
        place_ref[side * rows : (side + 1) * rows, :] = functools.reduce(jnp.add, hits).astype(BF16)


def pick(held, capacity, begin, block_refs, place_ref, out_refs):
    tokens = place_ref.shape[2]
    for j, ref in enumerate(block_refs):
        scaled = jnp.dot(place_ref[begin + j], ref[:tokens, :], preferred_element_type=F32).astype(BF16)
        for side, out_ref in enumerate(out_refs):
            for e in range(held):
                at = (side * held + e) * capacity
                out_ref[e, j * capacity : (j + 1) * capacity, :] = scaled[at : at + capacity]


def pick_kernel(held, capacity, chosen, first, at, count, *refs):
    block_refs, refs = refs[:count], refs[count:]
    if first:
        mine_ref, other_ref, place_ref = refs
        for j, ref in enumerate(block_refs):
            places(held, capacity, chosen, ref, place_ref.at[j])
    else:
        place_ref, mine_ref, other_ref = refs
    pick(held, capacity, at, block_refs, place_ref, (mine_ref, other_ref))


def turn_kernel(dp, hidden_ref, *refs):
    out_ref, refs = refs[-1], refs[:-1]
    parts, held, _, units = hidden_ref.shape
    share, across = units // dp, dp // 2
    me = lax.axis_index("expert") if parts > 1 else 0
    mine = lax.axis_index("dp")
    core, row = mine % 2, mine // 2
    for e in range(held):
        sources = [source_of(me, p) if parts > 1 else 0 for p in range(parts)]
        stacked = jnp.concatenate([hidden_ref[source, e] for source in sources], axis=0)
        turned = stacked.T
        for piece in range(dp):
            other = (piece % 2) ^ core
            step = (piece // 2 - row + across) % across
            out_ref[e, other, step] = turned[piece * share : (piece + 1) * share]


def cut_kernel(start, rows_ref, *refs):
    out_refs, sems = refs[:-1], refs[-1]
    copies = []
    for i, ref in enumerate(out_refs):
        at = slice(start, start + ref.shape[1])
        copies.append(pltpu.make_async_copy(rows_ref.at[:, at], ref, sems.at[i]))
        start += ref.shape[1]
    for copy in copies:
        copy.start()
    for copy in copies:
        copy.wait()


def stacked_rows(refs, e, at):
    rows = [ref[e, :, at] for ref in refs]
    return rows[0] if len(rows) == 1 else jnp.concatenate(rows, axis=0)


def term_kernel(start, turned_ref, *refs):
    part_refs, keep_ref, give_ref = refs[:-2], refs[-2], refs[-1]
    held, _, across, share, slots = turned_ref.shape
    at = slice(start, start + keep_ref.shape[3])
    for e in range(held):
        scaled = stacked_rows(part_refs, e, at)
        for other, ref in ((1, give_ref), (0, keep_ref)):
            left = turned_ref[e, other].reshape(across * share, slots)
            term = jnp.dot(left, scaled, preferred_element_type=F32).astype(BF16)
            for step in range(across):
                ref[step, e] = term[step * share : (step + 1) * share]


def pair_kernel(cuts, keep_ref, got_ref, *out_refs):
    out_refs = iter(out_refs)
    for step in range(1, keep_ref.shape[0]):
        start = 0
        for rows in cuts:
            at = slice(start, start + rows)
            pair = keep_ref[step, :, at].astype(F32) + got_ref[step, :, at].astype(F32)
            next(out_refs)[...] = pair.astype(BF16)
            start += rows


def last_kernel(cuts, start, *refs):
    out_ref, mark_ref, total_ref, sem = refs[-4:]
    mark_ref[...] = jnp.zeros(mark_ref.shape, F32)
    column = 0
    for rows_of in cuts:
        keep_ref, got_ref, *refs = refs
        across, held, _, width = keep_ref.shape
        others, refs = refs[: len(rows_of) * (across - 1)], refs[len(rows_of) * (across - 1) :]
        columns = slice(column, column + width)
        column += width
        for e in range(held):
            row = 0
            for cut, rows in enumerate(rows_of):
                at = slice(row, row + rows)
                total = keep_ref[0, e, at].astype(F32) + got_ref[0, e, at].astype(F32)
                for ref in others[cut :: len(rows_of)]:
                    total = total + ref[e].astype(F32)
                total_ref[at, e, columns] = total
                row += rows
    copy = pltpu.make_async_copy(
        total_ref, out_ref.at[:, :, start : start + total_ref.shape[2]], sem
    )
    copy.start()
    copy.wait()


def raw_kernel(parts, start, final, weight_ref, *refs):
    part_refs, refs = refs[:parts], refs[parts:]
    if start:
        acc_ref, refs = refs[0], refs[1:]
    width = part_refs[0].shape[2]
    for e in range(weight_ref.shape[0]):
        raw = lax.dot_general(
            stacked_rows(part_refs, e, slice(None)),
            weight_ref[e, :, start : start + width],
            (((1,), (1,)), ((), ())),
            preferred_element_type=F32,
        )
        if start:
            raw = raw + acc_ref[e]
        if not final:
            refs[0][e] = raw
            continue
        hidden_ref, grad_ref, sums_ref = refs
        sources, _, own, units = hidden_ref.shape
        me = lax.axis_index("expert") if sources > 1 else 0
        folds = []
        for part in range(sources):
            source = source_of(me, part) if sources > 1 else 0
            block = raw[part * own : (part + 1) * own]
            grad_ref[source, e] = block.astype(BF16)
            product = block * hidden_ref[source, e].astype(F32)
            folds.append(
                functools.reduce(jnp.add, [product[:, i : i + 128] for i in range(0, units, 128)])
            )
        folded = jnp.concatenate(folds, axis=0) if len(folds) > 1 else folds[0]
        sums_ref[e : e + 1, :] = jnp.sum(folded.T, axis=0, keepdims=True)


def prob_kernel(direct, capacity, flat_ref, probs_ref, *refs):
    out_ref, mark_ref = refs[-2:]
    mark_ref[...] = jnp.zeros(mark_ref.shape, F32)
    chosen, tokens = flat_ref.shape
    if direct:
        values = []
        for q in range(LINE * SIDES):
            at = (BACK.index(q // SIDES) + LINE * (q % SIDES)) * capacity
            ref = refs[q // SIDES]
            values += [ref[q % SIDES, e : e + 1, at : at + capacity] for e in range(ref.shape[1])]
        lanes = 128 // capacity
        values = jnp.concatenate(
            [
                jnp.concatenate([v.reshape(1, capacity) for v in values[i : i + lanes]], axis=1)
                for i in range(0, len(values), lanes)
            ],
            axis=0,
        )
        me = lax.axis_index("expert")
    else:
        values = refs[0][...]
        me = 0
    lines = values.shape[0]
    spare = jnp.zeros((-lines % 8, 128), F32)
    columns = jnp.concatenate([values, spare], axis=0).T if spare.size else values.T
    total, gates, word = gates_of(probs_ref[...])
    group = lines * 128 // (LINE * SIDES)
    picked = [jnp.zeros((1, tokens), F32) for _ in range(chosen)]
    for line in range(lines):
        at = lax.broadcasted_iota(I32, (128, tokens), 0) + line * 128
        q = at // group
        slot = (moved(me, q // SIDES, q % SIDES) if direct else q) * group + at % group
        for k in range(chosen):
            hit = jnp.where(flat_ref[k : k + 1, :] == slot, columns[:, line : line + 1], 0.0)
            picked[k] += jnp.sum(hit, axis=0, keepdims=True)
    picked = [picked[k] / word[k : k + 1] for k in range(chosen)]
    mixed = functools.reduce(jnp.add, [gates[k : k + 1] * picked[k] for k in range(chosen)])
    for k in range(chosen):
        out_ref[k : k + 1, :] = (picked[k] - mixed) / total


def chunks_of(features):
    unit = features // 16
    return [[6 * unit], [6 * unit, 4 * unit]]


def cuts_of(share, first):
    half = 16 * (share // 32)
    return [half, share - half] if first else [share]


sds = jax.ShapeDtypeStruct


class Relay:
    def __init__(self, call, grad_out, ids, probs, held, capacity, widths):
        tokens, features = grad_out.shape
        self.call, self.held, self.capacity, self.widths = call, held, capacity, widths
        self.tokens, self.chosen, self.place = tokens, ids.shape[0], {}
        self.flat, first = call(
            functools.partial(begin_kernel, LINE * SIDES * held, capacity),
            [sds(ids.shape, I32), sds((tokens + INFO, widths[0]), BF16)],
            ids,
            probs,
            grad_out,
            in_specs=[HBM] * 3,
            scratch_shapes=[
                pltpu.VMEM(ids.shape, I32),
                pltpu.VMEM(probs.shape, F32),
                pltpu.SemaphoreType.DMA((3,)),
            ],
            room=60,
            keep=False,
        )
        self.blocks, self.passed = [], []
        self.leave(first)
        rest = call(
            functools.partial(cut_kernel, widths[0]),
            [sds((tokens, w), BF16) for w in widths[1:]],
            grad_out,
            in_specs=[HBM],
            scratch_shapes=[pltpu.SemaphoreType.DMA((len(widths) - 1,))],
            after=[self.blocks[0][1]],
        )
        for own in rest:
            self.leave(own)

    def leave(self, own):
        on, back = self.along(own, 1), self.along(own, LINE - 1)
        self.blocks.append([own, on, back])
        self.passed.append(self.along(on, 1))

    def along(self, block, places):
        pairs = [(i, moved(i, places, 0)) for i in range(LINE * SIDES)]
        return lax.ppermute(block, "expert", pairs)

    def pick(self, c, name, blocks, at=0):
        held, capacity, count = self.held, self.capacity, len(blocks)
        rows = [sds((held, count * capacity, self.widths[c]), BF16)] * SIDES
        kernel = functools.partial(pick_kernel, held, capacity, self.chosen, c == 0, at, count)
        if c == 0:
            place = sds((count, SIDES * held * capacity, self.tokens), BF16)
            mine, other, self.place[name] = self.call(kernel, [*rows, place], *blocks)
        else:
            mine, other = self.call(kernel, rows, *blocks, self.place[name])
        return mine, lax.ppermute(other, "expert", [(i, i ^ 1) for i in range(LINE * SIDES)])

    def early(self, c):
        if c == 0:
            return [self.pick(c, "early", self.blocks[c])]
        own = self.pick(c, "early", self.blocks[c][:1])
        return [own, self.pick(c, "early", self.blocks[c][1:], 1)]

    def late(self, c, early):
        picked = [*early, self.pick(c, "late", [self.passed[c]])]
        return [mine for mine, _ in picked] + [other for _, other in picked]


def exchanged(grad_out, ids, probs, groups, held, capacity, widths):
    tokens = grad_out.shape[0]
    experts = groups * held
    slots = experts * capacity
    _, _, word = gates_of(probs)
    flat = ids * capacity + jnp.concatenate(slots_of(ids, experts), axis=0).astype(I32)
    slot = lax.broadcasted_iota(I32, (slots, tokens), 0)
    place = sum(jnp.where(f == slot, w, 0.0) for f, w in zip(flat, word)).astype(BF16)
    arrived, start = [], 0
    for width in widths:
        rows = grad_out[:, start : start + width]
        sent = jnp.dot(place, rows, preferred_element_type=F32).astype(BF16)
        got = lax.all_to_all(
            sent.reshape(groups, held, capacity, width),
            "expert",
            split_axis=0,
            concat_axis=0,
            tiled=True,
        )
        arrived.append([got.transpose(1, 0, 2, 3).reshape(held, groups * capacity, width)])
        start += width
    return flat, arrived


def body(grad_out, route_ids, route_probs, hidden, w_down):
    groups = lax.axis_size("expert")
    dp = lax.axis_size("dp")
    held, units, features = w_down.shape
    capacity = hidden.shape[3]
    slots = groups * held * capacity
    per_expert = slots // held
    tokens, chosen = route_ids.shape
    share, across = units // dp, dp // 2
    direct = groups == LINE * SIDES
    chunks = chunks_of(features)
    widths = [sum(chunk) for chunk in chunks]
    count = len(widths)

    ids, probs = route_ids.T, route_probs.T
    call = Chain()
    if direct:
        relay = Relay(call, grad_out, ids, probs, held, capacity, widths)
        flat, saved = relay.flat, hidden[0]
    else:
        flat, arrived = exchanged(grad_out, ids, probs, groups, held, capacity, widths)
        saved = hidden[0].transpose(1, 0, 2, 3).reshape(1, held, per_expert, units)
    turned = call(
        functools.partial(turn_kernel, dp),
        sds((held, 2, across, share, per_expert), BF16),
        saved,
    )
    starts = [sum(widths[:c]) for c in range(count)]
    state = {"raw": None, "grad": None}
    summed = []

    def accumulated(c):
        parts, width, final = arrived[c], widths[c], c == count - 1
        if final:
            outs = [sds(saved.shape, BF16), sds((held, per_expert), F32)]
        else:
            outs = [sds((held, per_expert, units), F32)]
        extra = ([state["raw"]] if c else []) + ([saved] if final else [])
        kernel = functools.partial(raw_kernel, len(parts), starts[c], final)
        made = call(
            kernel,
            outs,
            w_down,
            *parts,
            *extra,
        )
        state["raw"] = made if final else made[0]

    def termed(c, at, width):
        piece = sds((across, held, share, width), BF16)
        after = summed[0][2] if summed and at == 0 and direct else ()
        if direct and not c:
            after = [early[0][1]]
        kernel = functools.partial(term_kernel, at)
        keep, give = call(kernel, [piece, piece], turned, *arrived[c], after=after)
        got = lax.ppermute(give, "dp", [(i, i ^ 1) for i in range(dp)])
        return keep, got, starts[c] + at

    def paired(keep, got, start):
        cuts = cuts_of(share, not summed)
        pieces = [sds((held, rows, keep.shape[3]), BF16) for rows in cuts]
        pairs = call(functools.partial(pair_kernel, cuts), pieces * (across - 1), keep, got)
        others = []
        for i, pair in enumerate(pairs):
            step = 1 + i // len(cuts)
            shift = [(2 * r + k, 2 * ((r + step) % across) + k) for r in range(across) for k in range(2)]
            others.append(lax.ppermute(pair, "dp", shift))
        summed.append((keep, got, others, start))

    def finished(first, last):
        before = [] if state["grad"] is None else [state["grad"]]
        done = summed[first:last]
        args = [x for keep, got, others, _ in done for x in (keep, got, *others)]
        cuts = [cuts_of(share, j == 0) for j in range(first, last)]
        state["grad"], _ = call(
            functools.partial(last_kernel, cuts, done[0][3]),
            [sds((share, held, features), F32), sds((8, 128), F32)],
            *args,
            *before,
            in_specs=[VMEM] * len(args) + [ANY] * len(before),
            out_specs=[ANY, VMEM],
            input_output_aliases={len(args): 0} if before else {},
            scratch_shapes=[
                pltpu.VMEM((share, held, sum(keep.shape[3] for keep, *_ in done)), F32),
                pltpu.SemaphoreType.DMA,
            ],
        )

    if direct:
        arrived, early = [], relay.early(0)
    for c, chunk in enumerate(chunks):
        if direct:
            arrived.append(relay.late(c, early))
            if c + 1 < count:
                early = relay.early(c + 1)
        if c >= 1:
            accumulated(c - 1)
        terms = [termed(c, sum(chunk[:i]), width) for i, width in enumerate(chunk)]
        for term in terms:
            paired(*term)
    accumulated(count - 1)
    for j in range(len(summed) - 1):
        finished(j, j + 1)
    hidden_grad, sums = state["raw"]

    if direct:
        swap = [(i, i ^ 1) for i in range(groups)]
        both = jnp.stack([sums, lax.ppermute(sums, "expert", swap)])
        returned = [both] + [
            lax.ppermute(both, "expert", [(moved(i, d, 0), i) for i in range(groups)])
            for d in range(1, LINE)
        ]
    else:
        sums = sums.reshape(held, groups, capacity).transpose(1, 0, 2).reshape(groups, -1)
        hidden_grad = hidden_grad.reshape(held, groups, capacity, units).transpose(1, 0, 2, 3)
        returned = lax.all_to_all(sums, "expert", split_axis=0, concat_axis=0, tiled=True)
        returned = [returned.reshape(-1, 128)]
    prob_grad, call.last = call(
        functools.partial(prob_kernel, direct, capacity),
        [sds((chosen, tokens), F32), sds((8, 128), F32)],
        flat,
        probs,
        *returned,
    )
    prob_grad = prob_grad.T
    finished(len(summed) - 1, len(summed))
    weight_grad = state["grad"]
    return (hidden_grad.reshape(hidden.shape), prob_grad, weight_grad)


def solution(mesh):
    in_specs = (
        P(("dp", "expert"), None),
        P(("dp", "expert"), None),
        P(("dp", "expert"), None),
        P("dp", None, "expert", None, None),
        P("expert", None, None),
    )
    out_specs = (
        P("dp", None, "expert", None, None),
        P(("dp", "expert"), None),
        P("dp", "expert", None),
    )
    return jax.shard_map(body, mesh=mesh, in_specs=in_specs, out_specs=out_specs, check_vma=False)
```

```python
import functools

import jax
import jax.numpy as jnp
from jax import lax
from jax.experimental import pallas as pl
from jax.experimental.pallas import tpu as pltpu
from jax.sharding import PartitionSpec as P

F32, BF16, I32 = jnp.float32, jnp.bfloat16, jnp.int32
VMEM = pl.BlockSpec(memory_space=pltpu.VMEM)
ANY = pl.BlockSpec(memory_space=pl.ANY)
HBM = pl.BlockSpec(memory_space=pltpu.HBM)

LINE, SIDES = 4, 2
BACK = (0, 1, 3, 2)
INFO = 16


def moved(me, places, side):
    return (me // SIDES + places) % LINE * SIDES + (me % SIDES ^ side)


def source_of(me, part):
    return moved(me, LINE - BACK[part % LINE], part // LINE)


class Chain:
    def __init__(self):
        self.last = None

    def __call__(self, kernel, outs, *args, in_specs=None, keep=True, after=(), room=24, **kw):
        in_specs = list(in_specs or [VMEM] * len(args))
        count = len(args)
        body = kernel
        unread = [*after] if self.last is None else [self.last, *after]
        if unread:
            args, in_specs = (*args, *unread), in_specs + [ANY] * len(unread)

            def body(*refs):
                kernel(*refs[:count], *refs[count + len(unread) :])

        made = pl.pallas_call(
            body,
            out_shape=outs,
            in_specs=in_specs,
            compiler_params=pltpu.CompilerParams(vmem_limit_bytes=room * 1024 * 1024),
            cost_estimate=pl.CostEstimate(flops=1, bytes_accessed=1, transcendentals=0),
            **kw,
        )(*args)
        if keep:
            self.last = min(jax.tree.leaves(made), key=lambda x: x.size)
        return made


def gates_of(probs):
    total = jnp.sum(probs, axis=0, keepdims=True)
    gates = probs / total
    return total, gates, gates.astype(BF16).astype(F32)


def slots_of(ids, experts):
    chosen, tokens = ids.shape
    expert = lax.broadcasted_iota(I32, (experts, tokens), 0)
    named = [ids[k : k + 1] == expert for k in range(chosen)]
    hits = functools.reduce(jnp.add, [n.astype(F32) for n in named]).astype(BF16)
    row = lax.broadcasted_iota(I32, (tokens, tokens), 0)
    earlier = (row < lax.broadcasted_iota(I32, (tokens, tokens), 1)).astype(F32).astype(BF16)
    before = jnp.dot(hits, earlier, preferred_element_type=F32)
    return [jnp.sum(jnp.where(n, before, 0.0), axis=0, keepdims=True) for n in named]


def begin_kernel(experts, capacity, ids_ref, probs_ref, rows_ref, flat_ref, out_ref, *scratch):
    ids_got, probs_got, sems = scratch
    chosen, tokens = ids_got.shape
    width = out_ref.shape[1]
    copies = [
        pltpu.make_async_copy(ids_ref, ids_got, sems.at[0]),
        pltpu.make_async_copy(probs_ref, probs_got, sems.at[1]),
        pltpu.make_async_copy(rows_ref.at[:, :width], out_ref.at[:tokens], sems.at[2]),
    ]
    for copy in copies:
        copy.start()
    for copy in copies:
        copy.wait()
    ids = ids_got[...]
    _, _, word = gates_of(probs_got[...])
    slots = slots_of(ids, experts)
    for k in range(chosen):
        flat_ref[k : k + 1, :] = ids[k : k + 1] * capacity + slots[k].astype(I32)
    rest = jnp.zeros((INFO - 3 * chosen, tokens), F32)
    info = jnp.concatenate([ids.astype(F32), *slots, word, rest], axis=0).astype(BF16)
    out_ref[tokens:, :tokens] = info
    if width > tokens:
        out_ref[tokens:, tokens:] = jnp.zeros((INFO, width - tokens), BF16)


def places(held, capacity, chosen, ref, place_ref):
    tokens = place_ref.shape[1]
    rows = held * capacity
    me = lax.axis_index("expert")
    local = lax.broadcasted_iota(I32, (rows, tokens), 0)
    info = ref[tokens:, :tokens].astype(F32)
    flat = (info[:chosen] * capacity + info[chosen : 2 * chosen]).astype(I32)
    word = info[2 * chosen : 3 * chosen]
    for side in range(SIDES):
        slot = local + (me ^ side) * rows
        hits = [jnp.where(flat[k : k + 1] == slot, word[k : k + 1], 0.0) for k in range(chosen)]
        place_ref[side * rows : (side + 1) * rows, :] = functools.reduce(jnp.add, hits).astype(BF16)


def pick(held, capacity, begin, block_refs, place_ref, out_refs):
    tokens = place_ref.shape[2]
    for j, ref in enumerate(block_refs):
        scaled = jnp.dot(place_ref[begin + j], ref[:tokens, :], preferred_element_type=F32).astype(BF16)
        for side, out_ref in enumerate(out_refs):
            for e in range(held):
                at = (side * held + e) * capacity
                out_ref[e, j * capacity : (j + 1) * capacity, :] = scaled[at : at + capacity]


def pick_kernel(held, capacity, chosen, first, at, count, *refs):
    block_refs, refs = refs[:count], refs[count:]
    if first:
        mine_ref, other_ref, place_ref = refs
        for j, ref in enumerate(block_refs):
            places(held, capacity, chosen, ref, place_ref.at[j])
    else:
        place_ref, mine_ref, other_ref = refs
    pick(held, capacity, at, block_refs, place_ref, (mine_ref, other_ref))


def turn_kernel(dp, hidden_ref, *refs):
    out_ref, refs = refs[-1], refs[:-1]
    parts, held, _, units = hidden_ref.shape
    share, across = units // dp, dp // 2
    me = lax.axis_index("expert") if parts > 1 else 0
    mine = lax.axis_index("dp")
    core, row = mine % 2, mine // 2
    for e in range(held):
        sources = [source_of(me, p) if parts > 1 else 0 for p in range(parts)]
        stacked = jnp.concatenate([hidden_ref[source, e] for source in sources], axis=0)
        turned = stacked.T
        for piece in range(dp):
            other = (piece % 2) ^ core
            step = (piece // 2 - row + across) % across
            out_ref[e, other, step] = turned[piece * share : (piece + 1) * share]


def cut_kernel(start, rows_ref, *refs):
    out_refs, sems = refs[:-1], refs[-1]
    copies = []
    for i, ref in enumerate(out_refs):
        at = slice(start, start + ref.shape[1])
        copies.append(pltpu.make_async_copy(rows_ref.at[:, at], ref, sems.at[i]))
        start += ref.shape[1]
    for copy in copies:
        copy.start()
    for copy in copies:
        copy.wait()


def stacked_rows(refs, e, at):
    rows = [ref[e, :, at] for ref in refs]
    return rows[0] if len(rows) == 1 else jnp.concatenate(rows, axis=0)


def term_kernel(start, turned_ref, *refs):
    part_refs, keep_ref, give_ref = refs[:-2], refs[-2], refs[-1]
    held, _, across, share, slots = turned_ref.shape
    at = slice(start, start + keep_ref.shape[3])
    for e in range(held):
        scaled = stacked_rows(part_refs, e, at)
        for other, ref in ((1, give_ref), (0, keep_ref)):
            left = turned_ref[e, other].reshape(across * share, slots)
            term = jnp.dot(left, scaled, preferred_element_type=F32).astype(BF16)
            for step in range(across):
                ref[step, e] = term[step * share : (step + 1) * share]


def pair_kernel(cuts, keep_ref, got_ref, *out_refs):
    out_refs = iter(out_refs)
    for step in range(1, keep_ref.shape[0]):
        start = 0
        for rows in cuts:
            at = slice(start, start + rows)
            pair = keep_ref[step, :, at].astype(F32) + got_ref[step, :, at].astype(F32)
            next(out_refs)[...] = pair.astype(BF16)
            start += rows


def last_kernel(cuts, start, *refs):
    out_ref, mark_ref, total_ref, sem = refs[-4:]
    mark_ref[...] = jnp.zeros(mark_ref.shape, F32)
    column = 0
    for rows_of in cuts:
        keep_ref, got_ref, *refs = refs
        across, held, _, width = keep_ref.shape
        others, refs = refs[: len(rows_of) * (across - 1)], refs[len(rows_of) * (across - 1) :]
        columns = slice(column, column + width)
        column += width
        for e in range(held):
            row = 0
            for cut, rows in enumerate(rows_of):
                at = slice(row, row + rows)
                total = keep_ref[0, e, at].astype(F32) + got_ref[0, e, at].astype(F32)
                for ref in others[cut :: len(rows_of)]:
                    total = total + ref[e].astype(F32)
                total_ref[at, e, columns] = total
                row += rows
    copy = pltpu.make_async_copy(
        total_ref, out_ref.at[:, :, start : start + total_ref.shape[2]], sem
    )
    copy.start()
    copy.wait()


def raw_kernel(parts, start, final, weight_ref, *refs):
    part_refs, refs = refs[:parts], refs[parts:]
    if start:
        acc_ref, refs = refs[0], refs[1:]
    width = part_refs[0].shape[2]
    for e in range(weight_ref.shape[0]):
        raw = lax.dot_general(
            stacked_rows(part_refs, e, slice(None)),
            weight_ref[e, :, start : start + width],
            (((1,), (1,)), ((), ())),
            preferred_element_type=F32,
        )
        if start:
            raw = raw + acc_ref[e]
        if not final:
            refs[0][e] = raw
            continue
        hidden_ref, grad_ref, sums_ref = refs
        sources, _, own, units = hidden_ref.shape
        me = lax.axis_index("expert") if sources > 1 else 0
        folds = []
        for part in range(sources):
            source = source_of(me, part) if sources > 1 else 0
            block = raw[part * own : (part + 1) * own]
            grad_ref[source, e] = block.astype(BF16)
            product = block * hidden_ref[source, e].astype(F32)
            folds.append(
                functools.reduce(jnp.add, [product[:, i : i + 128] for i in range(0, units, 128)])
            )
        folded = jnp.concatenate(folds, axis=0) if len(folds) > 1 else folds[0]
        sums_ref[e : e + 1, :] = jnp.sum(folded.T, axis=0, keepdims=True)


def prob_kernel(direct, capacity, flat_ref, probs_ref, *refs):
    out_ref, mark_ref = refs[-2:]
    mark_ref[...] = jnp.zeros(mark_ref.shape, F32)
    chosen, tokens = flat_ref.shape
    if direct:
        values = []
        for q in range(LINE * SIDES):
            at = (BACK.index(q // SIDES) + LINE * (q % SIDES)) * capacity
            ref = refs[q // SIDES]
            values += [ref[q % SIDES, e : e + 1, at : at + capacity] for e in range(ref.shape[1])]
        lanes = 128 // capacity
        values = jnp.concatenate(
            [
                jnp.concatenate([v.reshape(1, capacity) for v in values[i : i + lanes]], axis=1)
                for i in range(0, len(values), lanes)
            ],
            axis=0,
        )
        me = lax.axis_index("expert")
    else:
        values = refs[0][...]
        me = 0
    lines = values.shape[0]
    spare = jnp.zeros((-lines % 8, 128), F32)
    columns = jnp.concatenate([values, spare], axis=0).T if spare.size else values.T
    total, gates, word = gates_of(probs_ref[...])
    group = lines * 128 // (LINE * SIDES)
    picked = [jnp.zeros((1, tokens), F32) for _ in range(chosen)]
    for line in range(lines):
        at = lax.broadcasted_iota(I32, (128, tokens), 0) + line * 128
        q = at // group
        slot = (moved(me, q // SIDES, q % SIDES) if direct else q) * group + at % group
        for k in range(chosen):
            hit = jnp.where(flat_ref[k : k + 1, :] == slot, columns[:, line : line + 1], 0.0)
            picked[k] += jnp.sum(hit, axis=0, keepdims=True)
    picked = [picked[k] / word[k : k + 1] for k in range(chosen)]
    mixed = functools.reduce(jnp.add, [gates[k : k + 1] * picked[k] for k in range(chosen)])
    for k in range(chosen):
        out_ref[k : k + 1, :] = (picked[k] - mixed) / total


def chunks_of(features):
    unit = features // 16
    return [[6 * unit], [5 * unit, 5 * unit]]


def cuts_of(share, first):
    half = 16 * (share // 32)
    return [half, share - half] if first else [share]


sds = jax.ShapeDtypeStruct


class Relay:
    def __init__(self, call, grad_out, ids, probs, held, capacity, widths):
        tokens, features = grad_out.shape
        self.call, self.held, self.capacity, self.widths = call, held, capacity, widths
        self.tokens, self.chosen, self.place = tokens, ids.shape[0], {}
        self.flat, first = call(
            functools.partial(begin_kernel, LINE * SIDES * held, capacity),
            [sds(ids.shape, I32), sds((tokens + INFO, widths[0]), BF16)],
            ids,
            probs,
            grad_out,
            in_specs=[HBM] * 3,
            scratch_shapes=[
                pltpu.VMEM(ids.shape, I32),
                pltpu.VMEM(probs.shape, F32),
                pltpu.SemaphoreType.DMA((3,)),
            ],
            room=60,
            keep=False,
        )
        self.blocks, self.passed = [], []
        self.leave(first)
        rest = call(
            functools.partial(cut_kernel, widths[0]),
            [sds((tokens, w), BF16) for w in widths[1:]],
            grad_out,
            in_specs=[HBM],
            scratch_shapes=[pltpu.SemaphoreType.DMA((len(widths) - 1,))],
            after=[self.blocks[0][1]],
        )
        for own in rest:
            self.leave(own)

    def leave(self, own):
        on, back = self.along(own, 1), self.along(own, LINE - 1)
        self.blocks.append([own, on, back])
        self.passed.append(self.along(on, 1))

    def along(self, block, places):
        pairs = [(i, moved(i, places, 0)) for i in range(LINE * SIDES)]
        return lax.ppermute(block, "expert", pairs)

    def pick(self, c, name, blocks, at=0):
        held, capacity, count = self.held, self.capacity, len(blocks)
        rows = [sds((held, count * capacity, self.widths[c]), BF16)] * SIDES
        kernel = functools.partial(pick_kernel, held, capacity, self.chosen, c == 0, at, count)
        if c == 0:
            place = sds((count, SIDES * held * capacity, self.tokens), BF16)
            mine, other, self.place[name] = self.call(kernel, [*rows, place], *blocks)
        else:
            mine, other = self.call(kernel, rows, *blocks, self.place[name])
        return mine, lax.ppermute(other, "expert", [(i, i ^ 1) for i in range(LINE * SIDES)])

    def early(self, c):
        if c == 0:
            return [self.pick(c, "early", self.blocks[c])]
        own = self.pick(c, "early", self.blocks[c][:1])
        return [own, self.pick(c, "early", self.blocks[c][1:], 1)]

    def late(self, c, early):
        picked = [*early, self.pick(c, "late", [self.passed[c]])]
        return [mine for mine, _ in picked] + [other for _, other in picked]


def exchanged(grad_out, ids, probs, groups, held, capacity, widths):
    tokens = grad_out.shape[0]
    experts = groups * held
    slots = experts * capacity
    _, _, word = gates_of(probs)
    flat = ids * capacity + jnp.concatenate(slots_of(ids, experts), axis=0).astype(I32)
    slot = lax.broadcasted_iota(I32, (slots, tokens), 0)
    place = sum(jnp.where(f == slot, w, 0.0) for f, w in zip(flat, word)).astype(BF16)
    arrived, start = [], 0
    for width in widths:
        rows = grad_out[:, start : start + width]
        sent = jnp.dot(place, rows, preferred_element_type=F32).astype(BF16)
        got = lax.all_to_all(
            sent.reshape(groups, held, capacity, width),
            "expert",
            split_axis=0,
            concat_axis=0,
            tiled=True,
        )
        arrived.append([got.transpose(1, 0, 2, 3).reshape(held, groups * capacity, width)])
        start += width
    return flat, arrived


def body(grad_out, route_ids, route_probs, hidden, w_down):
    groups = lax.axis_size("expert")
    dp = lax.axis_size("dp")
    held, units, features = w_down.shape
    capacity = hidden.shape[3]
    slots = groups * held * capacity
    per_expert = slots // held
    tokens, chosen = route_ids.shape
    share, across = units // dp, dp // 2
    direct = groups == LINE * SIDES
    chunks = chunks_of(features)
    widths = [sum(chunk) for chunk in chunks]
    count = len(widths)

    ids, probs = route_ids.T, route_probs.T
    call = Chain()
    if direct:
        relay = Relay(call, grad_out, ids, probs, held, capacity, widths)
        flat, saved = relay.flat, hidden[0]
    else:
        flat, arrived = exchanged(grad_out, ids, probs, groups, held, capacity, widths)
        saved = hidden[0].transpose(1, 0, 2, 3).reshape(1, held, per_expert, units)
    turned = call(
        functools.partial(turn_kernel, dp),
        sds((held, 2, across, share, per_expert), BF16),
        saved,
    )
    starts = [sum(widths[:c]) for c in range(count)]
    state = {"raw": None, "grad": None}
    summed = []

    def accumulated(c):
        parts, width, final = arrived[c], widths[c], c == count - 1
        if final:
            outs = [sds(saved.shape, BF16), sds((held, per_expert), F32)]
        else:
            outs = [sds((held, per_expert, units), F32)]
        extra = ([state["raw"]] if c else []) + ([saved] if final else [])
        kernel = functools.partial(raw_kernel, len(parts), starts[c], final)
        made = call(
            kernel,
            outs,
            w_down,
            *parts,
            *extra,
        )
        state["raw"] = made if final else made[0]

    def termed(c, at, width):
        piece = sds((across, held, share, width), BF16)
        after = summed[0][2] if summed and at == 0 and direct else ()
        if direct and not c:
            after = [early[0][1]]
        kernel = functools.partial(term_kernel, at)
        keep, give = call(kernel, [piece, piece], turned, *arrived[c], after=after)
        got = lax.ppermute(give, "dp", [(i, i ^ 1) for i in range(dp)])
        return keep, got, starts[c] + at

    def paired(keep, got, start):
        cuts = cuts_of(share, not summed)
        pieces = [sds((held, rows, keep.shape[3]), BF16) for rows in cuts]
        pairs = call(functools.partial(pair_kernel, cuts), pieces * (across - 1), keep, got)
        others = []
        for i, pair in enumerate(pairs):
            step = 1 + i // len(cuts)
            shift = [(2 * r + k, 2 * ((r + step) % across) + k) for r in range(across) for k in range(2)]
            others.append(lax.ppermute(pair, "dp", shift))
        summed.append((keep, got, others, start))

    def finished(first, last):
        before = [] if state["grad"] is None else [state["grad"]]
        done = summed[first:last]
        args = [x for keep, got, others, _ in done for x in (keep, got, *others)]
        cuts = [cuts_of(share, j == 0) for j in range(first, last)]
        state["grad"], _ = call(
            functools.partial(last_kernel, cuts, done[0][3]),
            [sds((share, held, features), F32), sds((8, 128), F32)],
            *args,
            *before,
            in_specs=[VMEM] * len(args) + [ANY] * len(before),
            out_specs=[ANY, VMEM],
            input_output_aliases={len(args): 0} if before else {},
            scratch_shapes=[
                pltpu.VMEM((share, held, sum(keep.shape[3] for keep, *_ in done)), F32),
                pltpu.SemaphoreType.DMA,
            ],
        )

    if direct:
        arrived, early = [], relay.early(0)
    for c, chunk in enumerate(chunks):
        if direct:
            arrived.append(relay.late(c, early))
            if c + 1 < count:
                early = relay.early(c + 1)
        if c >= 1:
            accumulated(c - 1)
        terms = [termed(c, sum(chunk[:i]), width) for i, width in enumerate(chunk)]
        for term in terms:
            paired(*term)
    accumulated(count - 1)
    for j in range(len(summed) - 1):
        finished(j, j + 1)
    hidden_grad, sums = state["raw"]

    if direct:
        swap = [(i, i ^ 1) for i in range(groups)]
        both = jnp.stack([sums, lax.ppermute(sums, "expert", swap)])
        returned = [both] + [
            lax.ppermute(both, "expert", [(moved(i, d, 0), i) for i in range(groups)])
            for d in range(1, LINE)
        ]
    else:
        sums = sums.reshape(held, groups, capacity).transpose(1, 0, 2).reshape(groups, -1)
        hidden_grad = hidden_grad.reshape(held, groups, capacity, units).transpose(1, 0, 2, 3)
        returned = lax.all_to_all(sums, "expert", split_axis=0, concat_axis=0, tiled=True)
        returned = [returned.reshape(-1, 128)]
    prob_grad, call.last = call(
        functools.partial(prob_kernel, direct, capacity),
        [sds((chosen, tokens), F32), sds((8, 128), F32)],
        flat,
        probs,
        *returned,
    )
    prob_grad = prob_grad.T
    finished(len(summed) - 1, len(summed))
    weight_grad = state["grad"]
    return (hidden_grad.reshape(hidden.shape), prob_grad, weight_grad)


def solution(mesh):
    in_specs = (
        P(("dp", "expert"), None),
        P(("dp", "expert"), None),
        P(("dp", "expert"), None),
        P("dp", None, "expert", None, None),
        P("expert", None, None),
    )
    out_specs = (
        P("dp", None, "expert", None, None),
        P(("dp", "expert"), None),
        P("dp", "expert", None),
    )
    return jax.shard_map(body, mesh=mesh, in_specs=in_specs, out_specs=out_specs, check_vma=False)
```
